512 devices in a mesh: row: 16 (over x, y), col: 32 (over z, core).
Axes of the slice: x: 4, y: 4, z: 16, core: 2. Of those that a mesh axis runs over, the one named last changes fastest.
Arguments:
- kernel: bfloat16 [16, 4, 32, 2, 256, 256], P('row', None, 'col'), as said below
Outputs:
- panels: float32 [16, 4, 2, 256, 256], P('row')
- schur: bfloat16 [16, 4, 32, 2, 256, 256], P('row', None, 'col')
Inputs may be any that keep to these rules, and one draw needn't show every extreme that they name: kernel describes a symmetric matrix whose leading 2 * 256 rows and columns form a positive definite block.
All inputs are finite; a program needn't handle non-finite values.
Results may differ from the reference program's by a relative error of at most 0.005.
Values may be sent and summed in bfloat16 or wider, within the bound.
A program may use at most 64 MiB of HBM per device.

```python
import jax
import jax.numpy as jnp
from jax import lax

NB = 256
BC_DEV = 2
PANELS = 2
BR_DEV = 4
ORDER = 16384
N_ROW = 16
N_COL = 32


def draw_kernel(key, part):
    key = jax.random.fold_in(key, 11)
    first_key = jax.random.fold_in(key, 0)
    base = jax.random.uniform(first_key, (ORDER, ORDER), jnp.float32, -1.0, 1.0)
    symmetric = 0.5 * (base + base.T)
    index = jnp.arange(ORDER, dtype=jnp.int32)
    leading = PANELS * NB
    nugget = 2.0 * leading ** 0.5
    on_diagonal = (index[:, None] == index[None, :]) & (index[:, None] < leading)
    symmetric = symmetric + jnp.where(on_diagonal, jnp.float32(nugget), jnp.float32(0.0))
    grid_rows = BR_DEV * N_ROW
    grid_cols = BC_DEV * N_COL
    layout = symmetric.reshape(grid_rows, NB, grid_cols, NB).transpose(0, 2, 1, 3)
    layout = layout.reshape(BR_DEV, N_ROW, BC_DEV, N_COL, NB, NB).transpose(1, 0, 3, 2, 4, 5)
    return layout.astype(jnp.bfloat16)


def setup_inputs(seed: int = 0) -> dict:
    key_of = jax.random.split(jax.random.key(seed), 2)
    return {
        "kernel": draw_kernel(jax.random.fold_in(key_of[1], 71), 0),
    }


def factorize(block):
    lower_factor = jnp.linalg.cholesky(block)
    identity = jnp.eye(block.shape[0], dtype=jnp.float32)
    inverse = lax.linalg.triangular_solve(lower_factor, identity, left_side=True, lower=True)
    return (lower_factor, inverse)

def reference(kernel):
    grid_rows = BR_DEV * N_ROW
    grid_cols = BC_DEV * N_COL
    blocks_all = kernel.transpose(1, 0, 3, 2, 4, 5).reshape(grid_rows, grid_cols, NB, NB)
    matrix = blocks_all.transpose(0, 2, 1, 3).reshape(ORDER, ORDER)
    block_index = jnp.arange(ORDER, dtype=jnp.int32) // NB
    panel_list = []
    for current in range(PANELS):
        start = current * NB
        diagonal = matrix[start:start + NB, start:start + NB].astype(jnp.float32)
        lower_factor, inverse = factorize(diagonal)
        column = matrix[:, start:start + NB].astype(jnp.float32)
        solved = jnp.dot(column, inverse.T, precision=lax.Precision.HIGHEST)
        below = (block_index > current)[:, None]
        strict = jnp.where(below, solved, jnp.zeros((), jnp.float32))
        panel_list.append(strict.at[start:start + NB].set(lower_factor))
        rounded = strict.astype(jnp.bfloat16)

        def update_rows(pair, rounded=rounded):
            rows_now, left_rows = pair
            change = jnp.dot(left_rows.astype(jnp.float32), rounded.T.astype(jnp.float32), preferred_element_type=jnp.float32)
            return (rows_now.astype(jnp.float32) - change).astype(jnp.bfloat16)
        matrix = lax.map(update_rows, (matrix.reshape(grid_rows, NB, ORDER), rounded.reshape(grid_rows, NB, NB)))
        matrix = matrix.reshape(ORDER, ORDER)
    keep = (block_index[:, None] >= PANELS) & (block_index[None, :] >= PANELS)
    schur = jnp.where(keep, matrix, jnp.zeros((), jnp.bfloat16))
    schur = schur.reshape(grid_rows, NB, grid_cols, NB).transpose(0, 2, 1, 3)
    schur = schur.reshape(BR_DEV, N_ROW, BC_DEV, N_COL, NB, NB).transpose(1, 0, 3, 2, 4, 5)
    panels = jnp.stack([piece.reshape(grid_rows, NB, NB) for piece in panel_list], axis=1)
    panels = panels.reshape(BR_DEV, N_ROW, PANELS, NB, NB).transpose(1, 0, 2, 3, 4)
    return (panels, schur)
```

```python
import functools

import jax
import jax.numpy as jnp
from jax import lax
from jax.experimental import pallas as pl
from jax.experimental.pallas import tpu as pltpu
from jax.sharding import PartitionSpec as P

MESH = pl.DeviceIdType.MESH
HI = lax.Precision.HIGHEST
GROUPS = ((0, 4), (4, 7), (7, 8))
SKIP = {0: 3, 3: 6, 6: 8, 13: 10, 10: 9}
BACK = {0: 13, 3: 2, 2: 1, 6: 5, 5: 4, 8: 7, 13: 14, 14: 15, 10: 11, 11: 12}


def lookup(key, pairs):
    value = jnp.int32(0)
    for k, v in pairs.items():
        value = jnp.where(key == k, jnp.int32(v), value)
    return value


def member(key, keys):
    hit = key == keys[0]
    for k in keys[1:]:
        hit = jnp.logical_or(hit, key == k)
    return hit


def eliminate(strips):
    row_iota = lax.broadcasted_iota(jnp.int32, (8, 128), 0)

    def row(v, i):
        return jnp.broadcast_to(v[i : i + 1, :], (8, 128))

    pivots = []
    for s in range(8):
        cols = []
        for t in range(s, 8):
            cols.append([jnp.broadcast_to(strips[t][:, 8 * s + i : 8 * s + i + 1], (8, 128)) for i in range(8)])
        head = strips[s]
        pivot = jnp.zeros((8, 128), jnp.float32)
        recips = []
        for i in range(8):
            own = cols[0][i]
            recip = 1.0 / row(own, i)
            pivot = jnp.where(row_iota == i, own, pivot)
            for j in range(i + 1, 8):
                factor = row(own, j) * recip
                for t in range(8 - s):
                    cols[t][j] = cols[t][j] - cols[t][i] * factor
            head = head - jnp.where(row_iota > i, own * recip, 0.0) * row(head, i)
            recips.append(recip)
        strips[s] = head
        pivots.append(pivot)
        heads = [row(head, i) * recips[i] for i in range(8)]
        for t in range(s + 1, 8):
            rest = strips[t]
            for i in range(8):
                rest = rest - cols[t - s][i] * heads[i]
            strips[t] = rest
    return strips, pivots


def dot32(a, b, dims):
    return lax.dot_general(a, b, (dims, ((), ())), precision=HI, preferred_element_type=jnp.float32)


def factor_two(q, g, xs):
    col_iota = lax.broadcasted_iota(jnp.int32, (8, 128), 1)
    row_iota = lax.broadcasted_iota(jnp.int32, (8, 128), 0)
    base = pl.multiple_of(q * 128, 128)
    for h in range(2):
        first = pl.multiple_of(base + 64 * h, 64)
        tile = g[pl.ds(first, 64), pl.ds(base, 128)]
        if h:
            tile = pltpu.roll(tile, 64, 1)
        strips = []
        for s in range(8):
            unit = jnp.where(col_iota == row_iota + 8 * s + 64, 1.0, 0.0)
            strips.append(jnp.where(col_iota < 64, tile[8 * s : 8 * s + 8, :], unit))
        strips, pivots = eliminate(strips)
        inverse = jnp.concatenate([a * lax.rsqrt(b) for a, b in zip(strips, pivots)], axis=0)[:, 64:]
        xs[2 * q + h] = jnp.concatenate([inverse[32:], inverse[:32]], axis=1)
        u = dot32(inverse, g[pl.ds(first, 64), :], ((1,), (0,)))
        g[...] = g[...] - dot32(u, u, ((0,), (0,)))


def gather_kernel(
    kern, acol, brow, gcol, xs,
    gbuf, g, p_send, p_recv, p_sib_send, p_sib_recv, m_send, m_recv,
    g_send, g_recv, g_sib_send, g_sib_recv, x_send, x_recv, lead_send, lead_recv, loc,
):
    r = lax.axis_index("row")
    c = lax.axis_index("col")
    x, y = lax.div(r, 4), lax.rem(r, 4)
    z, k = lax.div(c, 2), lax.rem(c, 2)
    sibling = c + 1 - 2 * k
    root = jnp.logical_and(r == 0, c == 0)
    head = z == 0
    skip_to = lookup(z, SKIP)
    back_to = lookup(z, BACK)
    has_skip = member(z, list(SKIP))
    has_back = member(z, list(BACK))
    parent = lookup(z, {v: q for q, v in list(SKIP.items()) + list(BACK.items())})

    def remote(src, dst, send, recv, row, col):
        return pltpu.make_async_remote_copy(
            src_ref=src, dst_ref=dst, send_sem=send, recv_sem=recv, device_id=(row, col), device_id_type=MESH
        )

    barrier = pltpu.get_barrier_semaphore()

    def signal(row, col):
        pl.semaphore_signal(barrier, inc=1, device_id=(row, col), device_id_type=MESH)

    own_panel = pltpu.make_async_copy(kern.at[0, :, 0, 0], acol.at[:, k], loc.at[0])
    own_rows = pltpu.make_async_copy(kern.at[0, 0, 0], brow.at[lax.rem(r, 2)], loc.at[1])
    own_piece = pltpu.make_async_copy(kern.at[0, 0, 0, 0, pl.ds(0, 32)], gcol.at[k, pl.ds(0, 32)], loc.at[2])
    own_lead = pltpu.make_async_copy(kern.at[0, 0, 0, 0], gbuf.at[0], loc.at[3])
    at_first = jnp.logical_and(r == 0, head)

    @pl.when(head)
    def _():
        own_panel.start()

    @pl.when(r < 2)
    def _():
        own_rows.start()

    @pl.when(at_first)
    def _():
        own_piece.start()

    @pl.when(root)
    def _():
        own_lead.start()
        signal(jnp.int32(1), jnp.int32(1))

    def greet(d, carry):
        signal(lax.rem(r + d, 16), c)
        return carry

    lax.fori_loop(1, 16, greet, 0)
    signal(r, sibling)

    @pl.when(jnp.logical_not(head))
    def _():
        signal(r, k)

        @pl.when(parent != 0)
        def _():
            signal(r, 2 * parent + k)

    @pl.when(jnp.logical_and(jnp.logical_and(head, k == 1), r != 0))
    def _():
        signal(jnp.int32(0), jnp.int32(0))

    children = has_skip.astype(jnp.int32) + has_back.astype(jnp.int32)
    lead_one = jnp.logical_and(r == 0, c == 1)
    lead_two = jnp.logical_and(r == 1, c == 1)
    count = 16 + jnp.where(head, 15, children) + jnp.where(root, 15, 0) + jnp.where(lead_two, 1, 0)
    pl.semaphore_wait(barrier, count)

    @pl.when(head)
    def _():
        own_panel.wait()

    @pl.when(r < 2)
    def _():
        own_rows.wait()

    @pl.when(at_first)
    def _():
        own_piece.wait()

    def panel_copies(i):
        block = acol.at[i, k]
        return (
            (has_skip, remote(block, block, p_send.at[i, 0], p_recv.at[i], r, 2 * skip_to + k)),
            (has_back, remote(block, block, p_send.at[i, 1], p_recv.at[i], r, 2 * back_to + k)),
            (None, remote(block, block, p_sib_send.at[i], p_sib_recv.at[i], r, sibling)),
        )

    def start_all(copies):
        for cond, copy in copies:
            if cond is None:
                copy.start()
            else:

                @pl.when(cond)
                def _(copy=copy):
                    copy.start()

    def finish_all(copies):
        for cond, copy in copies:
            if cond is None:
                copy.wait_send()
            else:

                @pl.when(cond)
                def _(copy=copy):
                    copy.wait_send()

    def panel_step(i):
        @pl.when(jnp.logical_not(head))
        def _():
            panel_copies(i)[0][1].wait_recv()

        start_all(panel_copies(i))

    def mirror_copies(s, j):
        block = brow.at[s, j]
        right, left = lax.rem(x + 1, 4), lax.rem(x + 3, 4)
        up, down = lax.rem(y + 1, 4), lax.rem(y + 3, 4)
        at_x = x == 0
        at_y = y == s
        if s == 0:
            ring_up, ring_down = y == 0, jnp.logical_or(y == 0, y == 3)
        else:
            ring_up, ring_down = jnp.logical_or(y == 1, y == 2), y == 1
        if s == 0:
            line_up, line_down = jnp.logical_or(x == 0, x == 1), x == 0
        else:
            line_up, line_down = x == 0, jnp.logical_or(x == 0, x == 3)
        if j == 0:
            ring_up = jnp.logical_and(ring_up, at_x)
            ring_down = jnp.logical_and(ring_down, at_x)
        else:
            line_up = jnp.logical_and(line_up, at_y)
            line_down = jnp.logical_and(line_down, at_y)
        targets = (
            (ring_up, x * 4 + up),
            (ring_down, x * 4 + down),
            (line_up, right * 4 + y),
            (line_down, left * 4 + y),
        )
        out = []
        for n, (cond, row) in enumerate(targets):
            out.append((cond, remote(block, block, m_send.at[2 * s + j, n], m_recv.at[2 * s + j], row, c)))
        return out

    def mirror_step(s, j):
        @pl.when(r != s)
        def _():
            mirror_copies(s, j)[0][1].wait_recv()

        start_all(mirror_copies(s, j))

    def piece(owner):
        return gcol.at[k, pl.ds(pl.multiple_of(32 * owner, 32), 32)]

    def scatter(i):
        owner = 8 * r + i
        return remote(
            kern.at[0, 0, 0, 0, pl.ds(32 * i, 32)], piece(owner), g_send.at[i], g_recv.at[owner], owner, c
        )

    def piece_down(d):
        return remote(piece(r), piece(r), g_send.at[d + 7], g_recv.at[r], r, 2 * d + k)

    def piece_across(d):
        return remote(piece(r), piece(r), g_send.at[d + 22], g_recv.at[r], lax.rem(r + d, 16), c)

    def piece_from(owner):
        return remote(piece(owner), piece(owner), g_send.at[0], g_recv.at[owner], r, sibling)

    leading_pair = remote(gcol.at[k], gcol.at[k], g_sib_send, g_sib_recv, r, sibling)

    def loop(lo, hi, body):
        def step(d, carry):
            body(d)
            return carry

        lax.fori_loop(lo, hi, step, 0)

    scattering = jnp.logical_and(head, r < 2)
    first_piece = jnp.where(r == 0, 1, 0)

    def leading_scatter():
        @pl.when(scattering)
        def _():
            loop(first_piece, 8, lambda i: scatter(i).start())

    def leading_spread():
        @pl.when(jnp.logical_not(at_first))
        def _():
            piece_from(r).wait_recv()

        @pl.when(head)
        def _():
            loop(1, 16, lambda d: piece_down(d).start())

        loop(1, 16, lambda d: piece_across(d).start())

    def leading_finish():
        loop(1, 16, lambda d: piece_from(lax.rem(r + d, 16)).wait_recv())
        leading_pair.start()

    def inverse_copy(n, slot, row, col):
        lo, hi = GROUPS[n]
        block = xs.at[pl.ds(lo, hi - lo)]
        return remote(block, block, x_send.at[n, slot], x_recv.at[n], row, col)

    def inverse_first(n, act):
        loop(1, 16, lambda d: act(inverse_copy(n, 14 + d, lax.rem(d + 8, 15) + 1, jnp.int32(0))))
        loop(1, 16, lambda d: act(inverse_copy(n, 29 + d, lax.rem(d + 8, 15) + 1, jnp.int32(1))))
        act(inverse_copy(n, 45, jnp.int32(0), jnp.int32(1)))

    def inverse_down(n, act):
        loop(1, 16, lambda d: act(inverse_copy(n, d - 1, r, 2 * (lax.rem(d + 6, 15) + 1) + k)))

    start = lambda copy: copy.start()
    done = lambda copy: copy.wait_send()

    def lead_copy(n):
        zero = jnp.int32(0)
        return remote(kern.at[0, 0, 0, 0], gbuf.at[n + 1], lead_send.at[n], lead_recv.at[n], zero, zero)

    @pl.when(lead_one)
    def _():
        lead_copy(0).start()

    @pl.when(lead_two)
    def _():
        lead_copy(1).start()

    leading_scatter()

    @pl.when(root)
    def _():
        for i in range(4):
            panel_step(i)
        mirror_step(0, 0)
        mirror_step(0, 1)
        leading_spread()
        own_lead.wait()
        lead_copy(0).wait_recv()
        lead_copy(1).wait_recv()
        g[0:256, 0:256] = gbuf[0].astype(jnp.float32)
        g[0:256, 256:512] = gbuf[1].astype(jnp.float32)
        g[256:512, 256:512] = gbuf[2].astype(jnp.float32)
        g[256:512, 0:256] = jnp.zeros((256, 256), jnp.float32)

        def two(q, carry):
            factor_two(q, g, xs)
            return carry

        lax.fori_loop(0, 2, two, 0)
        inverse_first(0, start)
        inverse_down(0, start)
        lax.fori_loop(2, 4, two, 0)
        for n in (1, 2):
            inverse_first(n, start)
            inverse_down(n, start)
        mirror_step(1, 0)
        mirror_step(1, 1)
        leading_finish()
        leading_pair.wait_recv()

    @pl.when(jnp.logical_not(root))
    def _():
        for s, j in ((0, 0), (1, 0), (0, 1), (1, 1)):
            mirror_step(s, j)
        leading_spread()
        for i in range(4):
            panel_step(i)
        leading_finish()
        leading_pair.wait_recv()
        for n in range(3):
            inverse_copy(n, 0, r, sibling).wait_recv()

            @pl.when(head)
            def _(n=n):
                inverse_down(n, start)

    for i in range(4):
        panel_copies(i)[2][1].wait_recv()
    for i in range(4):
        finish_all(panel_copies(i))
    for s in range(2):
        for j in range(2):
            finish_all(mirror_copies(s, j))

    @pl.when(lead_one)
    def _():
        lead_copy(0).wait_send()

    @pl.when(lead_two)
    def _():
        lead_copy(1).wait_send()

    @pl.when(scattering)
    def _():
        loop(first_piece, 8, lambda i: scatter(i).wait_send())

    @pl.when(head)
    def _():
        loop(1, 16, lambda d: piece_down(d).wait_send())
        for n in range(3):
            inverse_down(n, done)

    @pl.when(root)
    def _():
        for n in range(3):
            inverse_first(n, done)

    loop(1, 16, lambda d: piece_across(d).wait_send())
    leading_pair.wait_send()


def gather(kernel):
    bf16 = jnp.bfloat16
    return pl.pallas_call(
        gather_kernel,
        out_shape=(
            jax.ShapeDtypeStruct((4, 2, 256, 256), bf16),
            jax.ShapeDtypeStruct((2, 2, 256, 256), bf16),
            jax.ShapeDtypeStruct((2, 512, 256), bf16),
            jax.ShapeDtypeStruct((8, 32, 128), jnp.float32),
        ),
        in_specs=[pl.BlockSpec(memory_space=pl.ANY)],
        out_specs=(
            pl.BlockSpec(memory_space=pl.ANY),
            pl.BlockSpec(memory_space=pl.ANY),
            pl.BlockSpec(memory_space=pl.ANY),
            pl.BlockSpec(memory_space=pltpu.VMEM),
        ),
        scratch_shapes=[
            pltpu.VMEM((3, 256, 256), bf16),
            pltpu.VMEM((512, 512), jnp.float32),
            pltpu.SemaphoreType.DMA((4, 2)),
            pltpu.SemaphoreType.DMA((4,)),
            pltpu.SemaphoreType.DMA((4,)),
            pltpu.SemaphoreType.DMA((4,)),
            pltpu.SemaphoreType.DMA((4, 4)),
            pltpu.SemaphoreType.DMA((4,)),
            pltpu.SemaphoreType.DMA((38,)),
            pltpu.SemaphoreType.DMA((16,)),
            pltpu.SemaphoreType.DMA,
            pltpu.SemaphoreType.DMA,
            pltpu.SemaphoreType.DMA((3, 46)),
            pltpu.SemaphoreType.DMA((3,)),
            pltpu.SemaphoreType.DMA((2,)),
            pltpu.SemaphoreType.DMA((2,)),
            pltpu.SemaphoreType.DMA((4,)),
        ],
        compiler_params=pltpu.CompilerParams(
            collective_id=0, has_side_effects=True, vmem_limit_bytes=24 * 1024 * 1024
        ),
        name="gather_and_factor",
    )(kernel)


def split(a):
    high = a.astype(jnp.bfloat16)
    rest = a - high.astype(jnp.float32)
    middle = rest.astype(jnp.bfloat16)
    low = (rest - middle.astype(jnp.float32)).astype(jnp.bfloat16)
    return high, middle, low


def update_kernel(kern, acol, brow, gcol, xs, panels, schur, aug, parts):
    r = lax.axis_index("row")
    c = lax.axis_index("col")
    aug[:, 0:256] = gcol[0].astype(jnp.float32)
    aug[:, 256:512] = gcol[1].astype(jnp.float32)
    rows = lax.broadcasted_iota(jnp.int32, (512, 512), 0)
    cols = lax.broadcasted_iota(jnp.int32, (512, 512), 1)
    aug[:, 512:1024] = jnp.where(rows == cols, 1.0, 0.0)
    for s in range(8):
        packed = xs[s]
        inverse = jnp.concatenate([packed[:, 64:128], packed[:, 0:64]], axis=0)
        lines = dot32(inverse, aug[64 * s : 64 * s + 64, :], ((1,), (0,)))
        aug[64 * s : 64 * s + 64, :] = lines
        if s < 7:
            rest = pl.ds(64 * (s + 1), 512 - 64 * (s + 1))
            aug[rest, :] = aug[rest, :] - dot32(lines[:, 64 * (s + 1) : 512], lines, ((0,), (0,)))
    for n, part in enumerate(split(aug[:, 512:1024])):
        parts[n] = part

    mirror = []
    for j in range(2):
        total = jnp.zeros((512, 256), jnp.float32)
        for n in range(3):
            for s in range(2):
                total = total + jnp.dot(
                    parts[n, :, 256 * s : 256 * s + 256], brow[s, j], preferred_element_type=jnp.float32
                )
        mirror.append(total.astype(jnp.bfloat16))
    tri = lax.broadcasted_iota(jnp.int32, (256, 256), 0) >= lax.broadcasted_iota(jnp.int32, (256, 256), 1)
    for i in range(4):
        total = jnp.zeros((256, 512), jnp.float32)
        for n in range(3):
            for s in range(2):
                total = total + lax.dot_general(
                    acol[i, s], parts[n, :, 256 * s : 256 * s + 256],
                    (((1,), (1,)), ((), ())), preferred_element_type=jnp.float32,
                )
        first, second = total[:, 0:256], total[:, 256:512]
        if i == 0:
            first = jnp.where(jnp.logical_or(r != 0, tri), first, 0.0)
            second = jnp.where(jnp.logical_or(r > 1, jnp.logical_and(r == 1, tri)), second, 0.0)
        panels[0, i, 0] = first
        panels[0, i, 1] = second
        left = total.astype(jnp.bfloat16)
        for j in range(2):
            change = jnp.dot(left, mirror[j], preferred_element_type=jnp.float32)
            out = (kern[0, i, 0, j].astype(jnp.float32) - change).astype(jnp.bfloat16)
            if i == 0:
                out = jnp.where(r >= 2, out, jnp.zeros_like(out))
            if j == 0:
                out = jnp.where(c >= 2, out, jnp.zeros_like(out))
            schur[0, i, 0, j] = out


def update(kernel, acol, brow, gcol, xs):
    return pl.pallas_call(
        update_kernel,
        out_shape=(
            jax.ShapeDtypeStruct((1, 4, 2, 256, 256), jnp.float32),
            jax.ShapeDtypeStruct((1, 4, 1, 2, 256, 256), jnp.bfloat16),
        ),
        in_specs=[pl.BlockSpec(memory_space=pltpu.VMEM)] * 5,
        out_specs=(pl.BlockSpec(memory_space=pltpu.VMEM), pl.BlockSpec(memory_space=pltpu.VMEM)),
        scratch_shapes=[pltpu.VMEM((512, 1024), jnp.float32), pltpu.VMEM((3, 512, 512), jnp.bfloat16)],
        compiler_params=pltpu.CompilerParams(vmem_limit_bytes=48 * 1024 * 1024),
        name="solve_and_update",
    )(kernel, acol, brow, gcol, xs)


def per_device(kernel):
    return update(kernel, *gather(kernel))


def solution(mesh):
    in_specs = (P("row", None, "col", None, None, None),)
    out_specs = (P("row", None, None, None, None), P("row", None, "col", None, None, None))
    return jax.shard_map(per_device, mesh=mesh, in_specs=in_specs, out_specs=out_specs, check_vma=False)
```

```python
import functools

import jax
import jax.numpy as jnp
from jax import lax
from jax.experimental import pallas as pl
from jax.experimental.pallas import tpu as pltpu
from jax.sharding import PartitionSpec as P

MESH = pl.DeviceIdType.MESH
HI = lax.Precision.HIGHEST
GROUPS = ((0, 2), (2, 3), (3, 4))
HEAD = 1
SKIP = {0: 3, 3: 6, 6: 8, 13: 10, 10: 9}
BACK = {0: 13, 3: 2, 2: 1, 6: 5, 5: 4, 8: 7, 13: 14, 14: 15, 10: 11, 11: 12}


def lookup(key, pairs):
    value = jnp.int32(0)
    for k, v in pairs.items():
        value = jnp.where(key == k, jnp.int32(v), value)
    return value


def member(key, keys):
    hit = key == keys[0]
    for k in keys[1:]:
        hit = jnp.logical_or(hit, key == k)
    return hit


def eliminate(strips):
    row_iota = lax.broadcasted_iota(jnp.int32, (8, 128), 0)

    def row(v, i):
        return jnp.broadcast_to(v[i : i + 1, :], (8, 128))

    pivots = []
    for s in range(8):
        cols = []
        for t in range(s, 8):
            cols.append([jnp.broadcast_to(strips[t][:, 8 * s + i : 8 * s + i + 1], (8, 128)) for i in range(8)])
        head = strips[s]
        pivot = jnp.zeros((8, 128), jnp.float32)
        recips = []
        for i in range(8):
            own = cols[0][i]
            recip = 1.0 / row(own, i)
            pivot = jnp.where(row_iota == i, own, pivot)
            for j in range(i + 1, 8):
                factor = row(own, j) * recip
                for t in range(8 - s):
                    cols[t][j] = cols[t][j] - cols[t][i] * factor
            head = head - jnp.where(row_iota > i, own * recip, 0.0) * row(head, i)
            recips.append(recip)
        strips[s] = head
        pivots.append(pivot)
        heads = [row(head, i) * recips[i] for i in range(8)]
        for t in range(s + 1, 8):
            rest = strips[t]
            for i in range(8):
                rest = rest - cols[t - s][i] * heads[i]
            strips[t] = rest
    return strips, pivots


def dot32(a, b, dims):
    return lax.dot_general(a, b, (dims, ((), ())), precision=HI, preferred_element_type=jnp.float32)


def factor_block(q, h, g, store):
    col_iota = lax.broadcasted_iota(jnp.int32, (8, 128), 1)
    row_iota = lax.broadcasted_iota(jnp.int32, (8, 128), 0)
    base = pl.multiple_of(q * 128, 128)
    first = pl.multiple_of(base + 64 * h, 64)
    tile = g[pl.ds(first, 64), pl.ds(base, 128)]
    if h:
        tile = pltpu.roll(tile, 64, 1)
    strips = []
    for s in range(8):
        unit = jnp.where(col_iota == row_iota + 8 * s + 64, 1.0, 0.0)
        strips.append(jnp.where(col_iota < 64, tile[8 * s : 8 * s + 8, :], unit))
    strips, pivots = eliminate(strips)
    inverse = jnp.concatenate([a * lax.rsqrt(b) for a, b in zip(strips, pivots)], axis=0)[:, 64:]
    store(jnp.concatenate([inverse[32:], inverse[:32]], axis=1))
    lines = dot32(inverse, g[pl.ds(first, 64), :], ((1,), (0,)))
    rows = lax.broadcasted_iota(jnp.int32, (256, 512), 0)
    g[...] = g[...] - jnp.where(rows >= first + 64, dot32(lines[:, 0:256], lines, ((0,), (0,))), 0.0)
    g[pl.ds(first, 64), :] = lines


def set_identity(g):
    rows = lax.broadcasted_iota(jnp.int32, (256, 256), 0)
    cols = lax.broadcasted_iota(jnp.int32, (256, 256), 1)
    g[:, 256:512] = jnp.where(rows == cols, 1.0, 0.0)


def gather_kernel(
    kern, acol, brow, lead, xa, xs,
    gbuf, g, x_src, xa_src, a00, lead_stage, xa_stage, xs_stage,
    p_send, p_recv, p_sib_send, p_sib_recv, m_send, m_recv, m_sib_send, m_sib_recv,
    lead_send, lead_recv, a_send, a_recv, gs_send, gh_recv, gd_send, gd_recv, ga_send, ga_recv, gx_send, gx_recv,
    xr_send, xh_recv, xd_send, xd_recv, xx_send, xx_recv, loc,
):
    r = lax.axis_index("row")
    c = lax.axis_index("col")
    x, y = lax.div(r, 4), lax.rem(r, 4)
    z, k = lax.div(c, 2), lax.rem(c, 2)
    zero = jnp.int32(0)
    sibling = c + 1 - 2 * k
    both = jnp.logical_and
    core0, core1 = k == 0, k == 1
    top = z == 0
    inner = jnp.logical_not(top)
    root = both(r == 0, c == 0)
    aide = both(r == 0, c == 1)
    helper = both(r == 1, c == 1)
    head = both(z == HEAD, core0)
    runner = both(core0, inner)
    skip_to = lookup(z, SKIP)
    back_to = lookup(z, BACK)
    has_skip = member(z, list(SKIP))
    has_back = member(z, list(BACK))
    parent = lookup(z, {v: q for q, v in list(SKIP.items()) + list(BACK.items())})
    children = has_skip.astype(jnp.int32) + has_back.astype(jnp.int32)
    barrier = pltpu.get_barrier_semaphore()

    def remote(src, dst, send, recv, row, col):
        return pltpu.make_async_remote_copy(
            src_ref=src, dst_ref=dst, send_sem=send, recv_sem=recv, device_id=(row, col), device_id_type=MESH
        )

    def signal(row, col):
        pl.semaphore_signal(barrier, inc=1, device_id=(row, col), device_id_type=MESH)

    def loop(lo, hi, body):
        def step(d, carry):
            body(d)
            return carry

        lax.fori_loop(lo, hi, step, 0)

    def when(cond, body):
        @pl.when(cond)
        def _():
            body()

    def start(copy):
        copy.start()

    def sent(copy):
        copy.wait_send()

    own_panel = pltpu.make_async_copy(kern.at[0, :, 0, 0], acol.at[:, k], loc.at[0])
    own_rows = pltpu.make_async_copy(kern.at[0, 0, 0], brow.at[lax.rem(r, 2), :, k], loc.at[1])
    own_lead = pltpu.make_async_copy(kern.at[0, 0, 0, 0], gbuf.at[0], loc.at[2])
    when(root, lambda: own_lead.start())
    when(top, lambda: own_panel.start())
    when(r < 2, lambda: own_rows.start())

    signal(r, sibling)

    def greet_panel():
        signal(r, 2 * parent)
        when(parent == 0, lambda: signal(r, jnp.int32(1)))

    when(runner, greet_panel)

    def greet_plane():
        loop(1, 16, lambda d: signal(lax.rem(r + d, 16), c))
        when(z != HEAD, lambda: signal(r, jnp.int32(2 * HEAD)))

    when(core1, greet_plane)

    def greet_sources():
        signal(zero, zero)
        signal(zero, jnp.int32(1))
        signal(jnp.int32(1), jnp.int32(1))

    when(head, greet_sources)
    when(root, lambda: signal(jnp.int32(1), jnp.int32(1)))

    def arrive():
        plane = jnp.where(core1, 15, 0)
        line = jnp.where(top, 2, jnp.where(core0, children, 0))
        more = jnp.where(head, 15, 0) + jnp.where(root, 16, 0) + jnp.where(aide, 16, 0) + jnp.where(helper, 17, 0)
        pl.semaphore_wait(barrier, 1 + plane + line + more)
        when(top, lambda: own_panel.wait())
        when(r < 2, lambda: own_rows.wait())

    def panel_chunk(n):
        i, half, col = lax.div(n, 4), lax.rem(lax.div(n, 2), 2), lax.rem(n, 2)
        return acol.at[i, col, pl.ds(pl.multiple_of(128 * half, 128), 128)]

    def panel_skip(n):
        return remote(panel_chunk(n), panel_chunk(n), p_send.at[n, 0], p_recv.at[n], r, 2 * skip_to)

    def panel_back(n):
        return remote(panel_chunk(n), panel_chunk(n), p_send.at[n, 1], p_recv.at[n], r, 2 * back_to)

    def panel_pair(n):
        return remote(panel_chunk(n), panel_chunk(n), p_sib_send.at[n], p_sib_recv.at[n], r, sibling)

    def panel_top(act):
        def step(m):
            n = 2 * m + k
            act(panel_skip(n))
            act(panel_back(n))

        loop(0, 8, step)
        loop(0, 8, lambda m: act(panel_pair(2 * m + k)))

    def panel_line(n):
        panel_skip(n).wait_recv()
        when(has_skip, lambda: panel_skip(n).start())
        when(has_back, lambda: panel_back(n).start())
        panel_pair(n).start()

    def panel_line_sent(n):
        when(has_skip, lambda: panel_skip(n).wait_send())
        when(has_back, lambda: panel_back(n).wait_send())
        panel_pair(n).wait_send()

    def mirror_chunk(s, m):
        j, kc, half = lax.div(m, 4), lax.rem(lax.div(m, 2), 2), lax.rem(m, 2)
        return brow.at[s, j, kc, pl.ds(pl.multiple_of(128 * half, 128), 128)]

    def mirror_copy(s, m, way, row):
        return remote(mirror_chunk(s, m), mirror_chunk(s, m), m_send.at[8 * s + m, way], m_recv.at[8 * s + m], row, c)

    def mirror_pair(s, m):
        n = 8 * s + m
        return remote(mirror_chunk(s, m), mirror_chunk(s, m), m_sib_send.at[n], m_sib_recv.at[n], r, sibling)

    def mirror_feed(j, half):
        m = 4 * j + half
        n = 8 * r + m
        return remote(mirror_chunk(r, m), mirror_chunk(r, m), m_sib_send.at[n], m_recv.at[n], r, sibling)

    def mirror_each(s, m, act):
        j, kc = lax.div(m, 4), lax.rem(lax.div(m, 2), 2)
        rel = lax.rem(y + 4 - s, 4)
        ring = jnp.logical_or(j == 1, x == 0)
        line = jnp.logical_or(j == 0, rel == 0)
        ring_up = both(ring, jnp.logical_or(rel == 0, both(s == 1, rel == 1)))
        ring_down = both(ring, jnp.logical_or(rel == 0, both(s == 0, rel == 3)))
        line_up = both(line, jnp.logical_or(x == 0, both(s == 0, x == 1)))
        line_down = both(line, jnp.logical_or(x == 0, both(s == 1, x == 3)))
        when(ring_up, lambda: act(mirror_copy(s, m, 0, x * 4 + lax.rem(y + 1, 4))))
        when(ring_down, lambda: act(mirror_copy(s, m, 1, x * 4 + lax.rem(y + 3, 4))))
        when(line_up, lambda: act(mirror_copy(s, m, 2, lax.rem(x + 1, 4) * 4 + y)))
        when(line_down, lambda: act(mirror_copy(s, m, 3, lax.rem(x + 3, 4) * 4 + y)))
        when(both(kc == 0, r != s), lambda: act(mirror_pair(s, m)))

    def mirror_step(n):
        nearer = jnp.where(jnp.logical_or(y == 0, y == 3), 0, 1)
        s = lax.rem(lax.div(n, 8) + nearer, 2)
        m = lax.rem(n, 8)
        kc = lax.rem(lax.div(m, 2), 2)
        when(jnp.logical_or(r != s, kc == 0), lambda: mirror_copy(s, m, 0, r).wait_recv())
        mirror_each(s, m, start)

    def mirror_sent(n):
        mirror_each(lax.div(n, 8), lax.rem(n, 8), sent)

    def feeds(act):
        for j in range(2):
            for half in range(2):
                act(mirror_feed(j, half))

    def mirror_take():
        for s in range(2):

            def take(s=s):
                for j in range(2):
                    for half in range(2):
                        mirror_pair(s, 4 * j + half).wait_recv()

            when(r != s, take)

    def lead_from(src, n, p):
        rows = pl.ds(pl.multiple_of(16 * p, 16), 16)
        return remote(src.at[rows], lead_stage.at[n], gs_send.at[n, p], gh_recv.at[n], p, jnp.int32(2 * HEAD))

    own_block = kern.at[0, 0, 0, 0]

    def lead_scatter(src, n, act):
        loop(0, 16, lambda p: act(lead_from(src, n, p)))

    def down(buf, which, d):
        to = lax.rem(HEAD + d, 16)
        stage = lead_stage if which == 0 else xa_stage
        return remote(stage, buf.at[r], gd_send.at[which, d], gd_recv.at[which], r, 2 * to + 1)

    def across(buf, which, d):
        return remote(
            buf.at[r], buf.at[r], ga_send.at[which, d], ga_recv.at[which, r], lax.rem(r + d, 16), c
        )

    def piece_from(buf, which, p):
        return remote(buf.at[p], buf.at[p], ga_send.at[which, 0], ga_recv.at[which, p], r, sibling)

    def pair(buf, which):
        return remote(buf, buf, gx_send.at[which], gx_recv.at[which], r, sibling)

    def head_down(buf, which):
        loop(0, 16, lambda d: down(buf, which, lax.rem(d + 8, 16)).start())

    def spread(buf, which):
        down(buf, which, 0).wait_recv()
        loop(1, 16, lambda d: across(buf, which, lax.rem(d + 9, 15) + 1).start())

    def collect(buf, which):
        loop(1, 16, lambda d: piece_from(buf, which, lax.rem(r + d, 16)).wait_recv())
        pair(buf, which).start()

    def inverse_piece(p):
        return remote(xa_src.at[p], xa_stage, xr_send.at[0, p], xh_recv.at[0], p, jnp.int32(2 * HEAD))

    def inverse_block(n):
        lo, hi = GROUPS[n]
        return pl.ds(lo, hi - lo)

    def inverse_first(n, p):
        rows = inverse_block(n)
        return remote(x_src.at[rows], xs_stage.at[rows], xr_send.at[1 + n, p], xh_recv.at[1 + n], p, jnp.int32(2 * HEAD))

    def inverse_down(n, d):
        rows = inverse_block(n)
        to = lax.rem(HEAD + d, 16)
        return remote(xs_stage.at[rows], xs.at[rows], xd_send.at[n, d], xd_recv.at[n], r, 2 * to + 1)

    def inverse_pair(n):
        block = xs.at[inverse_block(n)]
        return remote(block, block, xx_send.at[n], xx_recv.at[n], r, sibling)

    def first_all(n, act):
        loop(0, 16, lambda p: act(inverse_first(n, lax.rem(p + 10, 16))))

    def down_all(n, act):
        loop(0, 16, lambda d: act(inverse_down(n, lax.rem(d + 8, 16))))

    def send_lead():
        return remote(own_block, a00, a_send, a_recv, r, sibling)

    def lead_copy(n):
        return remote(own_block, gbuf.at[n + 1], lead_send.at[n], lead_recv.at[n], zero, zero)

    def root_main():
        own_lead.wait()
        g[:, 0:256] = gbuf[0].astype(jnp.float32)
        set_identity(g)

        def second_half():
            lead_copy(0).wait_recv()
            lead_copy(1).wait_recv()
            side = dot32(g[:, 256:512], gbuf[1].astype(jnp.float32), ((1,), (0,)))
            g[:, 0:256] = gbuf[2].astype(jnp.float32) - dot32(side, side, ((0,), (0,)))
            set_identity(g)

        def bulk():
            arrive()
            send_lead().start()
            feeds(start)
            panel_top(start)

        def store_at(slot):
            def store(packed):
                x_src[slot] = packed
                for part in range(4):
                    xa_src[4 * slot + part] = packed[8 * part : 8 * part + 8]

            return store

        def step(it):
            when(it == 1, bulk)
            when(it == 2, second_half)
            q = lax.rem(it, 2)
            slot = 2 * q
            factor_block(q, 0, g, store_at(slot))
            when(it == 3, lambda: first_all(1, start))
            factor_block(q, 1, g, store_at(slot + 1))
            def after_first():
                loop(0, 16, lambda p: inverse_piece(p).start())
                loop(0, 16, lambda p: inverse_piece(p).wait_send())

            when(it == 1, after_first)
            when(it == 2, lambda: first_all(0, start))

        loop(0, 4, step)
        first_all(2, start)

    when(root, root_main)
    when(jnp.logical_not(root), arrive)

    def zero_top():
        when(aide, lambda: lead_copy(0).start())
        when(helper, lambda: lead_copy(1).start())
        panel_top(start)
        when(both(core0, r < 2), lambda: feeds(start))

    when(both(top, jnp.logical_not(root)), zero_top)
    when(both(both(core0, r < 2), inner), lambda: feeds(start))

    def aide_main():
        lead_scatter(own_block, 1, start)
        send_lead().wait_recv()
        lead_scatter(a00, 0, start)

    when(aide, aide_main)
    when(helper, lambda: lead_scatter(own_block, 2, start))

    def core1_main():
        loop(0, 16, mirror_step)
        spread(lead, 0)
        collect(lead, 0)
        spread(xa, 1)
        collect(xa, 1)
        for n in range(3):
            inverse_down(n, 0).wait_recv()
            inverse_pair(n).start()

    when(core1, core1_main)

    def head_main():
        for n in range(3):
            lead_from(own_block, n, 0).wait_recv()
        head_down(lead, 0)
        inverse_piece(0).wait_recv()
        head_down(xa, 1)
        for n in range(3):
            inverse_first(n, 0).wait_recv()
            down_all(n, start)

    when(head, head_main)
    when(runner, lambda: loop(0, 16, panel_line))

    def core0_take():
        mirror_take()
        pair(lead, 0).wait_recv()
        pair(xa, 1).wait_recv()
        for n in range(3):
            inverse_pair(n).wait_recv()

    when(core0, core0_take)
    when(both(core1, inner), lambda: loop(0, 16, lambda n: panel_pair(n).wait_recv()))
    when(top, lambda: loop(0, 8, lambda m: panel_pair(2 * m + 1 - k).wait_recv()))

    when(runner, lambda: loop(0, 16, panel_line_sent))
    when(top, lambda: panel_top(sent))
    when(both(core0, r < 2), lambda: feeds(sent))

    def core1_drain():
        loop(0, 16, mirror_sent)
        for which, buf in ((0, lead), (1, xa)):
            loop(1, 16, lambda d, which=which, buf=buf: across(buf, which, d).wait_send())
            pair(buf, which).wait_send()
        for n in range(3):
            inverse_pair(n).wait_send()

    when(core1, core1_drain)

    def head_drain():
        for which, buf in ((0, lead), (1, xa)):
            loop(0, 16, lambda d, which=which, buf=buf: down(buf, which, d).wait_send())
        for n in range(3):
            down_all(n, sent)

    when(head, head_drain)

    def aide_drain():
        lead_copy(0).wait_send()
        lead_scatter(own_block, 1, sent)
        lead_scatter(a00, 0, sent)

    when(aide, aide_drain)

    def helper_drain():
        lead_copy(1).wait_send()
        lead_scatter(own_block, 2, sent)

    when(helper, helper_drain)

    def root_drain():
        send_lead().wait_send()
        for n in range(3):
            first_all(n, sent)

    when(root, root_drain)


def gather(kernel):
    bf16, f32 = jnp.bfloat16, jnp.float32
    dma = pltpu.SemaphoreType.DMA
    return pl.pallas_call(
        gather_kernel,
        out_shape=(
            jax.ShapeDtypeStruct((4, 2, 256, 256), bf16),
            jax.ShapeDtypeStruct((2, 2, 2, 256, 256), bf16),
            jax.ShapeDtypeStruct((16, 3, 16, 256), bf16),
            jax.ShapeDtypeStruct((16, 8, 128), f32),
            jax.ShapeDtypeStruct((4, 32, 128), f32),
        ),
        in_specs=[pl.BlockSpec(memory_space=pltpu.HBM)],
        out_specs=(pl.BlockSpec(memory_space=pl.ANY),) * 5,
        scratch_shapes=[
            pltpu.VMEM((3, 256, 256), bf16),
            pltpu.VMEM((256, 512), f32),
            pltpu.VMEM((4, 32, 128), f32),
            pltpu.VMEM((16, 8, 128), f32),
            pltpu.VMEM((256, 256), bf16),
            pltpu.VMEM((3, 16, 256), bf16),
            pltpu.VMEM((8, 128), f32),
            pltpu.VMEM((4, 32, 128), f32),
            dma((16, 2)), dma((16,)), dma((16,)), dma((16,)),
            dma((16, 4)), dma((16,)), dma((16,)), dma((16,)),
            dma((2,)), dma((2,)), dma, dma,
            dma((3, 16)), dma((3,)), dma((2, 16)), dma((2,)), dma((2, 16)), dma((2, 16)), dma((2,)), dma((2,)),
            dma((4, 16)), dma((4,)), dma((3, 16)), dma((3,)), dma((3,)), dma((3,)), dma((3,)),
        ],
        compiler_params=pltpu.CompilerParams(
            collective_id=0, has_side_effects=True, vmem_limit_bytes=24 * 1024 * 1024
        ),
        name="gather_and_factor",
    )(kernel)


def split(a):
    high = a.astype(jnp.bfloat16)
    rest = a - high.astype(jnp.float32)
    middle = rest.astype(jnp.bfloat16)
    low = (rest - middle.astype(jnp.float32)).astype(jnp.bfloat16)
    return high, middle, low


def assemble(start, packs, g):
    g[:, 0:256] = start
    set_identity(g)
    for n in range(4):
        packed = packs[n]
        inverse = jnp.concatenate([packed[:, 64:128], packed[:, 0:64]], axis=0)
        lo, hi = 64 * n, 64 * n + 64
        lines = dot32(inverse, g[lo:hi, :], ((1,), (0,)))
        g[lo:hi, :] = lines
        if n < 3:
            g[hi:256, :] = g[hi:256, :] - dot32(lines[:, hi:256], lines, ((0,), (0,)))
    return g[:, 256:512]


def update_kernel(kern, acol, brow, lead, xa, xs, panels, schur, g, inv, parts):
    r = lax.axis_index("row")
    c = lax.axis_index("col")
    k = lax.rem(c, 2)

    def block(n):
        return jnp.concatenate([lead[p, n] for p in range(16)], axis=0).astype(jnp.float32)

    first_packs = [jnp.concatenate([xa[4 * n + p] for p in range(4)], axis=0) for n in range(4)]
    inv[...] = jnp.zeros((512, 512), jnp.float32)
    inv[0:256, 0:256] = assemble(block(0), first_packs, g)
    side = dot32(inv[0:256, 0:256], block(1), ((1,), (0,)))
    inv[256:512, 256:512] = assemble(block(2) - dot32(side, side, ((0,), (0,))), [xs[n] for n in range(4)], g)
    low = dot32(side, inv[0:256, 0:256], ((0,), (0,)))
    inv[256:512, 0:256] = -dot32(inv[256:512, 256:512], low, ((1,), (0,)))
    for n, part in enumerate(split(inv[...])):
        parts[n] = part

    mirror = []
    for j in range(2):
        total = jnp.zeros((512, 256), jnp.float32)
        for n in range(3):
            for s in range(2):
                total = total + jnp.dot(
                    parts[n, :, 256 * s : 256 * s + 256], brow[s, j, k], preferred_element_type=jnp.float32
                )
        mirror.append(total.astype(jnp.bfloat16))
    tri = lax.broadcasted_iota(jnp.int32, (256, 256), 0) >= lax.broadcasted_iota(jnp.int32, (256, 256), 1)
    for i in range(4):
        total = jnp.zeros((256, 512), jnp.float32)
        for n in range(3):
            for s in range(2):
                total = total + lax.dot_general(
                    acol[i, s], parts[n, :, 256 * s : 256 * s + 256],
                    (((1,), (1,)), ((), ())), preferred_element_type=jnp.float32,
                )
        first, second = total[:, 0:256], total[:, 256:512]
        if i == 0:
            first = jnp.where(jnp.logical_or(r != 0, tri), first, 0.0)
            second = jnp.where(jnp.logical_or(r > 1, jnp.logical_and(r == 1, tri)), second, 0.0)
        panels[0, i, 0] = first
        panels[0, i, 1] = second
        left = total.astype(jnp.bfloat16)
        for j in range(2):
            change = jnp.dot(left, mirror[j], preferred_element_type=jnp.float32)
            out = (kern[0, i, 0, j].astype(jnp.float32) - change).astype(jnp.bfloat16)
            if i == 0:
                out = jnp.where(r >= 2, out, jnp.zeros_like(out))
            if j == 0:
                out = jnp.where(c >= 2, out, jnp.zeros_like(out))
            schur[0, i, 0, j] = out


def update(kernel, *gathered):
    return pl.pallas_call(
        update_kernel,
        out_shape=(
            jax.ShapeDtypeStruct((1, 4, 2, 256, 256), jnp.float32),
            jax.ShapeDtypeStruct((1, 4, 1, 2, 256, 256), jnp.bfloat16),
        ),
        in_specs=[pl.BlockSpec(memory_space=pltpu.VMEM)] * 6,
        out_specs=(pl.BlockSpec(memory_space=pltpu.VMEM), pl.BlockSpec(memory_space=pltpu.VMEM)),
        scratch_shapes=[
            pltpu.VMEM((256, 512), jnp.float32),
            pltpu.VMEM((512, 512), jnp.float32),
            pltpu.VMEM((3, 512, 512), jnp.bfloat16),
        ],
        compiler_params=pltpu.CompilerParams(vmem_limit_bytes=48 * 1024 * 1024),
        name="solve_and_update",
    )(kernel, *gathered)


def per_device(kernel):
    return update(kernel, *gather(kernel))


def solution(mesh):
    in_specs = (P("row", None, "col", None, None, None),)
    out_specs = (P("row", None, None, None, None), P("row", None, "col", None, None, None))
    return jax.shard_map(per_device, mesh=mesh, in_specs=in_specs, out_specs=out_specs, check_vma=False)
```

```python
import functools

import jax
import jax.numpy as jnp
from jax import lax
from jax.experimental import pallas as pl
from jax.experimental.pallas import tpu as pltpu
from jax.sharding import PartitionSpec as P

MESH = pl.DeviceIdType.MESH
HI = lax.Precision.HIGHEST
GROUPS = ((0, 2), (2, 3), (3, 4))
HEAD = 1
SKIP = {0: 3, 3: 6, 6: 8, 13: 10, 10: 9}
BACK = {0: 13, 3: 2, 2: 1, 6: 5, 5: 4, 8: 7, 13: 14, 14: 15, 10: 11, 11: 12}


def lookup(key, pairs):
    value = jnp.int32(0)
    for k, v in pairs.items():
        value = jnp.where(key == k, jnp.int32(v), value)
    return value


def member(key, keys):
    hit = key == keys[0]
    for k in keys[1:]:
        hit = jnp.logical_or(hit, key == k)
    return hit


def dot32(a, b, dims):
    return lax.dot_general(a, b, (dims, ((), ())), precision=HI, preferred_element_type=jnp.float32)


def row(v, i):
    return jnp.broadcast_to(v[i : i + 1, :], (8, 128))

def lane(v, i):
    return jnp.broadcast_to(v[:, i : i + 1], (8, 128))


def eliminate(strips, off):
    row_iota = lax.broadcasted_iota(jnp.int32, (8, 128), 0)
    strips = list(strips)
    diag = [lane(strips[0], off + i) for i in range(8)]
    pivots = []
    for s in range(8):
        later = range(s + 1, 8)
        cols = {t: [lane(strips[t], off + 8 * s + i) for i in range(8)] for t in later}
        if s < 7:
            raw = [lane(strips[s + 1], off + 8 * (s + 1) + i) for i in range(8)]
        head = strips[s]
        pivot = jnp.zeros((8, 128), jnp.float32)
        recips = []
        for i in range(8):
            own = diag[i]
            recip = 1.0 / row(own, i)
            recips.append(recip)
            pivot = jnp.where(row_iota == i, own, pivot)
            for j in range(i + 1, 8):
                line = row(own, j)
                diag[j] = diag[j] - (own * line) * recip
                factor = line * recip
                for t in later:
                    cols[t][j] = cols[t][j] - cols[t][i] * factor
            head = head - jnp.where(row_iota > i, own * recip, 0.0) * row(head, i)
        strips[s] = head
        pivots.append(pivot)
        if s < 7:
            near = cols[s + 1]
            scaled = [near[i] * recips[i] for i in range(8)]
            diag = []
            for j in range(8):
                terms = [scaled[i] * row(near[i], j) for i in range(8)]
                while len(terms) > 1:
                    terms = [terms[a] + terms[a + 1] for a in range(0, len(terms), 2)]
                diag.append(raw[j] - terms[0])
        heads = [row(head, i) * recips[i] for i in range(8)]
        for t in later:
            terms = [cols[t][i] * heads[i] for i in range(8)]
            while len(terms) > 1:
                terms = [terms[a] + terms[a + 1] for a in range(0, len(terms), 2)]
            strips[t] = strips[t] - terms[0]
    return strips, pivots


def factor_phase(g, store):
    col_iota = lax.broadcasted_iota(jnp.int32, (8, 128), 1)
    row_iota = lax.broadcasted_iota(jnp.int32, (8, 128), 0)
    for b in range(4):
        odd = b % 2
        lo = 64 + 64 * b
        win = 128 * (b // 2)
        off = 64 * odd
        strips = []
        tile = g[lo:lo+64, win:win+128]
        for s in range(8):
            if odd:
                unit = jnp.where(col_iota == row_iota + 8 * s, 1.0, 0.0)
                strips.append(jnp.where(col_iota >= 64, tile[8*s:8*s+8], unit))
            else:
                unit = jnp.where(col_iota == row_iota + 8 * s + 64, 1.0, 0.0)
                strips.append(jnp.where(col_iota < 64, tile[8*s:8*s+8], unit))
        strips, pivots = eliminate(strips, off)
        keep = (col_iota < 64) if odd else (col_iota >= 64)
        wide = jnp.concatenate([jnp.where(keep, a * lax.rsqrt(p), 0.0) for a, p in zip(strips, pivots)], axis=0)
        turned = pltpu.roll(wide, 64, 1)
        low = wide if odd else turned
        high = turned if odd else wide
        store(b, jnp.where(lax.broadcasted_iota(jnp.int32,(32,128),1) < 64, low[32:], high[:32]))
        base = lo if odd else lo - 64
        if b < 3:
            nwin = 128 * ((b + 1) // 2)
            u = dot32(wide, g[base:base+128, nwin:nwin+128], ((1,), (0,)))
            nxt = lo + 64
            noff = 64 * (1 - odd)
            if odd:
                g[nxt:nxt+64, nwin:nwin+128] = g[nxt:nxt+64, nwin:nwin+128] - dot32(u[:, 0:64], u, ((0,), (0,)))
            else:
                g[nxt:nxt+64, nwin:nwin+128] = g[nxt:nxt+64, nwin:nwin+128] - dot32(u, u, ((0,), (0,)))[64:128]
        lines = dot32(wide, g[base : base + 128, :], ((1,), (0,)))
        g[lo:lo+64, :] = lines
        if b < 3:
            first = 64 * (b + 1)
            change = dot32(lines[:, 0:256], lines, ((0,), (0,)))
            nxt = lo + 64
            nwin = 128 * ((b + 1) // 2)
            for lo_c, hi_c in ((0, nwin), (nwin + 128, 512)):
                if hi_c > lo_c:
                    g[nxt:nxt+64, lo_c:hi_c] = g[nxt:nxt+64, lo_c:hi_c] - change[first:first+64, lo_c:hi_c]
            if b < 2:
                g[nxt+64:320, :] = g[nxt+64:320, :] - change[first+64:256, :]


def set_identity(g):
    rows = lax.broadcasted_iota(jnp.int32, (256, 256), 0)
    cols = lax.broadcasted_iota(jnp.int32, (256, 256), 1)
    g[64:320, 256:512] = jnp.where(rows == cols, 1.0, 0.0)


def gather_kernel(
    kern, acol, brow, parts,
    lead, inv0, xs, gbuf, g, x_src, inv_src, lead_stage, inv_stage, xs_stage, work,
    p_send, p_recv, p_sib_send, p_sib_recv, m_send, m_recv, m_sib_send, m_sib_recv,
    lead_send, lead_recv, gs_send, gh_recv, gd_send, gd_recv, ga_send, ga_recv, gx_send, gx_recv,
    xr_send, xh_recv, xd_send, xd_recv, xx_send, xx_recv, loc,
):
    r = lax.axis_index("row")
    c = lax.axis_index("col")
    x, y = lax.div(r, 4), lax.rem(r, 4)
    z, k = lax.div(c, 2), lax.rem(c, 2)
    zero = jnp.int32(0)
    sibling = c + 1 - 2 * k
    both = jnp.logical_and
    core0, core1 = k == 0, k == 1
    top = z == 0
    inner = jnp.logical_not(top)
    root = both(r == 0, c == 0)
    aide = both(r == 0, c == 1)
    helper = both(r == 1, c == 1)
    head = both(z == HEAD, core0)
    runner = both(core0, inner)
    skip_to = lookup(z, SKIP)
    back_to = lookup(z, BACK)
    has_skip = member(z, list(SKIP))
    has_back = member(z, list(BACK))
    parent = lookup(z, {v: q for q, v in list(SKIP.items()) + list(BACK.items())})
    children = has_skip.astype(jnp.int32) + has_back.astype(jnp.int32)
    barrier = pltpu.get_barrier_semaphore()

    def remote(src, dst, send, recv, row, col):
        return pltpu.make_async_remote_copy(
            src_ref=src, dst_ref=dst, send_sem=send, recv_sem=recv, device_id=(row, col), device_id_type=MESH
        )

    def signal(row, col):
        pl.semaphore_signal(barrier, inc=1, device_id=(row, col), device_id_type=MESH)

    def loop(lo, hi, body):
        def step(d, carry):
            body(d)
            return carry

        lax.fori_loop(lo, hi, step, 0)

    def when(cond, body):
        @pl.when(cond)
        def _():
            body()

    def start(copy):
        copy.start()

    def sent(copy):
        copy.wait_send()

    own_panel = pltpu.make_async_copy(kern.at[0, :, 0, 0], acol.at[:, k], loc.at[0])
    own_rows = pltpu.make_async_copy(kern.at[0, 0, 0], brow.at[lax.rem(r, 2), :, k], loc.at[1])
    own_lead = pltpu.make_async_copy(kern.at[0, 0, 0, 0], gbuf.at[0], loc.at[2])
    when(root, lambda: own_lead.start())
    when(top, lambda: own_panel.start())
    when(r < 2, lambda: own_rows.start())

    signal(r, sibling)

    def greet_panel():
        signal(r, 2 * parent)
        when(parent == 0, lambda: signal(r, jnp.int32(1)))

    when(runner, greet_panel)

    def greet_plane():
        loop(1, 16, lambda d: signal(lax.rem(r + d, 16), c))
        when(z != HEAD, lambda: signal(r, jnp.int32(2 * HEAD)))

    when(core1, greet_plane)

    def greet_sources():
        signal(zero, zero)
        signal(zero, jnp.int32(1))
        signal(jnp.int32(1), jnp.int32(1))

    when(head, greet_sources)
    when(root, lambda: signal(jnp.int32(1), jnp.int32(1)))

    def arrive():
        plane = jnp.where(core1, 15, 0)
        line = jnp.where(top, 2, jnp.where(core0, children, 0))
        more = jnp.where(head, 15, 0) + jnp.where(root, 16, 0) + jnp.where(aide, 16, 0) + jnp.where(helper, 17, 0)
        pl.semaphore_wait(barrier, 1 + plane + line + more)
        when(top, lambda: own_panel.wait())
        when(r < 2, lambda: own_rows.wait())

    def panel_chunk(n):
        i, half, col = lax.div(n, 4), lax.rem(lax.div(n, 2), 2), lax.rem(n, 2)
        return acol.at[i, col, pl.ds(pl.multiple_of(128 * half, 128), 128)]

    def panel_skip(n):
        return remote(panel_chunk(n), panel_chunk(n), p_send.at[n, 0], p_recv.at[n], r, 2 * skip_to)

    def panel_back(n):
        return remote(panel_chunk(n), panel_chunk(n), p_send.at[n, 1], p_recv.at[n], r, 2 * back_to)

    def panel_pair(n):
        return remote(panel_chunk(n), panel_chunk(n), p_sib_send.at[n], p_sib_recv.at[n], r, sibling)

    def panel_top(act):
        def step(m):
            n = 2 * m + k
            act(panel_skip(n))
            act(panel_back(n))

        loop(0, 8, step)
        loop(0, 8, lambda m: act(panel_pair(2 * m + k)))

    def panel_line(n):
        panel_skip(n).wait_recv()
        when(has_skip, lambda: panel_skip(n).start())
        when(has_back, lambda: panel_back(n).start())
        panel_pair(n).start()

    def panel_line_sent(n):
        when(has_skip, lambda: panel_skip(n).wait_send())
        when(has_back, lambda: panel_back(n).wait_send())
        panel_pair(n).wait_send()

    def mirror_chunk(s, m):
        j, kc, half = lax.div(m, 4), lax.rem(lax.div(m, 2), 2), lax.rem(m, 2)
        return brow.at[s, j, kc, pl.ds(pl.multiple_of(128 * half, 128), 128)]

    def mirror_copy(s, m, way, row):
        return remote(mirror_chunk(s, m), mirror_chunk(s, m), m_send.at[8 * s + m, way], m_recv.at[8 * s + m], row, c)

    def mirror_pair(s, m):
        n = 8 * s + m
        return remote(mirror_chunk(s, m), mirror_chunk(s, m), m_sib_send.at[n], m_sib_recv.at[n], r, sibling)

    def mirror_feed(j, half):
        m = 4 * j + half
        n = 8 * r + m
        return remote(mirror_chunk(r, m), mirror_chunk(r, m), m_sib_send.at[n], m_recv.at[n], r, sibling)

    def mirror_each(s, m, act):
        j, kc = lax.div(m, 4), lax.rem(lax.div(m, 2), 2)
        rel = lax.rem(y + 4 - s, 4)
        ring = jnp.logical_or(j == 1, x == 0)
        line = jnp.logical_or(j == 0, rel == 0)
        ring_up = both(ring, jnp.logical_or(rel == 0, both(s == 1, rel == 1)))
        ring_down = both(ring, jnp.logical_or(rel == 0, both(s == 0, rel == 3)))
        line_up = both(line, jnp.logical_or(x == 0, both(s == 0, x == 1)))
        line_down = both(line, jnp.logical_or(x == 0, both(s == 1, x == 3)))
        when(ring_up, lambda: act(mirror_copy(s, m, 0, x * 4 + lax.rem(y + 1, 4))))
        when(ring_down, lambda: act(mirror_copy(s, m, 1, x * 4 + lax.rem(y + 3, 4))))
        when(line_up, lambda: act(mirror_copy(s, m, 2, lax.rem(x + 1, 4) * 4 + y)))
        when(line_down, lambda: act(mirror_copy(s, m, 3, lax.rem(x + 3, 4) * 4 + y)))
        when(both(kc == 0, r != s), lambda: act(mirror_pair(s, m)))

    def mirror_step(n):
        nearer = jnp.where(jnp.logical_or(y == 0, y == 3), 0, 1)
        s = lax.rem(lax.div(n, 8) + nearer, 2)
        m = lax.rem(n, 8)
        kc = lax.rem(lax.div(m, 2), 2)
        when(jnp.logical_or(r != s, kc == 0), lambda: mirror_copy(s, m, 0, r).wait_recv())
        mirror_each(s, m, start)

    def mirror_sent(n):
        mirror_each(lax.div(n, 8), lax.rem(n, 8), sent)

    def feeds(act):
        for j in range(2):
            for half in range(2):
                act(mirror_feed(j, half))

    def mirror_take():
        for s in range(2):

            def take(s=s):
                for j in range(2):
                    for half in range(2):
                        mirror_pair(s, 4 * j + half).wait_recv()

            when(r != s, take)

    def lead_from(src, n, p):
        rows = pl.ds(pl.multiple_of(16 * p, 16), 16)
        return remote(src.at[rows], lead_stage.at[n], gs_send.at[n, p], gh_recv.at[n], p, jnp.int32(2 * HEAD))

    own_block = kern.at[0, 0, 0, 0]

    def lead_scatter(src, n, act):
        loop(0, 16, lambda p: act(lead_from(src, n, p)))

    def down(buf, which, d):
        to = lax.rem(HEAD + d, 16)
        stage = lead_stage if which == 0 else inv_stage
        return remote(stage, buf.at[r], gd_send.at[which, d], gd_recv.at[which], r, 2 * to + 1)

    def across(buf, which, d):
        return remote(
            buf.at[r], buf.at[r], ga_send.at[which, d], ga_recv.at[which, r], lax.rem(r + d, 16), c
        )

    def piece_from(buf, which, p):
        return remote(buf.at[p], buf.at[p], ga_send.at[which, 0], ga_recv.at[which, p], r, sibling)

    def pair(buf, which):
        return remote(buf, buf, gx_send.at[which], gx_recv.at[which], r, sibling)

    def head_down(buf, which):
        loop(0, 16, lambda d: down(buf, which, lax.rem(d + 8, 16)).start())

    def spread(buf, which):
        down(buf, which, 0).wait_recv()
        loop(1, 16, lambda d: across(buf, which, lax.rem(d + 9, 15) + 1).start())

    def collect(buf, which):
        loop(1, 16, lambda d: piece_from(buf, which, lax.rem(r + d, 16)).wait_recv())
        pair(buf, which).start()

    def inverse_piece(p):
        return remote(inv_src.at[p], inv_stage, xr_send.at[0, p], xh_recv.at[0], p, jnp.int32(2 * HEAD))

    def inverse_block(n):
        lo, hi = GROUPS[n]
        return pl.ds(lo, hi - lo)

    def inverse_first(n, p):
        rows = inverse_block(n)
        return remote(x_src.at[rows], xs_stage.at[rows], xr_send.at[1 + n, p], xh_recv.at[1 + n], p, jnp.int32(2 * HEAD))

    def inverse_down(n, d):
        rows = inverse_block(n)
        to = lax.rem(HEAD + d, 16)
        return remote(xs_stage.at[rows], xs.at[rows], xd_send.at[n, d], xd_recv.at[n], r, 2 * to + 1)

    def inverse_pair(n):
        block = xs.at[inverse_block(n)]
        return remote(block, block, xx_send.at[n], xx_recv.at[n], r, sibling)

    def first_all(n, act):
        loop(0, 16, lambda p: act(inverse_first(n, lax.rem(p + 10, 16))))

    def down_all(n, act):
        loop(0, 16, lambda d: act(inverse_down(n, lax.rem(d + 8, 16))))

    def lead_copy(n):
        return remote(own_block, gbuf.at[n + 1], lead_send.at[n], lead_recv.at[n], zero, zero)

    def root_main():
        own_lead.wait()
        g[0:64, :] = jnp.zeros((64, 512), jnp.float32)
        g[320:384, :] = jnp.zeros((64, 512), jnp.float32)
        g[64:320, 0:256] = gbuf[0].astype(jnp.float32)
        set_identity(g)

        def second_half():
            arrive()
            feeds(start)
            panel_top(start)
            for p in range(16):
                inv_src[p] = g[64 + 16 * p : 80 + 16 * p, 256:512]
            loop(0, 16, lambda p: inverse_piece(p).start())
            lead_copy(0).wait_recv()
            lead_copy(1).wait_recv()
            side = dot32(g[64:320, 256:512], gbuf[1].astype(jnp.float32), ((1,), (0,)))
            g[64:320, 0:256] = gbuf[2].astype(jnp.float32) - dot32(side, side, ((0,), (0,)))
            set_identity(g)

        def phase(it):
            when(it == 1, second_half)

            def store(n, packed):
                x_src[n] = packed
                for which, (lo, hi) in enumerate(GROUPS):
                    if hi == n + 1:
                        when(it == 1, lambda which=which: first_all(which, start))

            factor_phase(g, store)

        loop(0, 2, phase)

    when(root, root_main)
    when(jnp.logical_not(root), arrive)

    def zero_top():
        when(aide, lambda: lead_copy(0).start())
        when(helper, lambda: lead_copy(1).start())
        panel_top(start)
        when(both(core0, r < 2), lambda: feeds(start))

    when(both(top, jnp.logical_not(root)), zero_top)
    when(both(both(core0, r < 2), inner), lambda: feeds(start))

    when(aide, lambda: lead_scatter(own_block, 0, start))
    when(helper, lambda: lead_scatter(own_block, 1, start))

    def core1_main():
        loop(0, 16, mirror_step)
        spread(lead, 0)
        spread(inv0, 1)
        collect(lead, 0)
        collect(inv0, 1)

    when(core1, core1_main)

    def head_main():
        for n in range(2):
            lead_from(own_block, n, 0).wait_recv()
        head_down(lead, 0)
        inverse_piece(0).wait_recv()
        head_down(inv0, 1)
        for n in range(3):
            inverse_first(n, 0).wait_recv()
            down_all(n, start)

    when(head, head_main)
    when(runner, lambda: loop(0, 16, panel_line))

    def core0_take():
        pair(lead, 0).wait_recv()
        pair(inv0, 1).wait_recv()

    when(core0, core0_take)
    take = {lo: n for n, (lo, hi) in enumerate(GROUPS)}

    def inverse_take(n):
        def first():
            inverse_down(n, 0).wait_recv()
            inverse_pair(n).start()

        when(core1, first)
        when(core0, lambda: inverse_pair(n).wait_recv())

    def put(lo, hi, left, values):
        high = values.astype(jnp.bfloat16)
        parts[0, lo:hi, left : left + 256] = high
        parts[1, lo:hi, left : left + 256] = (values - high.astype(jnp.float32)).astype(jnp.bfloat16)

    def block(n):
        return jnp.concatenate([lead[p, n] for p in range(16)], axis=0).astype(jnp.float32)

    first_inverse = jnp.concatenate([inv0[p] for p in range(16)], axis=0)
    put(0, 256, 0, first_inverse)
    put(0, 256, 256, jnp.zeros((256, 256), jnp.float32))
    side = dot32(first_inverse, block(0), ((1,), (0,)))
    work[:, 0:256] = block(1) - dot32(side, side, ((0,), (0,)))
    work[:, 256:512] = -dot32(side, first_inverse, ((0,), (0,)))
    rows = lax.broadcasted_iota(jnp.int32, (256, 256), 0)
    cols = lax.broadcasted_iota(jnp.int32, (256, 256), 1)
    work[:, 512:768] = jnp.where(rows == cols, 1.0, 0.0)
    for n in range(4):
        if n in take:
            inverse_take(take[n])
        packed = xs[n]
        inverse = jnp.concatenate([packed[:, 64:128], packed[:, 0:64]], axis=0)
        lo, hi = 64 * n, 64 * n + 64
        lines = dot32(inverse, work[lo:hi, :], ((1,), (0,)))
        put(256 + lo, 256 + hi, 0, lines[:, 256:512])
        put(256 + lo, 256 + hi, 256, lines[:, 512:768])
        if n < 3:
            work[hi:256, :] = work[hi:256, :] - dot32(lines[:, hi:256], lines, ((0,), (0,)))

    when(core0, mirror_take)
    when(both(core1, inner), lambda: loop(0, 16, lambda n: panel_pair(n).wait_recv()))
    when(top, lambda: loop(0, 8, lambda m: panel_pair(2 * m + 1 - k).wait_recv()))

    when(runner, lambda: loop(0, 16, panel_line_sent))
    when(top, lambda: panel_top(sent))
    when(both(core0, r < 2), lambda: feeds(sent))

    def core1_drain():
        loop(0, 16, mirror_sent)
        for which, buf in ((0, lead), (1, inv0)):
            loop(1, 16, lambda d, which=which, buf=buf: across(buf, which, d).wait_send())
            pair(buf, which).wait_send()
        for n in range(3):
            inverse_pair(n).wait_send()

    when(core1, core1_drain)

    def head_drain():
        for which, buf in ((0, lead), (1, inv0)):
            loop(0, 16, lambda d, which=which, buf=buf: down(buf, which, d).wait_send())
        for n in range(3):
            down_all(n, sent)

    when(head, head_drain)

    def aide_drain():
        lead_copy(0).wait_send()
        lead_scatter(own_block, 0, sent)

    when(aide, aide_drain)

    def helper_drain():
        lead_copy(1).wait_send()
        lead_scatter(own_block, 1, sent)

    when(helper, helper_drain)

    def root_drain():
        loop(0, 16, lambda p: inverse_piece(p).wait_send())
        for n in range(3):
            first_all(n, sent)

    when(root, root_drain)


def gather(kernel):
    bf16, f32 = jnp.bfloat16, jnp.float32
    dma = pltpu.SemaphoreType.DMA
    return pl.pallas_call(
        gather_kernel,
        out_shape=(
            jax.ShapeDtypeStruct((4, 2, 256, 256), bf16),
            jax.ShapeDtypeStruct((2, 2, 2, 256, 256), bf16),
            jax.ShapeDtypeStruct((2, 512, 512), bf16),
        ),
        in_specs=[pl.BlockSpec(memory_space=pltpu.HBM)],
        out_specs=(
            pl.BlockSpec(memory_space=pl.ANY),
            pl.BlockSpec(memory_space=pl.ANY),
            pl.BlockSpec(memory_space=pltpu.VMEM),
        ),
        scratch_shapes=[
            pltpu.VMEM((16, 2, 16, 256), bf16),
            pltpu.VMEM((16, 16, 256), f32),
            pltpu.VMEM((4, 32, 128), f32),
            pltpu.VMEM((3, 256, 256), bf16),
            pltpu.VMEM((384, 512), f32),
            pltpu.VMEM((4, 32, 128), f32),
            pltpu.VMEM((16, 16, 256), f32),
            pltpu.VMEM((2, 16, 256), bf16),
            pltpu.VMEM((16, 256), f32),
            pltpu.VMEM((4, 32, 128), f32),
            pltpu.VMEM((256, 768), f32),
            dma((16, 2)), dma((16,)), dma((16,)), dma((16,)),
            dma((16, 4)), dma((16,)), dma((16,)), dma((16,)),
            dma((2,)), dma((2,)),
            dma((2, 16)), dma((2,)), dma((2, 16)), dma((2,)), dma((2, 16)), dma((2, 16)), dma((2,)), dma((2,)),
            dma((4, 16)), dma((4,)), dma((3, 16)), dma((3,)), dma((3,)), dma((3,)), dma((3,)),
        ],
        compiler_params=pltpu.CompilerParams(
            collective_id=0, has_side_effects=True, vmem_limit_bytes=24 * 1024 * 1024
        ),
        name="gather_and_factor",
    )(kernel)


def update_kernel(kern, acol, brow, parts, panels, schur, old, pan, new, sems):
    r = lax.axis_index("row")
    c = lax.axis_index("col")
    k = lax.rem(c, 2)
    load = pltpu.make_async_copy(kern.at[0, :, 0], old, sems.at[0])
    load.start()
    mirror = []
    for j in range(2):
        halves = []
        for n in range(2):
            total = None
            for s in range(n + 1):
                for t in range(2):
                    term = jnp.dot(
                        parts[t, 256 * n : 256 * n + 256, 256 * s : 256 * s + 256],
                        brow[s, j, k],
                        preferred_element_type=jnp.float32,
                    )
                    total = term if total is None else total + term
            halves.append(total.astype(jnp.bfloat16))
        mirror.append(jnp.concatenate(halves, axis=0))
    tri = lax.broadcasted_iota(jnp.int32, (256, 256), 0) >= lax.broadcasted_iota(jnp.int32, (256, 256), 1)
    stores = []
    load.wait()
    for i in range(4):
        solved = []
        for n in range(2):
            total = None
            for s in range(n + 1):
                for t in range(2):
                    term = lax.dot_general(
                        acol[i, s],
                        parts[t, 256 * n : 256 * n + 256, 256 * s : 256 * s + 256],
                        (((1,), (1,)), ((), ())),
                        preferred_element_type=jnp.float32,
                    )
                    total = term if total is None else total + term
            solved.append(total)
        left = jnp.concatenate([a.astype(jnp.bfloat16) for a in solved], axis=1)
        if i == 0:
            solved[0] = jnp.where(jnp.logical_or(r != 0, tri), solved[0], 0.0)
            solved[1] = jnp.where(jnp.logical_or(r > 1, jnp.logical_and(r == 1, tri)), solved[1], 0.0)
        for n in range(2):
            pan[i, n] = solved[n]
        stores.append(pltpu.make_async_copy(pan.at[i], panels.at[0, i], sems.at[1 + 2 * i]))
        stores[-1].start()
        for j in range(2):
            change = jnp.dot(left, mirror[j], preferred_element_type=jnp.float32)
            out = (old[i, j].astype(jnp.float32) - change).astype(jnp.bfloat16)
            if i == 0:
                out = jnp.where(r >= 2, out, jnp.zeros_like(out))
            if j == 0:
                out = jnp.where(c >= 2, out, jnp.zeros_like(out))
            new[i, j] = out
        stores.append(pltpu.make_async_copy(new.at[i], schur.at[0, i, 0], sems.at[2 + 2 * i]))
        stores[-1].start()
    for store in stores:
        store.wait()


def update(kernel, *gathered):
    hbm = pl.BlockSpec(memory_space=pltpu.HBM)
    return pl.pallas_call(
        update_kernel,
        out_shape=(
            jax.ShapeDtypeStruct((1, 4, 2, 256, 256), jnp.float32),
            jax.ShapeDtypeStruct((1, 4, 1, 2, 256, 256), jnp.bfloat16),
        ),
        in_specs=[hbm] + [pl.BlockSpec(memory_space=pltpu.VMEM)] * 3,
        out_specs=(hbm, hbm),
        scratch_shapes=[
            pltpu.VMEM((4, 2, 256, 256), jnp.bfloat16),
            pltpu.VMEM((4, 2, 256, 256), jnp.float32),
            pltpu.VMEM((4, 2, 256, 256), jnp.bfloat16),
            pltpu.SemaphoreType.DMA((9,)),
        ],
        compiler_params=pltpu.CompilerParams(vmem_limit_bytes=32 * 1024 * 1024),
        name="solve_and_update",
    )(kernel, *gathered)


def per_device(kernel):
    return update(kernel, *gather(kernel))


def solution(mesh):
    in_specs = (P("row", None, "col", None, None, None),)
    out_specs = (P("row", None, None, None, None), P("row", None, "col", None, None, None))
    return jax.shard_map(per_device, mesh=mesh, in_specs=in_specs, out_specs=out_specs, check_vma=False)
```

```python
import functools

import jax
import jax.numpy as jnp
from jax import lax
from jax.experimental import pallas as pl
from jax.experimental.pallas import tpu as pltpu
from jax.sharding import PartitionSpec as P

MESH = pl.DeviceIdType.MESH
HI = lax.Precision.HIGHEST
GROUPS = ((0, 2), (2, 3), (3, 4))
PLANE = sorted(((a, b) for a in range(4) for b in range(4) if a or b), key=lambda d: -min(d[0], 4 - d[0]) - min(d[1], 4 - d[1]))
LINE = sorted(range(1, 16), key=lambda d: -min(d, 16 - d))
SKIP = {0: 3, 3: 6, 6: 8, 13: 10, 10: 9}
BACK = {0: 13, 3: 2, 2: 1, 6: 5, 5: 4, 8: 7, 13: 14, 14: 15, 10: 11, 11: 12}


def lookup(key, pairs):
    value = jnp.int32(0)
    for k, v in pairs.items():
        value = jnp.where(key == k, jnp.int32(v), value)
    return value


def member(key, keys):
    hit = key == keys[0]
    for k in keys[1:]:
        hit = jnp.logical_or(hit, key == k)
    return hit


def dot32(a, b, dims):
    return lax.dot_general(a, b, (dims, ((), ())), precision=HI, preferred_element_type=jnp.float32)


def row(v, i):
    return jnp.broadcast_to(v[i : i + 1, :], (8, 128))

def lane(v, i):
    return jnp.broadcast_to(v[:, i : i + 1], (8, 128))


def eliminate(strips, off):
    row_iota = lax.broadcasted_iota(jnp.int32, (8, 128), 0)
    strips = list(strips)
    diag = [lane(strips[0], off + i) for i in range(8)]
    pivots = []
    for s in range(8):
        later = range(s + 1, 8)
        cols = {t: [lane(strips[t], off + 8 * s + i) for i in range(8)] for t in later}
        if s < 7:
            raw = [lane(strips[s + 1], off + 8 * (s + 1) + i) for i in range(8)]
        head = strips[s]
        pivot = jnp.zeros((8, 128), jnp.float32)
        recips = []
        for i in range(8):
            own = diag[i]
            recip = 1.0 / row(own, i)
            recips.append(recip)
            pivot = jnp.where(row_iota == i, own, pivot)
            for j in range(i + 1, 8):
                line = row(own, j)
                diag[j] = diag[j] - (own * line) * recip
                factor = line * recip
                for t in later:
                    cols[t][j] = cols[t][j] - cols[t][i] * factor
            head = head - jnp.where(row_iota > i, own * recip, 0.0) * row(head, i)
        strips[s] = head
        pivots.append(pivot)
        if s < 7:
            near = cols[s + 1]
            scaled = [near[i] * recips[i] for i in range(8)]
            diag = []
            for j in range(8):
                terms = [scaled[i] * row(near[i], j) for i in range(8)]
                while len(terms) > 1:
                    terms = [terms[a] + terms[a + 1] for a in range(0, len(terms), 2)]
                diag.append(raw[j] - terms[0])
        heads = [row(head, i) * recips[i] for i in range(8)]
        for t in later:
            terms = [cols[t][i] * heads[i] for i in range(8)]
            while len(terms) > 1:
                terms = [terms[a] + terms[a + 1] for a in range(0, len(terms), 2)]
            strips[t] = strips[t] - terms[0]
    return strips, pivots


def factor_phase(g, store, middle):
    col_iota = lax.broadcasted_iota(jnp.int32, (8, 128), 1)
    row_iota = lax.broadcasted_iota(jnp.int32, (8, 128), 0)
    for b in range(4):
        odd = b % 2
        lo = 64 + 64 * b
        win = 128 * (b // 2)
        off = 64 * odd
        strips = []
        tile = g[lo:lo+64, win:win+128]
        for s in range(8):
            if odd:
                unit = jnp.where(col_iota == row_iota + 8 * s, 1.0, 0.0)
                strips.append(jnp.where(col_iota >= 64, tile[8*s:8*s+8], unit))
            else:
                unit = jnp.where(col_iota == row_iota + 8 * s + 64, 1.0, 0.0)
                strips.append(jnp.where(col_iota < 64, tile[8*s:8*s+8], unit))
        strips, pivots = eliminate(strips, off)
        keep = (col_iota < 64) if odd else (col_iota >= 64)
        wide = jnp.concatenate([jnp.where(keep, a * lax.rsqrt(p), 0.0) for a, p in zip(strips, pivots)], axis=0)
        turned = pltpu.roll(wide, 64, 1)
        low = wide if odd else turned
        high = turned if odd else wide
        if b == 1:
            middle()
        store(b, jnp.where(lax.broadcasted_iota(jnp.int32,(32,128),1) < 64, low[32:], high[:32]))
        base = lo if odd else lo - 64
        if b < 3:
            nwin = 128 * ((b + 1) // 2)
            u = dot32(wide, g[base:base+128, nwin:nwin+128], ((1,), (0,)))
            nxt = lo + 64
            noff = 64 * (1 - odd)
            if odd:
                g[nxt:nxt+64, nwin:nwin+128] = g[nxt:nxt+64, nwin:nwin+128] - dot32(u[:, 0:64], u, ((0,), (0,)))
            else:
                g[nxt:nxt+64, nwin:nwin+128] = g[nxt:nxt+64, nwin:nwin+128] - dot32(u, u, ((0,), (0,)))[64:128]
        lines = dot32(wide, g[base : base + 128, :], ((1,), (0,)))
        g[lo:lo+64, :] = lines
        if b < 3:
            first = 64 * (b + 1)
            change = dot32(lines[:, 0:256], lines, ((0,), (0,)))
            nxt = lo + 64
            nwin = 128 * ((b + 1) // 2)
            for lo_c, hi_c in ((0, nwin), (nwin + 128, 512)):
                if hi_c > lo_c:
                    g[nxt:nxt+64, lo_c:hi_c] = g[nxt:nxt+64, lo_c:hi_c] - change[first:first+64, lo_c:hi_c]
            if b < 2:
                g[nxt+64:320, :] = g[nxt+64:320, :] - change[first+64:256, :]


def set_identity(g):
    rows = lax.broadcasted_iota(jnp.int32, (256, 256), 0)
    cols = lax.broadcasted_iota(jnp.int32, (256, 256), 1)
    g[64:320, 256:512] = jnp.where(rows == cols, 1.0, 0.0)


def gather_kernel(
    kern, acol, brow, parts,
    lead, inv0, xs, gbuf, g, x_src, inv_src, lead_stage, inv_stage, xs_stage, work,
    p_send, p_recv, p_sib_send, p_sib_recv, m_send, m_recv, m_sib_send, m_sib_recv,
    lead_send, lead_recv, gs_send, gh_recv, gd_send, gd_recv, ga_send, ga_recv, gx_send, gx_recv,
    xr_send, xh_recv, xd_send, xd_recv, xx_send, xx_recv, loc,
):
    r = lax.axis_index("row")
    c = lax.axis_index("col")
    x, y = lax.div(r, 4), lax.rem(r, 4)
    z, k = lax.div(c, 2), lax.rem(c, 2)
    zero, one = jnp.int32(0), jnp.int32(1)
    sibling = c + 1 - 2 * k
    both, neither = jnp.logical_and, jnp.logical_not
    top = z == 0
    inner = neither(top)

    def hub_core(row):
        return jnp.where(both(top, row != 0), 0, 1)

    hub = k == hub_core(r)
    mate = neither(hub)
    root = both(r == 0, c == 0)
    aide = both(r == 0, c == 1)
    helper = both(r == 1, c == 1)
    head = both(c == 1, r != 0)
    runner = both(k == 0, inner)
    skip_to = lookup(z, SKIP)
    back_to = lookup(z, BACK)
    has_skip = member(z, list(SKIP))
    has_back = member(z, list(BACK))
    parent = lookup(z, {v: q for q, v in list(SKIP.items()) + list(BACK.items())})
    children = has_skip.astype(jnp.int32) + has_back.astype(jnp.int32)
    barrier = pltpu.get_barrier_semaphore()

    def remote(src, dst, send, recv, row, col):
        return pltpu.make_async_remote_copy(
            src_ref=src, dst_ref=dst, send_sem=send, recv_sem=recv, device_id=(row, col), device_id_type=MESH
        )

    def signal(row, col):
        pl.semaphore_signal(barrier, inc=1, device_id=(row, col), device_id_type=MESH)

    def loop(lo, hi, body):
        def step(d, carry):
            body(d)
            return carry

        lax.fori_loop(lo, hi, step, 0)

    def when(cond, body):
        @pl.when(cond)
        def _():
            body()

    def start(copy):
        copy.start()

    def sent(copy):
        copy.wait_send()

    def peer(d):
        return lax.rem(x + d[0], 4) * 4 + lax.rem(y + d[1], 4)

    own_block = kern.at[0, 0, 0, 0]
    own_panel = pltpu.make_async_copy(kern.at[0, :, 0, 0], acol.at[:, k], loc.at[0])
    own_rows = pltpu.make_async_copy(kern.at[0, 0, 0], brow.at[lax.rem(r, 2), :, k], loc.at[1])
    own_lead = pltpu.make_async_copy(own_block, gbuf.at[0], loc.at[2])
    aide_piece = pltpu.make_async_copy(own_block.at[pl.ds(0, 16)], lead.at[0, 0], loc.at[2])
    helper_piece = pltpu.make_async_copy(own_block.at[pl.ds(16, 16)], lead_stage.at[1], loc.at[2])
    when(root, lambda: own_lead.start())
    when(aide, lambda: aide_piece.start())
    when(helper, lambda: helper_piece.start())
    when(top, lambda: own_panel.start())
    when(r < 2, lambda: own_rows.start())

    signal(r, sibling)

    def greet_panel():
        signal(r, 2 * parent)
        when(parent == 0, lambda: signal(r, one))

    when(runner, greet_panel)

    def greet_plane():
        for d in PLANE:
            signal(peer(d), 2 * z + hub_core(peer(d)))
        when(inner, lambda: signal(r, one))

    when(hub, greet_plane)

    def greet_sources():
        signal(zero, zero)
        signal(zero, one)
        when(r != 1, lambda: signal(one, one))

    when(head, greet_sources)
    when(jnp.logical_or(root, aide), lambda: signal(one, one))

    def arrive():
        plane = jnp.where(hub, 15, 0)
        line = jnp.where(top, 2, jnp.where(k == 0, children, 0))
        down = jnp.where(c == 1, 15, 0)
        more = jnp.where(root, 15, 0) + jnp.where(aide, 15, 0) + jnp.where(helper, 16, 0)
        pl.semaphore_wait(barrier, 1 + plane + line + down + more)
        when(top, lambda: own_panel.wait())
        when(r < 2, lambda: own_rows.wait())
        when(aide, lambda: aide_piece.wait())
        when(helper, lambda: helper_piece.wait())

    def panel_chunk(n):
        col, i, half = lax.div(n, 8), lax.rem(lax.div(n, 2), 4), lax.rem(n, 2)
        return acol.at[i, col, pl.ds(pl.multiple_of(128 * half, 128), 128)]

    def panel_skip(n):
        return remote(panel_chunk(n), panel_chunk(n), p_send.at[n, 0], p_recv.at[n], r, 2 * skip_to)

    def panel_back(n):
        return remote(panel_chunk(n), panel_chunk(n), p_send.at[n, 1], p_recv.at[n], r, 2 * back_to)

    def panel_pair(n):
        return remote(panel_chunk(n), panel_chunk(n), p_sib_send.at[n], p_sib_recv.at[n], r, sibling)

    def panel_top(act):
        def step(m):
            act(panel_skip(8 * k + m))
            act(panel_back(8 * k + m))

        loop(0, 8, step)
        loop(0, 8, lambda m: act(panel_pair(8 * k + m)))

    def panel_line(t):
        n = lax.rem(t + jnp.where(r == 0, 8, 0), 16)
        panel_skip(n).wait_recv()
        when(has_skip, lambda: panel_skip(n).start())
        when(has_back, lambda: panel_back(n).start())
        panel_pair(n).start()

    def panel_line_sent(n):
        when(has_skip, lambda: panel_skip(n).wait_send())
        when(has_back, lambda: panel_back(n).wait_send())
        panel_pair(n).wait_send()

    def mirror_chunk(s, m):
        j, kc, half = lax.div(m, 4), lax.rem(lax.div(m, 2), 2), lax.rem(m, 2)
        return brow.at[s, j, kc, pl.ds(pl.multiple_of(128 * half, 128), 128)]

    def mirror_copy(s, m, way, row):
        chunk = mirror_chunk(s, m)
        return remote(chunk, chunk, m_send.at[8 * s + m, way], m_recv.at[8 * s + m], row, 2 * z + hub_core(row))

    def mirror_pair(s, m):
        n = 8 * s + m
        return remote(mirror_chunk(s, m), mirror_chunk(s, m), m_sib_send.at[n], m_sib_recv.at[n], r, sibling)

    def mirror_feed(j, half):
        m = 4 * j + 2 * k + half
        n = 8 * r + m
        return remote(mirror_chunk(r, m), mirror_chunk(r, m), m_sib_send.at[n], m_recv.at[n], r, sibling)

    def mirror_each(s, m, act):
        j, kc = lax.div(m, 4), lax.rem(lax.div(m, 2), 2)
        rel = lax.rem(y + 4 - s, 4)
        ring = jnp.logical_or(j == 1, x == 0)
        line = jnp.logical_or(j == 0, rel == 0)
        ring_up = both(ring, jnp.logical_or(rel == 0, both(s == 1, rel == 1)))
        ring_down = both(ring, jnp.logical_or(rel == 0, both(s == 0, rel == 3)))
        line_up = both(line, jnp.logical_or(x == 0, both(s == 0, x == 1)))
        line_down = both(line, jnp.logical_or(x == 0, both(s == 1, x == 3)))
        when(ring_up, lambda: act(mirror_copy(s, m, 0, peer((0, 1)))))
        when(ring_down, lambda: act(mirror_copy(s, m, 1, peer((0, 3)))))
        when(line_up, lambda: act(mirror_copy(s, m, 2, peer((1, 0)))))
        when(line_down, lambda: act(mirror_copy(s, m, 3, peer((3, 0)))))
        when(both(kc != k, r != s), lambda: act(mirror_pair(s, m)))

    def mirror_step(n):
        nearer = jnp.where(jnp.logical_or(y == 0, y == 3), 0, 1)
        s = lax.rem(lax.div(n, 8) + nearer, 2)
        m = lax.rem(n, 8)
        kc = lax.rem(lax.div(m, 2), 2)
        when(jnp.logical_or(r != s, kc != k), lambda: mirror_copy(s, m, 0, r).wait_recv())
        mirror_each(s, m, start)

    def mirror_sent(n):
        mirror_each(lax.div(n, 8), lax.rem(n, 8), sent)

    def feeds(act):
        for j in range(2):
            for half in range(2):
                act(mirror_feed(j, half))

    def mirror_take():
        for s in range(2):

            def take(s=s):
                for j in range(2):
                    for half in range(2):
                        mirror_pair(s, 4 * j + 2 * k + half).wait_recv()

            when(r != s, take)

    def lead_from(n, p):
        rows = own_block.at[pl.ds(16 * p, 16)]
        to = lead.at[0, n] if p == 0 else lead_stage.at[n]
        return remote(rows, to, gs_send.at[p], gh_recv.at[n], jnp.int32(p), one)

    def lead_scatter(n, act):
        for p in range(16):
            if p != n:
                act(lead_from(n, p))

    def head_copies(buf, stage, send, recv):
        out = []
        for d in LINE:
            out.append((None, remote(stage, buf, send.at[d], recv, r, jnp.int32(2 * d + 1))))
        out.append((r != 0, remote(stage, buf, send.at[0], recv, r, zero)))
        return out

    def each(copies, act):
        for cond, copy in copies:
            if cond is None:
                act(copy)
            else:
                when(cond, lambda copy=copy: act(copy))

    def down(which, act):
        buf, stage = ((lead, lead_stage), (inv0, inv_stage))[which]
        send, recv = gd_send.at[which], gd_recv.at[which]
        when(r != 0, lambda: each(head_copies(buf.at[r], stage, send, recv), act))
        when(r == 0, lambda: each(head_copies(buf.at[0], buf.at[0], send, recv), act))

    def down_taken(which):
        buf = (lead, inv0)[which]
        remote(buf.at[r], buf.at[r], gd_send.at[which, 0], gd_recv.at[which], r, sibling).wait_recv()

    def across(which, act):
        buf = (lead, inv0)[which]
        for n, d in enumerate(PLANE):
            row = peer(d)
            act(remote(buf.at[r], buf.at[r], ga_send.at[which, n], ga_recv.at[which, r], row, 2 * z + hub_core(row)))

    def pair(which):
        buf = (lead, inv0)[which]
        return remote(buf, buf, gx_send.at[which], gx_recv.at[which], r, sibling)

    def spread(which):
        when(neither(aide), lambda: down_taken(which))
        across(which, start)

    def collect(which):
        buf = (lead, inv0)[which]

        def take(d):
            p = lax.rem(r + d, 16)
            remote(buf.at[p], buf.at[p], ga_send.at[which, 0], ga_recv.at[which, p], r, sibling).wait_recv()

        loop(1, 16, take)
        pair(which).start()

    def inverse_piece(p):
        to = inv0.at[0] if p == 0 else inv_stage
        return remote(inv_src.at[p], to, xr_send.at[0, p], xh_recv.at[0], jnp.int32(p), one)

    def inverse_first(n, p):
        lo, hi = GROUPS[n]
        rows = pl.ds(lo, hi - lo)
        to = xs if p == 0 else xs_stage
        return remote(x_src.at[rows], to.at[rows], xr_send.at[1 + n, p], xh_recv.at[1 + n], jnp.int32(p), one)

    def from_root(act, copy):
        for d in PLANE:
            act(copy(4 * d[0] + d[1]))
        act(copy(0))

    def first_all(n, act):
        from_root(act, lambda p: inverse_first(n, p))

    def inverse_down(n, act):
        lo, hi = GROUPS[n]
        rows = pl.ds(lo, hi - lo)
        send, recv = xd_send.at[n], xd_recv.at[n]
        when(r != 0, lambda: each(head_copies(xs.at[rows], xs_stage.at[rows], send, recv), act))
        when(r == 0, lambda: each(head_copies(xs.at[rows], xs.at[rows], send, recv), act))

    def inverse_taken(n):
        lo, hi = GROUPS[n]
        rows = xs.at[pl.ds(lo, hi - lo)]
        remote(rows, rows, xd_send.at[n, 0], xd_recv.at[n], r, sibling).wait_recv()

    def inverse_pair(n):
        lo, hi = GROUPS[n]
        rows = xs.at[pl.ds(lo, hi - lo)]
        return remote(rows, rows, xx_send.at[n], xx_recv.at[n], r, sibling)

    def lead_copy(n):
        return remote(own_block, gbuf.at[n + 1], lead_send.at[n], lead_recv.at[n], zero, zero)

    def root_main():
        own_lead.wait()
        g[0:64, :] = jnp.zeros((64, 512), jnp.float32)
        g[320:384, :] = jnp.zeros((64, 512), jnp.float32)
        g[64:320, 0:256] = gbuf[0].astype(jnp.float32)
        set_identity(g)

        def bulk():
            arrive()
            feeds(start)
            panel_top(start)

        def second_half():
            for p in range(16):
                inv_src[p] = g[64 + 16 * p : 80 + 16 * p, 256:512]
            from_root(start, inverse_piece)
            lead_copy(0).wait_recv()
            lead_copy(1).wait_recv()
            side = dot32(g[64:320, 256:512], gbuf[1].astype(jnp.float32), ((1,), (0,)))
            g[64:320, 0:256] = gbuf[2].astype(jnp.float32) - dot32(side, side, ((0,), (0,)))
            set_identity(g)

        def phase(it):
            def store(n, packed):
                x_src[n] = packed
                for which, (lo, hi) in enumerate(GROUPS):
                    if hi == n + 1:
                        when(it == 1, lambda which=which: first_all(which, start))

            factor_phase(g, store, lambda: when(it == 0, bulk))
            when(it == 0, second_half)

        loop(0, 2, phase)

    when(root, root_main)
    when(neither(root), arrive)

    def top_sends():
        when(aide, lambda: lead_copy(0).start())
        when(helper, lambda: lead_copy(1).start())
        panel_top(start)
        when(aide, lambda: lead_scatter(0, start))
        when(helper, lambda: lead_scatter(1, start))

    when(both(top, neither(root)), top_sends)
    when(both(both(mate, r < 2), neither(root)), lambda: feeds(start))

    def hub_main():
        loop(0, 16, mirror_step)

        def aide_down():
            lead_from(1, 0).wait_recv()
            down(0, start)
            inverse_piece(0).wait_recv()
            down(1, start)

        when(aide, aide_down)
        spread(0)
        spread(1)
        collect(0)
        collect(1)

    when(hub, hub_main)

    def head_main():
        lead_from(0, 1).wait_recv()
        when(neither(helper), lambda: lead_from(1, 2).wait_recv())
        down(0, start)
        inverse_piece(1).wait_recv()
        down(1, start)
        for n in range(3):
            inverse_first(n, 1).wait_recv()
            inverse_down(n, start)

    when(head, head_main)
    when(runner, lambda: loop(0, 16, panel_line))

    def mate_take():
        pair(0).wait_recv()
        pair(1).wait_recv()

    when(mate, mate_take)
    take = {lo: n for n, (lo, hi) in enumerate(GROUPS)}

    def inverse_take(n):
        def as_hub():
            def as_aide():
                inverse_first(n, 0).wait_recv()
                inverse_down(n, start)

            when(aide, as_aide)
            when(neither(aide), lambda: inverse_taken(n))
            inverse_pair(n).start()

        when(hub, as_hub)
        when(mate, lambda: inverse_pair(n).wait_recv())

    def put(lo, hi, left, values):
        high = values.astype(jnp.bfloat16)
        parts[0, lo:hi, left : left + 256] = high
        parts[1, lo:hi, left : left + 256] = (values - high.astype(jnp.float32)).astype(jnp.bfloat16)

    def block(n):
        return jnp.concatenate([lead[p, n] for p in range(16)], axis=0).astype(jnp.float32)

    first_inverse = jnp.concatenate([inv0[p] for p in range(16)], axis=0)
    put(0, 256, 0, first_inverse)
    put(0, 256, 256, jnp.zeros((256, 256), jnp.float32))
    side = dot32(first_inverse, block(0), ((1,), (0,)))
    work[:, 0:256] = block(1) - dot32(side, side, ((0,), (0,)))
    work[:, 256:512] = -dot32(side, first_inverse, ((0,), (0,)))
    rows = lax.broadcasted_iota(jnp.int32, (256, 256), 0)
    cols = lax.broadcasted_iota(jnp.int32, (256, 256), 1)
    work[:, 512:768] = jnp.where(rows == cols, 1.0, 0.0)
    for n in range(4):
        if n in take:
            inverse_take(take[n])
        packed = xs[n]
        inverse = jnp.concatenate([packed[:, 64:128], packed[:, 0:64]], axis=0)
        lo, hi = 64 * n, 64 * n + 64
        lines = dot32(inverse, work[lo:hi, :], ((1,), (0,)))
        put(256 + lo, 256 + hi, 0, lines[:, 256:512])
        put(256 + lo, 256 + hi, 256, lines[:, 512:768])
        if n < 3:
            work[hi:256, :] = work[hi:256, :] - dot32(lines[:, hi:256], lines, ((0,), (0,)))

    when(mate, mirror_take)
    when(both(hub, inner), lambda: loop(0, 16, lambda n: panel_pair(n).wait_recv()))
    when(top, lambda: loop(0, 8, lambda m: panel_pair(8 * (1 - k) + m).wait_recv()))

    when(runner, lambda: loop(0, 16, panel_line_sent))
    when(top, lambda: panel_top(sent))
    when(both(mate, r < 2), lambda: feeds(sent))

    def hub_drain():
        loop(0, 16, mirror_sent)
        for which in range(2):
            across(which, sent)
            pair(which).wait_send()
        for n in range(3):
            inverse_pair(n).wait_send()

    when(hub, hub_drain)

    def line_drain():
        for which in range(2):
            down(which, sent)
        for n in range(3):
            inverse_down(n, sent)

    when(c == 1, line_drain)

    def aide_drain():
        lead_copy(0).wait_send()
        lead_scatter(0, sent)

    when(aide, aide_drain)

    def helper_drain():
        lead_copy(1).wait_send()
        lead_scatter(1, sent)

    when(helper, helper_drain)

    def root_drain():
        from_root(sent, inverse_piece)
        for n in range(3):
            first_all(n, sent)

    when(root, root_drain)


def gather(kernel):
    bf16, f32 = jnp.bfloat16, jnp.float32
    dma = pltpu.SemaphoreType.DMA
    return pl.pallas_call(
        gather_kernel,
        out_shape=(
            jax.ShapeDtypeStruct((4, 2, 256, 256), bf16),
            jax.ShapeDtypeStruct((2, 2, 2, 256, 256), bf16),
            jax.ShapeDtypeStruct((2, 512, 512), bf16),
        ),
        in_specs=[pl.BlockSpec(memory_space=pltpu.HBM)],
        out_specs=(
            pl.BlockSpec(memory_space=pl.ANY),
            pl.BlockSpec(memory_space=pl.ANY),
            pl.BlockSpec(memory_space=pltpu.VMEM),
        ),
        scratch_shapes=[
            pltpu.VMEM((16, 2, 16, 256), bf16),
            pltpu.VMEM((16, 16, 256), f32),
            pltpu.VMEM((4, 32, 128), f32),
            pltpu.VMEM((3, 256, 256), bf16),
            pltpu.VMEM((384, 512), f32),
            pltpu.VMEM((4, 32, 128), f32),
            pltpu.VMEM((16, 16, 256), f32),
            pltpu.VMEM((2, 16, 256), bf16),
            pltpu.VMEM((16, 256), f32),
            pltpu.VMEM((4, 32, 128), f32),
            pltpu.VMEM((256, 768), f32),
            dma((16, 2)), dma((16,)), dma((16,)), dma((16,)),
            dma((16, 4)), dma((16,)), dma((16,)), dma((16,)),
            dma((2,)), dma((2,)),
            dma((16,)), dma((2,)), dma((2, 16)), dma((2,)), dma((2, 16)), dma((2, 16)), dma((2,)), dma((2,)),
            dma((4, 16)), dma((4,)), dma((3, 16)), dma((3,)), dma((3,)), dma((3,)), dma((3,)),
        ],
        compiler_params=pltpu.CompilerParams(
            collective_id=0, has_side_effects=True, vmem_limit_bytes=24 * 1024 * 1024
        ),
        name="gather_and_factor",
    )(kernel)


def update_kernel(kern, acol, brow, parts, panels, schur, old, pan, new, sems):
    r = lax.axis_index("row")
    c = lax.axis_index("col")
    k = lax.rem(c, 2)
    load = pltpu.make_async_copy(kern.at[0, :, 0], old, sems.at[0])
    load.start()
    mirror = []
    for j in range(2):
        halves = []
        for n in range(2):
            total = None
            for s in range(n + 1):
                for t in range(2):
                    term = jnp.dot(
                        parts[t, 256 * n : 256 * n + 256, 256 * s : 256 * s + 256],
                        brow[s, j, k],
                        preferred_element_type=jnp.float32,
                    )
                    total = term if total is None else total + term
            halves.append(total.astype(jnp.bfloat16))
        mirror.append(jnp.concatenate(halves, axis=0))
    tri = lax.broadcasted_iota(jnp.int32, (256, 256), 0) >= lax.broadcasted_iota(jnp.int32, (256, 256), 1)
    stores = []
    load.wait()
    for i in range(4):
        solved = []
        for n in range(2):
            total = None
            for s in range(n + 1):
                for t in range(2):
                    term = lax.dot_general(
                        acol[i, s],
                        parts[t, 256 * n : 256 * n + 256, 256 * s : 256 * s + 256],
                        (((1,), (1,)), ((), ())),
                        preferred_element_type=jnp.float32,
                    )
                    total = term if total is None else total + term
            solved.append(total)
        left = jnp.concatenate([a.astype(jnp.bfloat16) for a in solved], axis=1)
        if i == 0:
            solved[0] = jnp.where(jnp.logical_or(r != 0, tri), solved[0], 0.0)
            solved[1] = jnp.where(jnp.logical_or(r > 1, jnp.logical_and(r == 1, tri)), solved[1], 0.0)
        for n in range(2):
            pan[i, n] = solved[n]
        stores.append(pltpu.make_async_copy(pan.at[i], panels.at[0, i], sems.at[1 + 2 * i]))
        stores[-1].start()
        for j in range(2):
            change = jnp.dot(left, mirror[j], preferred_element_type=jnp.float32)
            out = (old[i, j].astype(jnp.float32) - change).astype(jnp.bfloat16)
            if i == 0:
                out = jnp.where(r >= 2, out, jnp.zeros_like(out))
            if j == 0:
                out = jnp.where(c >= 2, out, jnp.zeros_like(out))
            new[i, j] = out
        stores.append(pltpu.make_async_copy(new.at[i], schur.at[0, i, 0], sems.at[2 + 2 * i]))
        stores[-1].start()
    for store in stores:
        store.wait()


def update(kernel, *gathered):
    hbm = pl.BlockSpec(memory_space=pltpu.HBM)
    return pl.pallas_call(
        update_kernel,
        out_shape=(
            jax.ShapeDtypeStruct((1, 4, 2, 256, 256), jnp.float32),
            jax.ShapeDtypeStruct((1, 4, 1, 2, 256, 256), jnp.bfloat16),
        ),
        in_specs=[hbm] + [pl.BlockSpec(memory_space=pltpu.VMEM)] * 3,
        out_specs=(hbm, hbm),
        scratch_shapes=[
            pltpu.VMEM((4, 2, 256, 256), jnp.bfloat16),
            pltpu.VMEM((4, 2, 256, 256), jnp.float32),
            pltpu.VMEM((4, 2, 256, 256), jnp.bfloat16),
            pltpu.SemaphoreType.DMA((9,)),
        ],
        compiler_params=pltpu.CompilerParams(vmem_limit_bytes=32 * 1024 * 1024),
        name="solve_and_update",
    )(kernel, *gathered)


def per_device(kernel):
    kernel = pltpu.with_memory_space_constraint(kernel, pltpu.HBM)
    return update(kernel, *gather(kernel))


def solution(mesh):
    in_specs = (P("row", None, "col", None, None, None),)
    out_specs = (P("row", None, None, None, None), P("row", None, "col", None, None, None))
    return jax.shard_map(per_device, mesh=mesh, in_specs=in_specs, out_specs=out_specs, check_vma=False)
```

```python
import functools

import jax
import jax.numpy as jnp
from jax import lax
from jax.experimental import pallas as pl
from jax.experimental.pallas import tpu as pltpu
from jax.sharding import PartitionSpec as P

MESH = pl.DeviceIdType.MESH
HI = lax.Precision.HIGHEST
GROUPS = ((0, 3), (3, 4))
PLANE = sorted(((a, b) for a in range(4) for b in range(4) if a or b), key=lambda d: -min(d[0], 4 - d[0]) - min(d[1], 4 - d[1]))
NEAR = ((0, 1), (0, 3), (1, 0), (3, 0))
LINE = sorted(range(1, 16), key=lambda d: -min(d, 16 - d))
SKIP = {0: 3, 3: 6, 6: 8, 13: 10, 10: 9}
BACK = {0: 13, 3: 2, 2: 1, 6: 5, 5: 4, 8: 7, 13: 14, 14: 15, 10: 11, 11: 12}


def lookup(key, pairs):
    value = jnp.int32(0)
    for k, v in pairs.items():
        value = jnp.where(key == k, jnp.int32(v), value)
    return value


def member(key, keys):
    hit = key == keys[0]
    for k in keys[1:]:
        hit = jnp.logical_or(hit, key == k)
    return hit


def dot32(a, b, dims):
    return lax.dot_general(a, b, (dims, ((), ())), precision=HI, preferred_element_type=jnp.float32)


def row(v, i):
    return jnp.broadcast_to(v[i : i + 1, :], (8, 128))

def lane(v, i):
    return jnp.broadcast_to(v[:, i : i + 1], (8, 128))


def eliminate(strips, off):
    row_iota = lax.broadcasted_iota(jnp.int32, (8, 128), 0)
    strips = list(strips)
    diag = [lane(strips[0], off + i) for i in range(8)]
    pivots = []
    for s in range(8):
        later = range(s + 1, 8)
        cols = {t: [lane(strips[t], off + 8 * s + i) for i in range(8)] for t in later}
        if s < 7:
            raw = [lane(strips[s + 1], off + 8 * (s + 1) + i) for i in range(8)]
        head = strips[s]
        pivot = jnp.zeros((8, 128), jnp.float32)
        recips = []
        for i in range(8):
            own = diag[i]
            recip = 1.0 / row(own, i)
            recips.append(recip)
            pivot = jnp.where(row_iota == i, own, pivot)
            for j in range(i + 1, 8):
                line = row(own, j)
                diag[j] = diag[j] - (own * line) * recip
                factor = line * recip
                for t in later:
                    cols[t][j] = cols[t][j] - cols[t][i] * factor
            head = head - jnp.where(row_iota > i, own * recip, 0.0) * row(head, i)
        strips[s] = head
        pivots.append(pivot)
        if s < 7:
            near = cols[s + 1]
            scaled = [near[i] * recips[i] for i in range(8)]
            diag = []
            for j in range(8):
                terms = [scaled[i] * row(near[i], j) for i in range(8)]
                while len(terms) > 1:
                    terms = [terms[a] + terms[a + 1] for a in range(0, len(terms), 2)]
                diag.append(raw[j] - terms[0])
        heads = [row(head, i) * recips[i] for i in range(8)]
        for t in later:
            terms = [cols[t][i] * heads[i] for i in range(8)]
            while len(terms) > 1:
                terms = [terms[a] + terms[a + 1] for a in range(0, len(terms), 2)]
            strips[t] = strips[t] - terms[0]
    return strips, pivots


def factor_phase(g, store, middle):
    col_iota = lax.broadcasted_iota(jnp.int32, (8, 128), 1)
    row_iota = lax.broadcasted_iota(jnp.int32, (8, 128), 0)
    for b in range(4):
        odd = b % 2
        lo = 64 + 64 * b
        win = 128 * (b // 2)
        off = 64 * odd
        strips = []
        tile = g[lo:lo+64, win:win+128]
        for s in range(8):
            if odd:
                unit = jnp.where(col_iota == row_iota + 8 * s, 1.0, 0.0)
                strips.append(jnp.where(col_iota >= 64, tile[8*s:8*s+8], unit))
            else:
                unit = jnp.where(col_iota == row_iota + 8 * s + 64, 1.0, 0.0)
                strips.append(jnp.where(col_iota < 64, tile[8*s:8*s+8], unit))
        strips, pivots = eliminate(strips, off)
        keep = (col_iota < 64) if odd else (col_iota >= 64)
        wide = jnp.concatenate([jnp.where(keep, a * lax.rsqrt(p), 0.0) for a, p in zip(strips, pivots)], axis=0)
        turned = pltpu.roll(wide, 64, 1)
        low = wide if odd else turned
        high = turned if odd else wide
        if b == 2:
            middle()
        store(b, jnp.where(lax.broadcasted_iota(jnp.int32,(32,128),1) < 64, low[32:], high[:32]))
        base = lo if odd else lo - 64
        if b < 3:
            nwin = 128 * ((b + 1) // 2)
            u = dot32(wide, g[base:base+128, nwin:nwin+128], ((1,), (0,)))
            nxt = lo + 64
            noff = 64 * (1 - odd)
            if odd:
                g[nxt:nxt+64, nwin:nwin+128] = g[nxt:nxt+64, nwin:nwin+128] - dot32(u[:, 0:64], u, ((0,), (0,)))
            else:
                g[nxt:nxt+64, nwin:nwin+128] = g[nxt:nxt+64, nwin:nwin+128] - dot32(u, u, ((0,), (0,)))[64:128]
        lines = dot32(wide, g[base : base + 128, :], ((1,), (0,)))
        g[lo:lo+64, :] = lines
        if b < 3:
            first = 64 * (b + 1)
            change = dot32(lines[:, 0:256], lines, ((0,), (0,)))
            nxt = lo + 64
            nwin = 128 * ((b + 1) // 2)
            for lo_c, hi_c in ((0, nwin), (nwin + 128, 512)):
                if hi_c > lo_c:
                    g[nxt:nxt+64, lo_c:hi_c] = g[nxt:nxt+64, lo_c:hi_c] - change[first:first+64, lo_c:hi_c]
            if b < 2:
                g[nxt+64:320, :] = g[nxt+64:320, :] - change[first+64:256, :]


def set_identity(g):
    rows = lax.broadcasted_iota(jnp.int32, (256, 256), 0)
    cols = lax.broadcasted_iota(jnp.int32, (256, 256), 1)
    g[64:320, 256:512] = jnp.where(rows == cols, 1.0, 0.0)


def gather_kernel(
    kern, acol, brow, parts,
    lead, inv0, xs, gbuf, g, x_src, inv_src, work,
    p_send, p_recv, p_sib_send, p_sib_recv, m_send, m_recv, m_sib_send, m_sib_recv,
    lead_send, lead_recv, gs_send, gh_recv, gd_send, gd_recv, ga_send, ga_recv, gx_send, gx_recv,
    xr_send, xh_recv, xd_send, xd_recv, xx_send, xx_recv, loc,
):
    r = lax.axis_index("row")
    c = lax.axis_index("col")
    x, y = lax.div(r, 4), lax.rem(r, 4)
    z, k = lax.div(c, 2), lax.rem(c, 2)
    zero, one = jnp.int32(0), jnp.int32(1)
    sibling = c + 1 - 2 * k
    both, neither = jnp.logical_and, jnp.logical_not
    top = z == 0
    inner = neither(top)

    def hub_core(row):
        return jnp.where(both(top, row != 0), 0, 1)

    hub = k == hub_core(r)
    mate = neither(hub)
    root = both(r == 0, c == 0)
    aide = both(r == 0, c == 1)
    helper = both(r == 1, c == 1)
    head = both(c == 1, r != 0)
    runner = both(k == 0, inner)
    skip_to = lookup(z, SKIP)
    back_to = lookup(z, BACK)
    has_skip = member(z, list(SKIP))
    has_back = member(z, list(BACK))
    parent = lookup(z, {v: q for q, v in list(SKIP.items()) + list(BACK.items())})
    children = has_skip.astype(jnp.int32) + has_back.astype(jnp.int32)
    barrier = pltpu.get_barrier_semaphore()

    def remote(src, dst, send, recv, row, col):
        return pltpu.make_async_remote_copy(
            src_ref=src, dst_ref=dst, send_sem=send, recv_sem=recv, device_id=(row, col), device_id_type=MESH
        )

    def signal(row, col):
        pl.semaphore_signal(barrier, inc=1, device_id=(row, col), device_id_type=MESH)

    def loop(lo, hi, body):
        def step(d, carry):
            body(d)
            return carry

        lax.fori_loop(lo, hi, step, 0)

    def when(cond, body):
        @pl.when(cond)
        def _():
            body()

    def start(copy):
        copy.start()

    def sent(copy):
        copy.wait_send()

    def peer(d):
        return lax.rem(x + d[0], 4) * 4 + lax.rem(y + d[1], 4)

    own_block = kern.at[0, 0, 0, 0]
    own_panel = pltpu.make_async_copy(kern.at[0, :, 0, 0], acol.at[:, k], loc.at[0])
    own_rows = pltpu.make_async_copy(kern.at[0, 0, 0], brow.at[lax.rem(r, 2), :, k], loc.at[1])
    own_lead = pltpu.make_async_copy(own_block, gbuf.at[0], loc.at[2])
    aide_piece = pltpu.make_async_copy(own_block.at[pl.ds(0, 16)], lead.at[0, 0], loc.at[2])
    helper_piece = pltpu.make_async_copy(own_block.at[pl.ds(16, 16)], lead.at[1, 1], loc.at[2])
    when(root, lambda: own_lead.start())
    when(aide, lambda: aide_piece.start())
    when(helper, lambda: helper_piece.start())
    when(top, lambda: own_panel.start())
    when(r < 2, lambda: own_rows.start())

    signal(r, sibling)

    def greet_panel():
        signal(r, 2 * parent)
        when(parent == 0, lambda: signal(r, one))

    when(runner, greet_panel)

    def greet_plane():
        for d in PLANE:
            signal(peer(d), c)
        when(inner, lambda: signal(r, one))
        when(both(inner, r == 0), lambda: signal(r, zero))

    when(k == 1, greet_plane)

    def greet_mirror():
        for d in NEAR:
            signal(peer(d), hub_core(peer(d)))

    when(both(hub, top), greet_mirror)

    def greet_sources():
        signal(zero, zero)
        signal(zero, one)
        when(r != 1, lambda: signal(one, one))

    when(head, greet_sources)
    when(jnp.logical_or(root, aide), lambda: signal(one, one))

    def arrive():
        plane = jnp.where(k == 1, 15, 0) + jnp.where(both(hub, top), 4, 0)
        line = jnp.where(top, 2, jnp.where(k == 0, children, 0))
        down = jnp.where(c == 1, 15, 0)
        more = jnp.where(root, 30, 0) + jnp.where(aide, 15, 0) + jnp.where(helper, 16, 0)
        pl.semaphore_wait(barrier, 1 + plane + line + down + more)
        when(top, lambda: own_panel.wait())
        when(r < 2, lambda: own_rows.wait())
        when(aide, lambda: aide_piece.wait())
        when(helper, lambda: helper_piece.wait())

    def panel_chunk(n):
        col, i, half = lax.div(n, 8), lax.rem(lax.div(n, 2), 4), lax.rem(n, 2)
        return acol.at[i, col, pl.ds(pl.multiple_of(128 * half, 128), 128)]

    def panel_skip(n):
        return remote(panel_chunk(n), panel_chunk(n), p_send.at[n, 0], p_recv.at[n], r, 2 * skip_to)

    def panel_back(n):
        return remote(panel_chunk(n), panel_chunk(n), p_send.at[n, 1], p_recv.at[n], r, 2 * back_to)

    def panel_pair(n):
        return remote(panel_chunk(n), panel_chunk(n), p_sib_send.at[n], p_sib_recv.at[n], r, sibling)

    def panel_top(act):
        def step(m):
            act(panel_skip(8 * k + m))
            act(panel_back(8 * k + m))

        loop(0, 8, step)
        loop(0, 8, lambda m: act(panel_pair(8 * k + m)))

    def panel_line(t):
        n = lax.rem(t + jnp.where(r == 0, 8, 0), 16)
        panel_skip(n).wait_recv()
        when(has_skip, lambda: panel_skip(n).start())
        when(has_back, lambda: panel_back(n).start())
        panel_pair(n).start()

    def panel_line_sent(n):
        when(has_skip, lambda: panel_skip(n).wait_send())
        when(has_back, lambda: panel_back(n).wait_send())
        panel_pair(n).wait_send()

    def mirror_chunk(s, m):
        j, kc, half = lax.div(m, 4), lax.rem(lax.div(m, 2), 2), lax.rem(m, 2)
        return brow.at[s, j, kc, pl.ds(pl.multiple_of(128 * half, 128), 128)]

    def mirror_copy(s, m, way, row):
        chunk = mirror_chunk(s, m)
        return remote(chunk, chunk, m_send.at[8 * s + m, way], m_recv.at[8 * s + m], row, 2 * z + hub_core(row))

    def mirror_pair(s, m):
        n = 8 * s + m
        return remote(mirror_chunk(s, m), mirror_chunk(s, m), m_sib_send.at[n], m_sib_recv.at[n], r, sibling)

    def mirror_feed(j, half):
        m = 4 * j + 2 * k + half
        n = 8 * r + m
        return remote(mirror_chunk(r, m), mirror_chunk(r, m), m_sib_send.at[n], m_recv.at[n], r, sibling)

    def mirror_each(s, m, act):
        j, kc = lax.div(m, 4), lax.rem(lax.div(m, 2), 2)
        rel = lax.rem(y + 4 - s, 4)
        ring = jnp.logical_or(j == 1, x == 0)
        line = jnp.logical_or(j == 0, rel == 0)
        ring_up = both(ring, jnp.logical_or(rel == 0, both(s == 1, rel == 1)))
        ring_down = both(ring, jnp.logical_or(rel == 0, both(s == 0, rel == 3)))
        line_up = both(line, jnp.logical_or(x == 0, both(s == 0, x == 1)))
        line_down = both(line, jnp.logical_or(x == 0, both(s == 1, x == 3)))
        when(ring_up, lambda: act(mirror_copy(s, m, 0, peer((0, 1)))))
        when(ring_down, lambda: act(mirror_copy(s, m, 1, peer((0, 3)))))
        when(line_up, lambda: act(mirror_copy(s, m, 2, peer((1, 0)))))
        when(line_down, lambda: act(mirror_copy(s, m, 3, peer((3, 0)))))
        when(both(kc != k, r != s), lambda: act(mirror_pair(s, m)))

    def mirror_step(n):
        nearer = jnp.where(jnp.logical_or(y == 0, y == 3), 0, 1)
        s = lax.rem(lax.div(n, 8) + nearer, 2)
        m = lax.rem(n, 8)
        kc = lax.rem(lax.div(m, 2), 2)
        when(jnp.logical_or(r != s, kc != k), lambda: mirror_copy(s, m, 0, r).wait_recv())
        mirror_each(s, m, start)

    def mirror_sent(n):
        mirror_each(lax.div(n, 8), lax.rem(n, 8), sent)

    def feeds(act):
        for j in range(2):
            for half in range(2):
                act(mirror_feed(j, half))

    def mirror_take():
        for s in range(2):

            def take(s=s):
                for j in range(2):
                    for half in range(2):
                        mirror_pair(s, 4 * j + 2 * k + half).wait_recv()

            when(r != s, take)

    def lead_from(n, p):
        rows = own_block.at[pl.ds(16 * p, 16)]
        return remote(rows, lead.at[p, n], gs_send.at[p], gh_recv.at[n], jnp.int32(p), one)

    def lead_scatter(n, act):
        for p in range(16):
            if p != n:
                act(lead_from(n, p))

    def down(which, act):
        piece = (lead, inv0)[which].at[r]
        for d in LINE:
            act(remote(piece, piece, gd_send.at[which, d], gd_recv.at[which], r, jnp.int32(2 * d + 1)))

    def across(which, act):
        piece = (lead, inv0)[which].at[r]
        for n, d in enumerate(PLANE):
            act(remote(piece, piece, ga_send.at[which, n], ga_recv.at[which, r], peer(d), c))

    def pair(which):
        buf = (lead, inv0)[which]
        return remote(buf, buf, gx_send.at[which], gx_recv.at[which], r, sibling)

    def piece_taken(which):
        piece = (lead, inv0)[which].at[r]
        remote(piece, piece, gd_send.at[which, 0], gd_recv.at[which], r, sibling).wait_recv()

    def collect(which):
        buf = (lead, inv0)[which]

        def take(d):
            p = lax.rem(r + d, 16)
            remote(buf.at[p], buf.at[p], ga_send.at[which, 0], ga_recv.at[which, p], r, sibling).wait_recv()

        loop(1, 16, take)
        pair(which).start()

    def inverse_piece(p):
        return remote(inv_src.at[p], inv0.at[p], xr_send.at[0, p], xh_recv.at[0], jnp.int32(p), one)

    def inverse_rows(buf, n):
        lo, hi = GROUPS[n]
        return buf.at[pl.ds(lo, hi - lo)]

    def inverse_first(n, p):
        return remote(
            inverse_rows(x_src, n), inverse_rows(xs, n), xr_send.at[1 + n, p], xh_recv.at[1 + n], jnp.int32(p), one
        )

    def from_root(act, copy):
        for d in PLANE:
            act(copy(4 * d[0] + d[1]))
        act(copy(0))

    def inverse_down(n, act, src):
        for d in LINE:
            act(remote(
                inverse_rows(src, n), inverse_rows(xs, n), xd_send.at[n, d], xd_recv.at[n], r, jnp.int32(2 * d + 1)
            ))

    def first_all(n, act):
        inverse_down(n, act, x_src)
        from_root(act, lambda p: inverse_first(n, p))

    def inverse_taken(n):
        rows = inverse_rows(xs, n)
        remote(rows, rows, xd_send.at[n, 0], xd_recv.at[n], r, sibling).wait_recv()

    def inverse_pair(n):
        rows = inverse_rows(xs, n)
        return remote(rows, rows, xx_send.at[n], xx_recv.at[n], r, sibling)

    def lead_copy(n):
        return remote(own_block, gbuf.at[n + 1], lead_send.at[n], lead_recv.at[n], zero, zero)

    def root_main():
        own_lead.wait()
        g[0:64, :] = jnp.zeros((64, 512), jnp.float32)
        g[320:384, :] = jnp.zeros((64, 512), jnp.float32)
        g[64:320, 0:256] = gbuf[0].astype(jnp.float32)
        set_identity(g)

        def bulk():
            arrive()
            feeds(start)
            panel_top(start)

        def second_half():
            for p in range(16):
                inv_src[p] = g[64 + 16 * p : 80 + 16 * p, 256:512]
            from_root(start, inverse_piece)
            lead_copy(0).wait_recv()
            lead_copy(1).wait_recv()
            side = dot32(g[64:320, 256:512], gbuf[1].astype(jnp.float32), ((1,), (0,)))
            g[64:320, 0:256] = gbuf[2].astype(jnp.float32) - dot32(side, side, ((0,), (0,)))
            set_identity(g)

        def phase(it):
            def store(n, packed):
                x_src[n] = packed
                for which, (lo, hi) in enumerate(GROUPS):
                    if hi == n + 1:
                        when(it == 1, lambda which=which: first_all(which, start))

            factor_phase(g, store, lambda: when(it == 0, bulk))
            when(it == 0, second_half)

        loop(0, 2, phase)

    when(root, root_main)
    when(neither(root), arrive)

    def top_sends():
        when(aide, lambda: lead_copy(0).start())
        when(helper, lambda: lead_copy(1).start())
        panel_top(start)
        when(aide, lambda: lead_scatter(0, start))
        when(helper, lambda: lead_scatter(1, start))

    when(both(top, neither(root)), top_sends)
    when(both(both(mate, r < 2), neither(root)), lambda: feeds(start))

    def top_spread(which):
        down(which, start)
        across(which, start)

    def aide_main():
        loop(0, 8, mirror_step)
        lead_from(1, 0).wait_recv()
        top_spread(0)
        inverse_piece(0).wait_recv()
        top_spread(1)
        loop(8, 16, mirror_step)

    when(aide, aide_main)
    when(both(hub, neither(aide)), lambda: loop(0, 16, mirror_step))

    def head_main():
        lead_from(0, 1).wait_recv()
        when(neither(helper), lambda: lead_from(1, 2).wait_recv())
        top_spread(0)
        inverse_piece(1).wait_recv()
        top_spread(1)
        for n in range(2):
            inverse_first(n, 1).wait_recv()
            inverse_down(n, start, xs)

    when(head, head_main)

    def line_spread():
        for which in range(2):
            piece_taken(which)
            across(which, start)

    when(both(k == 1, inner), line_spread)

    def core1_collect():
        collect(0)
        collect(1)

    when(k == 1, core1_collect)
    when(runner, lambda: loop(0, 16, panel_line))

    def core0_take():
        pair(0).wait_recv()
        pair(1).wait_recv()

    when(k == 0, core0_take)
    take = {lo: n for n, (lo, hi) in enumerate(GROUPS)}

    def inverse_take(n):
        def first():
            when(aide, lambda: inverse_first(n, 0).wait_recv())
            when(inner, lambda: inverse_taken(n))
            inverse_pair(n).start()

        when(k == 1, first)
        when(k == 0, lambda: inverse_pair(n).wait_recv())

    def put(lo, hi, left, values):
        high = values.astype(jnp.bfloat16)
        parts[0, lo:hi, left : left + 256] = high
        parts[1, lo:hi, left : left + 256] = (values - high.astype(jnp.float32)).astype(jnp.bfloat16)

    def block(n):
        return jnp.concatenate([lead[p, n] for p in range(16)], axis=0).astype(jnp.float32)

    first_inverse = jnp.concatenate([inv0[p] for p in range(16)], axis=0)
    put(0, 256, 0, first_inverse)
    put(0, 256, 256, jnp.zeros((256, 256), jnp.float32))
    side = dot32(first_inverse, block(0), ((1,), (0,)))
    work[:, 0:256] = block(1) - dot32(side, side, ((0,), (0,)))
    work[:, 256:512] = -dot32(side, first_inverse, ((0,), (0,)))
    rows = lax.broadcasted_iota(jnp.int32, (256, 256), 0)
    cols = lax.broadcasted_iota(jnp.int32, (256, 256), 1)
    work[:, 512:768] = jnp.where(rows == cols, 1.0, 0.0)
    for n in range(4):
        if n in take:
            inverse_take(take[n])
        packed = xs[n]
        inverse = jnp.concatenate([packed[:, 64:128], packed[:, 0:64]], axis=0)
        lo, hi = 64 * n, 64 * n + 64
        lines = dot32(inverse, work[lo:hi, :], ((1,), (0,)))
        put(256 + lo, 256 + hi, 0, lines[:, 256:512])
        put(256 + lo, 256 + hi, 256, lines[:, 512:768])
        if n < 3:
            work[hi:256, :] = work[hi:256, :] - dot32(lines[:, hi:256], lines, ((0,), (0,)))

    when(mate, mirror_take)
    when(both(k == 1, inner), lambda: loop(0, 16, lambda n: panel_pair(n).wait_recv()))
    when(top, lambda: loop(0, 8, lambda m: panel_pair(8 * (1 - k) + m).wait_recv()))

    when(runner, lambda: loop(0, 16, panel_line_sent))
    when(top, lambda: panel_top(sent))
    when(both(mate, r < 2), lambda: feeds(sent))

    when(hub, lambda: loop(0, 16, mirror_sent))

    def core1_drain():
        for which in range(2):
            across(which, sent)
            pair(which).wait_send()
        for n in range(2):
            inverse_pair(n).wait_send()

    when(k == 1, core1_drain)

    def line_drain():
        for which in range(2):
            down(which, sent)

    when(c == 1, line_drain)

    def head_drain():
        for n in range(2):
            inverse_down(n, sent, xs)

    when(head, head_drain)

    def aide_drain():
        lead_copy(0).wait_send()
        lead_scatter(0, sent)

    when(aide, aide_drain)

    def helper_drain():
        lead_copy(1).wait_send()
        lead_scatter(1, sent)

    when(helper, helper_drain)

    def root_drain():
        from_root(sent, inverse_piece)
        for n in range(2):
            first_all(n, sent)

    when(root, root_drain)


def gather(kernel):
    bf16, f32 = jnp.bfloat16, jnp.float32
    dma = pltpu.SemaphoreType.DMA
    return pl.pallas_call(
        gather_kernel,
        out_shape=(
            jax.ShapeDtypeStruct((4, 2, 256, 256), bf16),
            jax.ShapeDtypeStruct((2, 2, 2, 256, 256), bf16),
            jax.ShapeDtypeStruct((2, 512, 512), bf16),
        ),
        in_specs=[pl.BlockSpec(memory_space=pltpu.HBM)],
        out_specs=(
            pl.BlockSpec(memory_space=pl.ANY),
            pl.BlockSpec(memory_space=pl.ANY),
            pl.BlockSpec(memory_space=pltpu.VMEM),
        ),
        scratch_shapes=[
            pltpu.VMEM((16, 2, 16, 256), bf16),
            pltpu.VMEM((16, 16, 256), f32),
            pltpu.VMEM((4, 32, 128), f32),
            pltpu.VMEM((3, 256, 256), bf16),
            pltpu.VMEM((384, 512), f32),
            pltpu.VMEM((4, 32, 128), f32),
            pltpu.VMEM((16, 16, 256), f32),
            pltpu.VMEM((256, 768), f32),
            dma((16, 2)), dma((16,)), dma((16,)), dma((16,)),
            dma((16, 4)), dma((16,)), dma((16,)), dma((16,)),
            dma((2,)), dma((2,)),
            dma((16,)), dma((2,)), dma((2, 16)), dma((2,)), dma((2, 16)), dma((2, 16)), dma((2,)), dma((2,)),
            dma((3, 16)), dma((3,)), dma((2, 16)), dma((2,)), dma((2,)), dma((2,)), dma((3,)),
        ],
        compiler_params=pltpu.CompilerParams(
            collective_id=0, has_side_effects=True, vmem_limit_bytes=24 * 1024 * 1024
        ),
        name="gather_and_factor",
    )(kernel)


def update_kernel(kern, acol, brow, parts, panels, schur, old, pan, new, sems):
    r = lax.axis_index("row")
    c = lax.axis_index("col")
    k = lax.rem(c, 2)
    load = pltpu.make_async_copy(kern.at[0, :, 0], old, sems.at[0])
    load.start()
    mirror = []
    for j in range(2):
        halves = []
        for n in range(2):
            total = None
            for s in range(n + 1):
                for t in range(2):
                    term = jnp.dot(
                        parts[t, 256 * n : 256 * n + 256, 256 * s : 256 * s + 256],
                        brow[s, j, k],
                        preferred_element_type=jnp.float32,
                    )
                    total = term if total is None else total + term
            halves.append(total.astype(jnp.bfloat16))
        mirror.append(jnp.concatenate(halves, axis=0))
    tri = lax.broadcasted_iota(jnp.int32, (256, 256), 0) >= lax.broadcasted_iota(jnp.int32, (256, 256), 1)
    stores = []
    load.wait()
    for i in range(4):
        solved = []
        for n in range(2):
            total = None
            for s in range(n + 1):
                for t in range(2):
                    term = lax.dot_general(
                        acol[i, s],
                        parts[t, 256 * n : 256 * n + 256, 256 * s : 256 * s + 256],
                        (((1,), (1,)), ((), ())),
                        preferred_element_type=jnp.float32,
                    )
                    total = term if total is None else total + term
            solved.append(total)
        left = jnp.concatenate([a.astype(jnp.bfloat16) for a in solved], axis=1)
        if i == 0:
            solved[0] = jnp.where(jnp.logical_or(r != 0, tri), solved[0], 0.0)
            solved[1] = jnp.where(jnp.logical_or(r > 1, jnp.logical_and(r == 1, tri)), solved[1], 0.0)
        for n in range(2):
            pan[i, n] = solved[n]
        stores.append(pltpu.make_async_copy(pan.at[i], panels.at[0, i], sems.at[1 + 2 * i]))
        stores[-1].start()
        for j in range(2):
            change = jnp.dot(left, mirror[j], preferred_element_type=jnp.float32)
            out = (old[i, j].astype(jnp.float32) - change).astype(jnp.bfloat16)
            if i == 0:
                out = jnp.where(r >= 2, out, jnp.zeros_like(out))
            if j == 0:
                out = jnp.where(c >= 2, out, jnp.zeros_like(out))
            new[i, j] = out
        stores.append(pltpu.make_async_copy(new.at[i], schur.at[0, i, 0], sems.at[2 + 2 * i]))
        stores[-1].start()
    for store in stores:
        store.wait()


def update(kernel, *gathered):
    hbm = pl.BlockSpec(memory_space=pltpu.HBM)
    return pl.pallas_call(
        update_kernel,
        out_shape=(
            jax.ShapeDtypeStruct((1, 4, 2, 256, 256), jnp.float32),
            jax.ShapeDtypeStruct((1, 4, 1, 2, 256, 256), jnp.bfloat16),
        ),
        in_specs=[hbm] + [pl.BlockSpec(memory_space=pltpu.VMEM)] * 3,
        out_specs=(hbm, hbm),
        scratch_shapes=[
            pltpu.VMEM((4, 2, 256, 256), jnp.bfloat16),
            pltpu.VMEM((4, 2, 256, 256), jnp.float32),
            pltpu.VMEM((4, 2, 256, 256), jnp.bfloat16),
            pltpu.SemaphoreType.DMA((9,)),
        ],
        compiler_params=pltpu.CompilerParams(vmem_limit_bytes=32 * 1024 * 1024),
        name="solve_and_update",
    )(kernel, *gathered)


def per_device(kernel):
    kernel = pltpu.with_memory_space_constraint(kernel, pltpu.HBM)
    return update(kernel, *gather(kernel))


def solution(mesh):
    in_specs = (P("row", None, "col", None, None, None),)
    out_specs = (P("row", None, None, None, None), P("row", None, "col", None, None, None))
    return jax.shard_map(per_device, mesh=mesh, in_specs=in_specs, out_specs=out_specs, check_vma=False)
```

```python
import functools

import jax
import jax.numpy as jnp
from jax import lax
from jax.experimental import pallas as pl
from jax.experimental.pallas import tpu as pltpu
from jax.sharding import PartitionSpec as P

MESH = pl.DeviceIdType.MESH
HI = lax.Precision.HIGHEST
PLANE = sorted(((a, b) for a in range(4) for b in range(4) if a or b), key=lambda d: -min(d[0], 4 - d[0]) - min(d[1], 4 - d[1]))
NEAR = ((0, 1), (0, 3), (1, 0), (3, 0))
LINE = sorted(range(1, 16), key=lambda d: -min(d, 16 - d))
SKIP = {0: 3, 3: 6, 6: 8, 13: 10, 10: 9}
BACK = {0: 13, 3: 2, 2: 1, 6: 5, 5: 4, 8: 7, 13: 14, 14: 15, 10: 11, 11: 12}


def lookup(key, pairs):
    value = jnp.int32(0)
    for k, v in pairs.items():
        value = jnp.where(key == k, jnp.int32(v), value)
    return value


def member(key, keys):
    hit = key == keys[0]
    for k in keys[1:]:
        hit = jnp.logical_or(hit, key == k)
    return hit


def dot32(a, b, dims):
    return lax.dot_general(a, b, (dims, ((), ())), precision=HI, preferred_element_type=jnp.float32)


def row(v, i):
    return jnp.broadcast_to(v[i : i + 1, :], (8, 128))

def lane(v, i):
    return jnp.broadcast_to(v[:, i : i + 1], (8, 128))


def eliminate(strips, off):
    row_iota = lax.broadcasted_iota(jnp.int32, (8, 128), 0)
    strips = list(strips)
    diag = [lane(strips[0], off + i) for i in range(8)]
    pivots = []
    for s in range(8):
        later = range(s + 1, 8)
        cols = {t: [lane(strips[t], off + 8 * s + i) for i in range(8)] for t in later}
        if s < 7:
            raw = [lane(strips[s + 1], off + 8 * (s + 1) + i) for i in range(8)]
        head = strips[s]
        pivot = jnp.zeros((8, 128), jnp.float32)
        recips = []
        for i in range(8):
            own = diag[i]
            recip = 1.0 / row(own, i)
            recips.append(recip)
            pivot = jnp.where(row_iota == i, own, pivot)
            for j in range(i + 1, 8):
                line = row(own, j)
                diag[j] = diag[j] - (own * line) * recip
                factor = line * recip
                for t in later:
                    cols[t][j] = cols[t][j] - cols[t][i] * factor
            head = head - jnp.where(row_iota > i, own * recip, 0.0) * row(head, i)
        strips[s] = head
        pivots.append(pivot)
        if s < 7:
            near = cols[s + 1]
            scaled = [near[i] * recips[i] for i in range(8)]
            diag = []
            for j in range(8):
                terms = [scaled[i] * row(near[i], j) for i in range(8)]
                while len(terms) > 1:
                    terms = [terms[a] + terms[a + 1] for a in range(0, len(terms), 2)]
                diag.append(raw[j] - terms[0])
        heads = [row(head, i) * recips[i] for i in range(8)]
        for t in later:
            terms = [cols[t][i] * heads[i] for i in range(8)]
            while len(terms) > 1:
                terms = [terms[a] + terms[a + 1] for a in range(0, len(terms), 2)]
            strips[t] = strips[t] - terms[0]
    return strips, pivots


def factor_phase(g, store, middle):
    col_iota = lax.broadcasted_iota(jnp.int32, (8, 128), 1)
    row_iota = lax.broadcasted_iota(jnp.int32, (8, 128), 0)
    for b in range(4):
        odd = b % 2
        lo = 64 + 64 * b
        win = 128 * (b // 2)
        off = 64 * odd
        strips = []
        tile = g[lo:lo+64, win:win+128]
        for s in range(8):
            if odd:
                unit = jnp.where(col_iota == row_iota + 8 * s, 1.0, 0.0)
                strips.append(jnp.where(col_iota >= 64, tile[8*s:8*s+8], unit))
            else:
                unit = jnp.where(col_iota == row_iota + 8 * s + 64, 1.0, 0.0)
                strips.append(jnp.where(col_iota < 64, tile[8*s:8*s+8], unit))
        strips, pivots = eliminate(strips, off)
        keep = (col_iota < 64) if odd else (col_iota >= 64)
        wide = jnp.concatenate([jnp.where(keep, a * lax.rsqrt(p), 0.0) for a, p in zip(strips, pivots)], axis=0)
        turned = pltpu.roll(wide, 64, 1)
        low = wide if odd else turned
        high = turned if odd else wide
        if b == 1:
            middle()
        store(b, jnp.where(lax.broadcasted_iota(jnp.int32,(32,128),1) < 64, low[32:], high[:32]))
        base = lo if odd else lo - 64
        if b < 3:
            nwin = 128 * ((b + 1) // 2)
            u = dot32(wide, g[base:base+128, nwin:nwin+128], ((1,), (0,)))
            nxt = lo + 64
            noff = 64 * (1 - odd)
            if odd:
                g[nxt:nxt+64, nwin:nwin+128] = g[nxt:nxt+64, nwin:nwin+128] - dot32(u[:, 0:64], u, ((0,), (0,)))
            else:
                g[nxt:nxt+64, nwin:nwin+128] = g[nxt:nxt+64, nwin:nwin+128] - dot32(u, u, ((0,), (0,)))[64:128]
        lines = dot32(wide, g[base : base + 128, :], ((1,), (0,)))
        g[lo:lo+64, :] = lines
        if b < 3:
            first = 64 * (b + 1)
            change = dot32(lines[:, 0:256], lines, ((0,), (0,)))
            nxt = lo + 64
            nwin = 128 * ((b + 1) // 2)
            for lo_c, hi_c in ((0, nwin), (nwin + 128, 512)):
                if hi_c > lo_c:
                    g[nxt:nxt+64, lo_c:hi_c] = g[nxt:nxt+64, lo_c:hi_c] - change[first:first+64, lo_c:hi_c]
            if b < 2:
                g[nxt+64:320, :] = g[nxt+64:320, :] - change[first+64:256, :]


def set_identity(g):
    rows = lax.broadcasted_iota(jnp.int32, (256, 256), 0)
    cols = lax.broadcasted_iota(jnp.int32, (256, 256), 1)
    g[64:320, 256:512] = jnp.where(rows == cols, 1.0, 0.0)


def gather_kernel(
    kern, acol, brow, parts,
    lead, inv0, inv1, xs, gbuf, g, x_src, inv_src, inv1_src, work,
    p_send, p_recv, p_sib_send, p_sib_recv, m_send, m_recv, m_sib_send, m_sib_recv,
    lead_send, lead_recv, gs_send, gh_recv, gd_send, gd_recv, ga_send, ga_recv, parts_send, parts_recv,
    xr_send, xh_recv, xd_send, xd_recv, loc,
):
    r = lax.axis_index("row")
    c = lax.axis_index("col")
    x, y = lax.div(r, 4), lax.rem(r, 4)
    z, k = lax.div(c, 2), lax.rem(c, 2)
    zero, one = jnp.int32(0), jnp.int32(1)
    sibling = c + 1 - 2 * k
    both, neither = jnp.logical_and, jnp.logical_not
    top = z == 0
    inner = neither(top)

    def hub_core(row):
        return jnp.where(both(top, row != 0), 0, 1)

    hub = k == hub_core(r)
    mate = neither(hub)
    root = both(r == 0, c == 0)
    aide = both(r == 0, c == 1)
    helper = both(r == 1, c == 1)
    head = both(c == 1, r != 0)
    runner = both(k == 0, inner)
    skip_to = lookup(z, SKIP)
    back_to = lookup(z, BACK)
    has_skip = member(z, list(SKIP))
    has_back = member(z, list(BACK))
    parent = lookup(z, {v: q for q, v in list(SKIP.items()) + list(BACK.items())})
    children = has_skip.astype(jnp.int32) + has_back.astype(jnp.int32)
    barrier = pltpu.get_barrier_semaphore()

    def remote(src, dst, send, recv, row, col):
        return pltpu.make_async_remote_copy(
            src_ref=src, dst_ref=dst, send_sem=send, recv_sem=recv, device_id=(row, col), device_id_type=MESH
        )

    def signal(row, col):
        pl.semaphore_signal(barrier, inc=1, device_id=(row, col), device_id_type=MESH)

    def loop(lo, hi, body):
        def step(d, carry):
            body(d)
            return carry

        lax.fori_loop(lo, hi, step, 0)

    def when(cond, body):
        @pl.when(cond)
        def _():
            body()

    def start(copy):
        copy.start()

    def sent(copy):
        copy.wait_send()

    def peer(d):
        return lax.rem(x + d[0], 4) * 4 + lax.rem(y + d[1], 4)

    own_block = kern.at[0, 0, 0, 0]
    own_panel = pltpu.make_async_copy(kern.at[0, :, 0, 0], acol.at[:, k], loc.at[0])
    own_rows = pltpu.make_async_copy(kern.at[0, 0, 0], brow.at[lax.rem(r, 2), :, k], loc.at[1])
    own_lead = pltpu.make_async_copy(own_block, gbuf.at[0], loc.at[2])
    aide_piece = pltpu.make_async_copy(own_block.at[pl.ds(0, 16)], lead.at[0, 0], loc.at[2])
    helper_piece = pltpu.make_async_copy(own_block.at[pl.ds(16, 16)], lead.at[1, 1], loc.at[2])
    when(root, lambda: own_lead.start())
    when(aide, lambda: aide_piece.start())
    when(helper, lambda: helper_piece.start())
    when(top, lambda: own_panel.start())
    when(r < 2, lambda: own_rows.start())

    signal(r, sibling)

    def greet_panel():
        signal(r, 2 * parent)
        when(parent == 0, lambda: signal(r, one))

    when(runner, greet_panel)

    def greet_plane():
        for d in PLANE:
            signal(peer(d), c)
        when(inner, lambda: signal(r, one))

    when(k == 1, greet_plane)

    def greet_mirror():
        for d in NEAR:
            signal(peer(d), hub_core(peer(d)))

    when(both(hub, top), greet_mirror)

    def greet_sources():
        signal(zero, zero)
        signal(zero, one)
        when(r != 1, lambda: signal(one, one))

    when(head, greet_sources)
    when(jnp.logical_or(root, aide), lambda: signal(one, one))

    def arrive():
        plane = jnp.where(k == 1, 15, 0) + jnp.where(both(hub, top), 4, 0)
        line = jnp.where(top, 2, jnp.where(k == 0, children, 0))
        down = jnp.where(c == 1, 15, 0)
        more = jnp.where(root, 15, 0) + jnp.where(aide, 15, 0) + jnp.where(helper, 16, 0)
        pl.semaphore_wait(barrier, 1 + plane + line + down + more)
        when(top, lambda: own_panel.wait())
        when(r < 2, lambda: own_rows.wait())
        when(aide, lambda: aide_piece.wait())
        when(helper, lambda: helper_piece.wait())

    def panel_chunk(n):
        col, i, quarter = lax.div(n, 16), lax.rem(lax.div(n, 4), 4), lax.rem(n, 4)
        return acol.at[i, col, pl.ds(pl.multiple_of(64 * quarter, 64), 64)]

    def panel_skip(n):
        return remote(panel_chunk(n), panel_chunk(n), p_send.at[n, 0], p_recv.at[n], r, 2 * skip_to)

    def panel_back(n):
        return remote(panel_chunk(n), panel_chunk(n), p_send.at[n, 1], p_recv.at[n], r, 2 * back_to)

    def panel_pair(n):
        return remote(panel_chunk(n), panel_chunk(n), p_sib_send.at[n], p_sib_recv.at[n], r, sibling)

    def panel_top(act):
        def step(m):
            act(panel_skip(16 * k + m))
            act(panel_back(16 * k + m))

        loop(0, 16, step)
        loop(0, 16, lambda m: act(panel_pair(16 * k + m)))

    def panel_line(t):
        n = t
        panel_skip(n).wait_recv()
        when(has_skip, lambda: panel_skip(n).start())
        when(has_back, lambda: panel_back(n).start())
        panel_pair(n).start()

    def panel_line_sent(n):
        when(has_skip, lambda: panel_skip(n).wait_send())
        when(has_back, lambda: panel_back(n).wait_send())
        panel_pair(n).wait_send()

    def mirror_chunk(s, m):
        j, kc, half = lax.div(m, 4), lax.rem(lax.div(m, 2), 2), lax.rem(m, 2)
        return brow.at[s, j, kc, pl.ds(pl.multiple_of(128 * half, 128), 128)]

    def mirror_copy(s, m, way, row):
        chunk = mirror_chunk(s, m)
        return remote(chunk, chunk, m_send.at[8 * s + m, way], m_recv.at[8 * s + m], row, 2 * z + hub_core(row))

    def mirror_pair(s, m):
        n = 8 * s + m
        return remote(mirror_chunk(s, m), mirror_chunk(s, m), m_sib_send.at[n], m_sib_recv.at[n], r, sibling)

    def mirror_feed(j, half):
        m = 4 * j + 2 * k + half
        n = 8 * r + m
        return remote(mirror_chunk(r, m), mirror_chunk(r, m), m_sib_send.at[n], m_recv.at[n], r, sibling)

    def mirror_each(s, m, act):
        j, kc = lax.div(m, 4), lax.rem(lax.div(m, 2), 2)
        rel = lax.rem(y + 4 - s, 4)
        ring = jnp.logical_or(j == 1, x == 0)
        line = jnp.logical_or(j == 0, rel == 0)
        ring_up = both(ring, jnp.logical_or(rel == 0, both(s == 1, rel == 1)))
        ring_down = both(ring, jnp.logical_or(rel == 0, both(s == 0, rel == 3)))
        line_up = both(line, jnp.logical_or(x == 0, both(s == 0, x == 1)))
        line_down = both(line, jnp.logical_or(x == 0, both(s == 1, x == 3)))
        when(ring_up, lambda: act(mirror_copy(s, m, 0, peer((0, 1)))))
        when(ring_down, lambda: act(mirror_copy(s, m, 1, peer((0, 3)))))
        when(line_up, lambda: act(mirror_copy(s, m, 2, peer((1, 0)))))
        when(line_down, lambda: act(mirror_copy(s, m, 3, peer((3, 0)))))
        when(both(kc != k, r != s), lambda: act(mirror_pair(s, m)))

    def mirror_step(n):
        nearer = jnp.where(jnp.logical_or(y == 0, y == 3), 0, 1)
        s = lax.rem(lax.div(n, 8) + nearer, 2)
        m = lax.rem(n, 8)
        kc = lax.rem(lax.div(m, 2), 2)
        when(jnp.logical_or(r != s, kc != k), lambda: mirror_copy(s, m, 0, r).wait_recv())
        mirror_each(s, m, start)

    def mirror_sent(n):
        mirror_each(lax.div(n, 8), lax.rem(n, 8), sent)

    def feeds(act):
        for j in range(2):
            for half in range(2):
                act(mirror_feed(j, half))

    def mirror_take():
        for s in range(2):

            def take(s=s):
                for j in range(2):
                    for half in range(2):
                        mirror_pair(s, 4 * j + 2 * k + half).wait_recv()

            when(r != s, take)

    def lead_from(n, p):
        rows = own_block.at[pl.ds(16 * p, 16)]
        return remote(rows, lead.at[p, n], gs_send.at[p], gh_recv.at[n], jnp.int32(p), one)

    def lead_scatter(n, act):
        for p in range(16):
            if p != n:
                act(lead_from(n, p))

    def view(which, p):
        if which < 2:
            return (lead, inv0)[which].at[p]
        return inv1.at[lax.div(p, 2)]

    def takes_part(which, row):
        return row >= 0 if which < 2 else lax.rem(row, 2) == 0

    def down(which, act):
        def go():
            for d in LINE:
                act(remote(
                    view(which, r), view(which, r), gd_send.at[which, d], gd_recv.at[which], r, jnp.int32(2 * d + 1)
                ))

        when(takes_part(which, r), go)

    def across(which, act):
        def go():
            for n, d in enumerate(PLANE):
                act(remote(view(which, r), view(which, r), ga_send.at[which, n], ga_recv.at[which, r], peer(d), c))

        when(takes_part(which, r), go)

    def piece_taken(which):
        copy = remote(view(which, r), view(which, r), gd_send.at[which, 0], gd_recv.at[which], r, sibling)
        when(takes_part(which, r), lambda: copy.wait_recv())

    def collect(which):
        def take(d):
            p = lax.rem(r + d, 16)
            copy = remote(view(which, p), view(which, p), ga_send.at[which, 0], ga_recv.at[which, p], r, sibling)
            when(takes_part(which, p), lambda: copy.wait_recv())

        loop(1, 16, take)

    def inverse_piece(p):
        return remote(inv_src.at[p], inv0.at[p], xr_send.at[0, p], xh_recv.at[0], jnp.int32(p), one)

    def next_piece(p):
        return remote(inv1_src.at[p // 2], inv1.at[p // 2], xr_send.at[1, p], xh_recv.at[1], jnp.int32(p), one)

    def inverse_first(n, p):
        return remote(x_src.at[n], xs.at[n], xr_send.at[2 + n, p], xh_recv.at[2 + n], jnp.int32(p), one)

    def from_root(act, copy, step=1):
        for d in PLANE:
            p = 4 * d[0] + d[1]
            if p % step == 0:
                act(copy(p))
        act(copy(0))

    def inverse_down(n, act):
        for d in LINE:
            act(remote(xs.at[n], xs.at[n], xd_send.at[n, d], xd_recv.at[n], r, jnp.int32(2 * d + 1)))

    def inverse_taken(n):
        remote(xs.at[n], xs.at[n], xd_send.at[n, 0], xd_recv.at[n], r, sibling).wait_recv()

    def parts_pair(n):
        block = parts.at[0] if n == 0 else parts.at[pl.ds(1, 2)]
        return remote(block, block, parts_send.at[n], parts_recv.at[n], r, sibling)

    def lead_copy(n):
        return remote(own_block, gbuf.at[n + 1], lead_send.at[n], lead_recv.at[n], zero, zero)

    def root_main():
        own_lead.wait()
        g[0:64, :] = jnp.zeros((64, 512), jnp.float32)
        g[320:384, :] = jnp.zeros((64, 512), jnp.float32)
        g[64:320, 0:256] = gbuf[0].astype(jnp.float32)
        set_identity(g)

        def bulk():
            arrive()
            feeds(start)
            panel_top(start)

        def second_half():
            for p in range(16):
                inv_src[p] = g[64 + 16 * p : 80 + 16 * p, 256:512]
            from_root(start, inverse_piece)
            lead_copy(0).wait_recv()
            lead_copy(1).wait_recv()
            side = dot32(g[64:320, 256:512], gbuf[1].astype(jnp.float32), ((1,), (0,)))
            g[64:320, 0:256] = gbuf[2].astype(jnp.float32) - dot32(side, side, ((0,), (0,)))
            set_identity(g)

        def phase(it):
            def store(n, packed):
                if n < 2:
                    for part in range(4):
                        inv1_src[4 * n + part] = packed[8 * part : 8 * part + 8]
                    if n == 1:
                        when(it == 1, lambda: from_root(start, next_piece, 2))
                else:
                    x_src[n - 2] = packed
                    when(it == 1, lambda: from_root(start, lambda p: inverse_first(n - 2, p)))

            factor_phase(g, store, lambda: when(it == 0, bulk))
            when(it == 0, second_half)

        loop(0, 2, phase)

    when(root, root_main)
    when(neither(root), arrive)

    def top_sends():
        when(aide, lambda: lead_copy(0).start())
        when(helper, lambda: lead_copy(1).start())
        panel_top(start)
        when(aide, lambda: lead_scatter(0, start))
        when(helper, lambda: lead_scatter(1, start))

    when(both(top, neither(root)), top_sends)
    when(both(both(mate, r < 2), neither(root)), lambda: feeds(start))

    def top_spread(which):
        down(which, start)
        across(which, start)

    def head_inverses(p):
        when(takes_part(2, r), lambda: next_piece(p).wait_recv())
        top_spread(2)
        for n in range(2):
            inverse_first(n, p).wait_recv()
            inverse_down(n, start)

    def aide_main():
        loop(0, 8, mirror_step)
        lead_from(1, 0).wait_recv()
        top_spread(0)
        inverse_piece(0).wait_recv()
        top_spread(1)
        loop(8, 16, mirror_step)
        head_inverses(0)

    when(aide, aide_main)
    when(both(hub, neither(aide)), lambda: loop(0, 16, mirror_step))

    def head_main():
        lead_from(0, 1).wait_recv()
        when(neither(helper), lambda: lead_from(1, 2).wait_recv())
        top_spread(0)
        inverse_piece(1).wait_recv()
        top_spread(1)
        head_inverses(2)

    when(head, head_main)

    def line_spread():
        for which in range(3):
            piece_taken(which)
            across(which, start)

    when(both(k == 1, inner), line_spread)
    when(runner, lambda: loop(0, 32, panel_line))

    def put(block, lo, hi, values):
        high = values.astype(jnp.bfloat16)
        parts[block, 0, lo:hi] = high
        parts[block, 1, lo:hi] = (values - high.astype(jnp.float32)).astype(jnp.bfloat16)

    def assemble():
        def block(n):
            return jnp.concatenate([lead[p, n] for p in range(16)], axis=0).astype(jnp.float32)

        collect(0)
        collect(1)
        first_inverse = jnp.concatenate([inv0[p] for p in range(16)], axis=0)
        put(0, 0, 256, first_inverse)
        parts_pair(0).start()
        side = dot32(first_inverse, block(0), ((1,), (0,)))
        work[:, 0:256] = block(1) - dot32(side, side, ((0,), (0,)))
        work[:, 256:512] = -dot32(side, first_inverse, ((0,), (0,)))
        rows = lax.broadcasted_iota(jnp.int32, (256, 256), 0)
        cols = lax.broadcasted_iota(jnp.int32, (256, 256), 1)
        work[:, 512:768] = jnp.where(rows == cols, 1.0, 0.0)
        collect(2)
        for n in range(4):
            if n < 2:
                packed = jnp.concatenate([inv1[4 * n + p] for p in range(4)], axis=0)
            else:
                when(inner, lambda: inverse_taken(n - 2))
                packed = xs[n - 2]
            inverse = jnp.concatenate([packed[:, 64:128], packed[:, 0:64]], axis=0)
            lo, hi = 64 * n, 64 * n + 64
            lines = dot32(inverse, work[lo:hi, :], ((1,), (0,)))
            put(1, lo, hi, lines[:, 256:512])
            put(2, lo, hi, lines[:, 512:768])
            if n < 3:
                work[hi:256, :] = work[hi:256, :] - dot32(lines[:, hi:256], lines, ((0,), (0,)))
        parts_pair(1).start()

    when(k == 1, assemble)

    def parts_take():
        parts_pair(0).wait_recv()
        parts_pair(1).wait_recv()

    when(k == 0, parts_take)
    when(mate, mirror_take)
    when(both(k == 1, inner), lambda: loop(0, 32, lambda n: panel_pair(n).wait_recv()))
    when(top, lambda: loop(0, 16, lambda m: panel_pair(16 * (1 - k) + m).wait_recv()))

    when(runner, lambda: loop(0, 32, panel_line_sent))
    when(top, lambda: panel_top(sent))
    when(both(mate, r < 2), lambda: feeds(sent))

    when(hub, lambda: loop(0, 16, mirror_sent))

    def core1_drain():
        for which in range(3):
            across(which, sent)
        for n in range(2):
            parts_pair(n).wait_send()

    when(k == 1, core1_drain)

    def line_drain():
        for which in range(3):
            down(which, sent)
        for n in range(2):
            inverse_down(n, sent)

    when(c == 1, line_drain)

    def aide_drain():
        lead_copy(0).wait_send()
        lead_scatter(0, sent)

    when(aide, aide_drain)

    def helper_drain():
        lead_copy(1).wait_send()
        lead_scatter(1, sent)

    when(helper, helper_drain)

    def root_drain():
        from_root(sent, inverse_piece)
        from_root(sent, next_piece, 2)
        for n in range(2):
            from_root(sent, lambda p, n=n: inverse_first(n, p))

    when(root, root_drain)


def gather(kernel):
    bf16, f32 = jnp.bfloat16, jnp.float32
    dma = pltpu.SemaphoreType.DMA
    return pl.pallas_call(
        gather_kernel,
        out_shape=(
            jax.ShapeDtypeStruct((4, 2, 256, 256), bf16),
            jax.ShapeDtypeStruct((2, 2, 2, 256, 256), bf16),
            jax.ShapeDtypeStruct((3, 2, 256, 256), bf16),
        ),
        in_specs=[pl.BlockSpec(memory_space=pltpu.HBM)],
        out_specs=(
            pl.BlockSpec(memory_space=pl.ANY),
            pl.BlockSpec(memory_space=pl.ANY),
            pl.BlockSpec(memory_space=pltpu.VMEM),
        ),
        scratch_shapes=[
            pltpu.VMEM((16, 2, 16, 256), bf16),
            pltpu.VMEM((16, 16, 256), f32),
            pltpu.VMEM((8, 8, 128), f32),
            pltpu.VMEM((2, 32, 128), f32),
            pltpu.VMEM((3, 256, 256), bf16),
            pltpu.VMEM((384, 512), f32),
            pltpu.VMEM((2, 32, 128), f32),
            pltpu.VMEM((16, 16, 256), f32),
            pltpu.VMEM((8, 8, 128), f32),
            pltpu.VMEM((256, 768), f32),
            dma((32, 2)), dma((32,)), dma((32,)), dma((32,)),
            dma((16, 4)), dma((16,)), dma((16,)), dma((16,)),
            dma((2,)), dma((2,)),
            dma((16,)), dma((2,)), dma((3, 16)), dma((3,)), dma((3, 16)), dma((3, 16)), dma((2,)), dma((2,)),
            dma((4, 16)), dma((4,)), dma((2, 16)), dma((2,)), dma((3,)),
        ],
        compiler_params=pltpu.CompilerParams(
            collective_id=0, has_side_effects=True, vmem_limit_bytes=24 * 1024 * 1024
        ),
        name="gather_and_factor",
    )(kernel)


def update_kernel(kern, acol, brow, parts, panels, schur, old, pan, new, sems):
    r = lax.axis_index("row")
    c = lax.axis_index("col")
    k = lax.rem(c, 2)
    load = pltpu.make_async_copy(kern.at[0, :, 0], old, sems.at[0])
    load.start()
    mirror = []
    for j in range(2):
        halves = []
        for n in range(2):
            total = None
            for s in range(n + 1):
                for t in range(2):
                    term = jnp.dot(
                        parts[n + s, t],
                        brow[s, j, k],
                        preferred_element_type=jnp.float32,
                    )
                    total = term if total is None else total + term
            halves.append(total.astype(jnp.bfloat16))
        mirror.append(jnp.concatenate(halves, axis=0))
    tri = lax.broadcasted_iota(jnp.int32, (256, 256), 0) >= lax.broadcasted_iota(jnp.int32, (256, 256), 1)
    stores = []
    load.wait()
    for i in range(4):
        solved = []
        for n in range(2):
            total = None
            for s in range(n + 1):
                for t in range(2):
                    term = lax.dot_general(
                        acol[i, s],
                        parts[n + s, t],
                        (((1,), (1,)), ((), ())),
                        preferred_element_type=jnp.float32,
                    )
                    total = term if total is None else total + term
            solved.append(total)
        left = jnp.concatenate([a.astype(jnp.bfloat16) for a in solved], axis=1)
        if i == 0:
            solved[0] = jnp.where(jnp.logical_or(r != 0, tri), solved[0], 0.0)
            solved[1] = jnp.where(jnp.logical_or(r > 1, jnp.logical_and(r == 1, tri)), solved[1], 0.0)
        for n in range(2):
            pan[i, n] = solved[n]
        stores.append(pltpu.make_async_copy(pan.at[i], panels.at[0, i], sems.at[1 + 2 * i]))
        stores[-1].start()
        for j in range(2):
            change = jnp.dot(left, mirror[j], preferred_element_type=jnp.float32)
            out = (old[i, j].astype(jnp.float32) - change).astype(jnp.bfloat16)
            if i == 0:
                out = jnp.where(r >= 2, out, jnp.zeros_like(out))
            if j == 0:
                out = jnp.where(c >= 2, out, jnp.zeros_like(out))
            new[i, j] = out
        stores.append(pltpu.make_async_copy(new.at[i], schur.at[0, i, 0], sems.at[2 + 2 * i]))
        stores[-1].start()
    for store in stores:
        store.wait()


def update(kernel, *gathered):
    hbm = pl.BlockSpec(memory_space=pltpu.HBM)
    return pl.pallas_call(
        update_kernel,
        out_shape=(
            jax.ShapeDtypeStruct((1, 4, 2, 256, 256), jnp.float32),
            jax.ShapeDtypeStruct((1, 4, 1, 2, 256, 256), jnp.bfloat16),
        ),
        in_specs=[hbm] + [pl.BlockSpec(memory_space=pltpu.VMEM)] * 3,
        out_specs=(hbm, hbm),
        scratch_shapes=[
            pltpu.VMEM((4, 2, 256, 256), jnp.bfloat16),
            pltpu.VMEM((4, 2, 256, 256), jnp.float32),
            pltpu.VMEM((4, 2, 256, 256), jnp.bfloat16),
            pltpu.SemaphoreType.DMA((9,)),
        ],
        compiler_params=pltpu.CompilerParams(vmem_limit_bytes=32 * 1024 * 1024),
        name="solve_and_update",
    )(kernel, *gathered)


def per_device(kernel):
    kernel = pltpu.with_memory_space_constraint(kernel, pltpu.HBM)
    return update(kernel, *gather(kernel))


def solution(mesh):
    in_specs = (P("row", None, "col", None, None, None),)
    out_specs = (P("row", None, None, None, None), P("row", None, "col", None, None, None))
    return jax.shard_map(per_device, mesh=mesh, in_specs=in_specs, out_specs=out_specs, check_vma=False)
```

```python
import functools

import jax
import jax.numpy as jnp
from jax import lax
from jax.experimental import pallas as pl
from jax.experimental.pallas import tpu as pltpu
from jax.sharding import PartitionSpec as P

MESH = pl.DeviceIdType.MESH
HI = lax.Precision.HIGHEST
PLANE = sorted(((a, b) for a in range(4) for b in range(4) if a or b), key=lambda d: -min(d[0], 4 - d[0]) - min(d[1], 4 - d[1]))
NEAR = ((0, 1), (0, 3), (1, 0), (3, 0))
LINE = sorted(range(1, 16), key=lambda d: -min(d, 16 - d))
FIRST = (8, 4, 12, 1, 15)
RELAY = {4: (2, 6, 3, 5), 8: (7, 9), 12: (10, 14, 11, 13)}
SKIP = {0: 3, 3: 6, 6: 8, 13: 10, 10: 9}
BACK = {0: 13, 3: 2, 2: 1, 6: 5, 5: 4, 8: 7, 13: 14, 14: 15, 10: 11, 11: 12}


def lookup(key, pairs):
    value = jnp.int32(0)
    for k, v in pairs.items():
        value = jnp.where(key == k, jnp.int32(v), value)
    return value


def member(key, keys):
    hit = key == keys[0]
    for k in keys[1:]:
        hit = jnp.logical_or(hit, key == k)
    return hit


def dot32(a, b, dims):
    return lax.dot_general(a, b, (dims, ((), ())), precision=HI, preferred_element_type=jnp.float32)


def row(v, i):
    return jnp.broadcast_to(v[i : i + 1, :], (8, 128))

def lane(v, i):
    return jnp.broadcast_to(v[:, i : i + 1], (8, 128))


def eliminate(strips, off):
    row_iota = lax.broadcasted_iota(jnp.int32, (8, 128), 0)
    strips = list(strips)
    diag = [lane(strips[0], off + i) for i in range(8)]
    pivots = []
    for s in range(8):
        later = range(s + 1, 8)
        cols = {t: [lane(strips[t], off + 8 * s + i) for i in range(8)] for t in later}
        if s < 7:
            raw = [lane(strips[s + 1], off + 8 * (s + 1) + i) for i in range(8)]
        head = strips[s]
        pivot = jnp.zeros((8, 128), jnp.float32)
        recips = []
        for i in range(8):
            own = diag[i]
            recip = 1.0 / row(own, i)
            recips.append(recip)
            pivot = jnp.where(row_iota == i, own, pivot)
            for j in range(i + 1, 8):
                line = row(own, j)
                diag[j] = diag[j] - (own * line) * recip
                factor = line * recip
                for t in later:
                    cols[t][j] = cols[t][j] - cols[t][i] * factor
            head = head - jnp.where(row_iota > i, own * recip, 0.0) * row(head, i)
        strips[s] = head
        pivots.append(pivot)
        if s < 7:
            near = cols[s + 1]
            scaled = [near[i] * recips[i] for i in range(8)]
            diag = []
            for j in range(8):
                terms = [scaled[i] * row(near[i], j) for i in range(8)]
                while len(terms) > 1:
                    terms = [terms[a] + terms[a + 1] for a in range(0, len(terms), 2)]
                diag.append(raw[j] - terms[0])
        heads = [row(head, i) * recips[i] for i in range(8)]
        for t in later:
            terms = [cols[t][i] * heads[i] for i in range(8)]
            while len(terms) > 1:
                terms = [terms[a] + terms[a + 1] for a in range(0, len(terms), 2)]
            strips[t] = strips[t] - terms[0]
    return strips, pivots


def factor_phase(g, store, middle):
    col_iota = lax.broadcasted_iota(jnp.int32, (8, 128), 1)
    row_iota = lax.broadcasted_iota(jnp.int32, (8, 128), 0)
    for b in range(4):
        odd = b % 2
        lo = 64 + 64 * b
        win = 128 * (b // 2)
        off = 64 * odd
        strips = []
        tile = g[lo:lo+64, win:win+128]
        for s in range(8):
            if odd:
                unit = jnp.where(col_iota == row_iota + 8 * s, 1.0, 0.0)
                strips.append(jnp.where(col_iota >= 64, tile[8*s:8*s+8], unit))
            else:
                unit = jnp.where(col_iota == row_iota + 8 * s + 64, 1.0, 0.0)
                strips.append(jnp.where(col_iota < 64, tile[8*s:8*s+8], unit))
        strips, pivots = eliminate(strips, off)
        keep = (col_iota < 64) if odd else (col_iota >= 64)
        wide = jnp.concatenate([jnp.where(keep, a * lax.rsqrt(p), 0.0) for a, p in zip(strips, pivots)], axis=0)
        turned = pltpu.roll(wide, 64, 1)
        low = wide if odd else turned
        high = turned if odd else wide
        if b == 1:
            middle()
        store(b, jnp.where(lax.broadcasted_iota(jnp.int32,(32,128),1) < 64, low[32:], high[:32]))
        base = lo if odd else lo - 64
        if b < 3:
            nwin = 128 * ((b + 1) // 2)
            u = dot32(wide, g[base:base+128, nwin:nwin+128], ((1,), (0,)))
            nxt = lo + 64
            noff = 64 * (1 - odd)
            if odd:
                g[nxt:nxt+64, nwin:nwin+128] = g[nxt:nxt+64, nwin:nwin+128] - dot32(u[:, 0:64], u, ((0,), (0,)))
            else:
                g[nxt:nxt+64, nwin:nwin+128] = g[nxt:nxt+64, nwin:nwin+128] - dot32(u, u, ((0,), (0,)))[64:128]
        lines = dot32(wide, g[base : base + 128, :], ((1,), (0,)))
        g[lo:lo+64, :] = lines
        if b < 3:
            first = 64 * (b + 1)
            change = dot32(lines[:, 0:256], lines, ((0,), (0,)))
            nxt = lo + 64
            nwin = 128 * ((b + 1) // 2)
            for lo_c, hi_c in ((0, nwin), (nwin + 128, 512)):
                if hi_c > lo_c:
                    g[nxt:nxt+64, lo_c:hi_c] = g[nxt:nxt+64, lo_c:hi_c] - change[first:first+64, lo_c:hi_c]
            if b < 2:
                g[nxt+64:320, :] = g[nxt+64:320, :] - change[first+64:256, :]


def set_identity(g):
    rows = lax.broadcasted_iota(jnp.int32, (256, 256), 0)
    cols = lax.broadcasted_iota(jnp.int32, (256, 256), 1)
    g[64:320, 256:512] = jnp.where(rows == cols, 1.0, 0.0)


def gather_kernel(
    kern, acol, brow, parts,
    lead, inv0, inv1, xs, gbuf, g, x_src, inv_src, inv1_src, work,
    p_send, p_recv, p_sib_send, p_sib_recv, m_send, m_recv, m_sib_send, m_sib_recv,
    lead_send, lead_recv, gs_send, gh_recv, gd_send, gd_recv, ga_send, ga_recv, parts_send, parts_recv,
    xr_send, xh_recv, xd_send, xd_recv, loc,
):
    r = lax.axis_index("row")
    c = lax.axis_index("col")
    x, y = lax.div(r, 4), lax.rem(r, 4)
    z, k = lax.div(c, 2), lax.rem(c, 2)
    zero, one = jnp.int32(0), jnp.int32(1)
    sibling = c + 1 - 2 * k
    both, neither = jnp.logical_and, jnp.logical_not
    top = z == 0
    inner = neither(top)

    def hub_core(row):
        return jnp.where(both(top, row != 0), 0, 1)

    hub = k == hub_core(r)
    mate = neither(hub)
    root = both(r == 0, c == 0)
    aide = both(r == 0, c == 1)
    helper = both(r == 1, c == 1)
    head = both(c == 1, r != 0)
    runner = both(k == 0, inner)
    skip_to = lookup(z, SKIP)
    back_to = lookup(z, BACK)
    has_skip = member(z, list(SKIP))
    has_back = member(z, list(BACK))
    parent = lookup(z, {v: q for q, v in list(SKIP.items()) + list(BACK.items())})
    children = has_skip.astype(jnp.int32) + has_back.astype(jnp.int32)
    relay_of = lookup(z, {v: q for q, vs in RELAY.items() for v in vs})
    barrier = pltpu.get_barrier_semaphore()

    def remote(src, dst, send, recv, row, col):
        return pltpu.make_async_remote_copy(
            src_ref=src, dst_ref=dst, send_sem=send, recv_sem=recv, device_id=(row, col), device_id_type=MESH
        )

    def signal(row, col):
        pl.semaphore_signal(barrier, inc=1, device_id=(row, col), device_id_type=MESH)

    def loop(lo, hi, body):
        def step(d, carry):
            body(d)
            return carry

        lax.fori_loop(lo, hi, step, 0)

    def when(cond, body):
        @pl.when(cond)
        def _():
            body()

    def start(copy):
        copy.start()

    def sent(copy):
        copy.wait_send()

    def peer(d):
        return lax.rem(x + d[0], 4) * 4 + lax.rem(y + d[1], 4)

    own_block = kern.at[0, 0, 0, 0]
    own_panel = pltpu.make_async_copy(kern.at[0, :, 0, 0], acol.at[:, k], loc.at[0])
    own_rows = pltpu.make_async_copy(kern.at[0, 0, 0], brow.at[lax.rem(r, 2), :, k], loc.at[1])
    own_lead = pltpu.make_async_copy(own_block, gbuf.at[0], loc.at[2])
    aide_piece = pltpu.make_async_copy(own_block.at[pl.ds(0, 16)], lead.at[0, 0], loc.at[2])
    helper_piece = pltpu.make_async_copy(own_block.at[pl.ds(16, 16)], lead.at[1, 1], loc.at[2])
    when(root, lambda: own_lead.start())
    when(aide, lambda: aide_piece.start())
    when(helper, lambda: helper_piece.start())
    when(top, lambda: own_panel.start())
    when(r < 2, lambda: own_rows.start())

    signal(r, sibling)

    def greet_panel():
        signal(r, 2 * parent)
        when(parent == 0, lambda: signal(r, one))

    when(runner, greet_panel)

    def greet_plane():
        for d in PLANE:
            signal(peer(d), c)
        when(inner, lambda: signal(r, one))
        when(relay_of != 0, lambda: signal(r, 2 * relay_of + 1))

    when(k == 1, greet_plane)

    def greet_mirror():
        for d in NEAR:
            signal(peer(d), hub_core(peer(d)))

    when(both(hub, top), greet_mirror)

    def greet_sources():
        signal(zero, zero)
        signal(zero, one)
        when(r != 1, lambda: signal(one, one))

    when(head, greet_sources)
    when(jnp.logical_or(root, aide), lambda: signal(one, one))

    def arrive():
        plane = jnp.where(k == 1, 15, 0) + jnp.where(both(hub, top), 4, 0)
        line = jnp.where(top, 2, jnp.where(k == 0, children, 0))
        down = jnp.where(c == 1, 15, 0)
        relays = jnp.where(jnp.logical_or(z == 4, z == 12), 4, jnp.where(z == 8, 2, 0))
        down = down + jnp.where(k == 1, relays, 0)
        more = jnp.where(root, 15, 0) + jnp.where(aide, 15, 0) + jnp.where(helper, 16, 0)
        pl.semaphore_wait(barrier, 1 + plane + line + down + more)
        when(top, lambda: own_panel.wait())
        when(r < 2, lambda: own_rows.wait())
        when(aide, lambda: aide_piece.wait())
        when(helper, lambda: helper_piece.wait())

    def panel_chunk(n):
        col, i, quarter = lax.div(n, 16), lax.rem(lax.div(n, 4), 4), lax.rem(n, 4)
        return acol.at[i, col, pl.ds(pl.multiple_of(64 * quarter, 64), 64)]

    def panel_skip(n):
        return remote(panel_chunk(n), panel_chunk(n), p_send.at[n, 0], p_recv.at[n], r, 2 * skip_to)

    def panel_back(n):
        return remote(panel_chunk(n), panel_chunk(n), p_send.at[n, 1], p_recv.at[n], r, 2 * back_to)

    def panel_pair(n):
        return remote(panel_chunk(n), panel_chunk(n), p_sib_send.at[n], p_sib_recv.at[n], r, sibling)

    def panel_top(act):
        def step(m):
            act(panel_skip(16 * k + m))
            act(panel_back(16 * k + m))

        loop(0, 16, step)
        loop(0, 16, lambda m: act(panel_pair(16 * k + m)))

    def panel_line(t):
        n = t
        panel_skip(n).wait_recv()
        when(has_skip, lambda: panel_skip(n).start())
        when(has_back, lambda: panel_back(n).start())
        panel_pair(n).start()

    def panel_line_sent(n):
        when(has_skip, lambda: panel_skip(n).wait_send())
        when(has_back, lambda: panel_back(n).wait_send())
        panel_pair(n).wait_send()

    def mirror_chunk(s, m):
        j, kc, half = lax.div(m, 4), lax.rem(lax.div(m, 2), 2), lax.rem(m, 2)
        return brow.at[s, j, kc, pl.ds(pl.multiple_of(128 * half, 128), 128)]

    def mirror_copy(s, m, way, row):
        chunk = mirror_chunk(s, m)
        return remote(chunk, chunk, m_send.at[8 * s + m, way], m_recv.at[8 * s + m], row, 2 * z + hub_core(row))

    def mirror_pair(s, m):
        n = 8 * s + m
        return remote(mirror_chunk(s, m), mirror_chunk(s, m), m_sib_send.at[n], m_sib_recv.at[n], r, sibling)

    def mirror_feed(j, half):
        m = 4 * j + 2 * k + half
        n = 8 * r + m
        return remote(mirror_chunk(r, m), mirror_chunk(r, m), m_sib_send.at[n], m_recv.at[n], r, sibling)

    def mirror_each(s, m, act):
        j, kc = lax.div(m, 4), lax.rem(lax.div(m, 2), 2)
        rel = lax.rem(y + 4 - s, 4)
        ring = jnp.logical_or(j == 1, x == 0)
        line = jnp.logical_or(j == 0, rel == 0)
        ring_up = both(ring, jnp.logical_or(rel == 0, both(s == 1, rel == 1)))
        ring_down = both(ring, jnp.logical_or(rel == 0, both(s == 0, rel == 3)))
        line_up = both(line, jnp.logical_or(x == 0, both(s == 0, x == 1)))
        line_down = both(line, jnp.logical_or(x == 0, both(s == 1, x == 3)))
        when(ring_up, lambda: act(mirror_copy(s, m, 0, peer((0, 1)))))
        when(ring_down, lambda: act(mirror_copy(s, m, 1, peer((0, 3)))))
        when(line_up, lambda: act(mirror_copy(s, m, 2, peer((1, 0)))))
        when(line_down, lambda: act(mirror_copy(s, m, 3, peer((3, 0)))))
        when(both(kc != k, r != s), lambda: act(mirror_pair(s, m)))

    def mirror_step(n):
        nearer = jnp.where(jnp.logical_or(y == 0, y == 3), 0, 1)
        s = lax.rem(lax.div(n, 8) + nearer, 2)
        m = lax.rem(n, 8)
        kc = lax.rem(lax.div(m, 2), 2)
        when(jnp.logical_or(r != s, kc != k), lambda: mirror_copy(s, m, 0, r).wait_recv())
        mirror_each(s, m, start)

    def mirror_sent(n):
        mirror_each(lax.div(n, 8), lax.rem(n, 8), sent)

    def feeds(act):
        for j in range(2):
            for half in range(2):
                act(mirror_feed(j, half))

    def mirror_take():
        for s in range(2):

            def take(s=s):
                for j in range(2):
                    for half in range(2):
                        mirror_pair(s, 4 * j + 2 * k + half).wait_recv()

            when(r != s, take)

    def lead_from(n, p):
        rows = own_block.at[pl.ds(16 * p, 16)]
        return remote(rows, lead.at[p, n], gs_send.at[p], gh_recv.at[n], jnp.int32(p), one)

    def lead_scatter(n, act):
        for p in range(16):
            if p != n:
                act(lead_from(n, p))

    def view(which, p):
        if which < 2:
            return (lead, inv0)[which].at[p]
        return inv1.at[lax.div(p, 2)]

    def takes_part(which, row):
        return row >= 0 if which < 2 else lax.rem(row, 2) == 0

    def line_copy(which, d):
        piece = view(which, r)
        return remote(piece, piece, gd_send.at[which, d], gd_recv.at[which], r, jnp.int32(2 * d + 1))

    def down(which, act):
        def go():
            for d in FIRST:
                act(line_copy(which, d))

        when(takes_part(which, r), go)

    def relay(act, copy):
        for q, targets in RELAY.items():

            def go(targets=targets):
                for d in targets:
                    act(copy(d))

            when(z == q, go)

    def relay_piece(which, act):
        when(takes_part(which, r), lambda: relay(act, lambda d: line_copy(which, d)))

    def across(which, act):
        def go():
            for n, d in enumerate(PLANE):
                act(remote(view(which, r), view(which, r), ga_send.at[which, n], ga_recv.at[which, r], peer(d), c))

        when(takes_part(which, r), go)

    def piece_taken(which):
        copy = remote(view(which, r), view(which, r), gd_send.at[which, 0], gd_recv.at[which], r, sibling)
        when(takes_part(which, r), lambda: copy.wait_recv())

    def collect(which):
        def take(d):
            p = lax.rem(r + d, 16)
            copy = remote(view(which, p), view(which, p), ga_send.at[which, 0], ga_recv.at[which, p], r, sibling)
            when(takes_part(which, p), lambda: copy.wait_recv())

        loop(1, 16, take)

    def inverse_piece(p):
        return remote(inv_src.at[p], inv0.at[p], xr_send.at[0, p], xh_recv.at[0], jnp.int32(p), one)

    def next_piece(p):
        return remote(inv1_src.at[p // 2], inv1.at[p // 2], xr_send.at[1, p], xh_recv.at[1], jnp.int32(p), one)

    def inverse_first(n, p):
        return remote(x_src.at[n], xs.at[n], xr_send.at[2 + n, p], xh_recv.at[2 + n], jnp.int32(p), one)

    def from_root(act, copy, step=1):
        for d in PLANE:
            p = 4 * d[0] + d[1]
            if p % step == 0:
                act(copy(p))
        act(copy(0))

    def inverse_copy(n, d):
        return remote(xs.at[n], xs.at[n], xd_send.at[n, d], xd_recv.at[n], r, jnp.int32(2 * d + 1))

    def inverse_down(n, act):
        for d in FIRST if n == 0 else LINE:
            act(inverse_copy(n, d))

    def inverse_relay(n, act):
        if n == 0:
            relay(act, lambda d: inverse_copy(n, d))

    def inverse_taken(n):
        remote(xs.at[n], xs.at[n], xd_send.at[n, 0], xd_recv.at[n], r, sibling).wait_recv()

    def parts_pair(n):
        block = parts.at[0] if n == 0 else parts.at[pl.ds(1, 2)]
        return remote(block, block, parts_send.at[n], parts_recv.at[n], r, sibling)

    def lead_copy(n):
        return remote(own_block, gbuf.at[n + 1], lead_send.at[n], lead_recv.at[n], zero, zero)

    def root_main():
        own_lead.wait()
        g[0:64, :] = jnp.zeros((64, 512), jnp.float32)
        g[320:384, :] = jnp.zeros((64, 512), jnp.float32)
        g[64:320, 0:256] = gbuf[0].astype(jnp.float32)
        set_identity(g)

        def bulk():
            arrive()
            feeds(start)
            panel_top(start)

        def second_half():
            for p in range(16):
                inv_src[p] = g[64 + 16 * p : 80 + 16 * p, 256:512]
            from_root(start, inverse_piece)
            lead_copy(0).wait_recv()
            lead_copy(1).wait_recv()
            side = dot32(g[64:320, 256:512], gbuf[1].astype(jnp.float32), ((1,), (0,)))
            g[64:320, 0:256] = gbuf[2].astype(jnp.float32) - dot32(side, side, ((0,), (0,)))
            set_identity(g)

        def phase(it):
            def store(n, packed):
                if n < 2:
                    for part in range(4):
                        inv1_src[4 * n + part] = packed[8 * part : 8 * part + 8]
                    if n == 1:
                        when(it == 1, lambda: from_root(start, next_piece, 2))
                else:
                    x_src[n - 2] = packed
                    when(it == 1, lambda: from_root(start, lambda p: inverse_first(n - 2, p)))

            factor_phase(g, store, lambda: when(it == 0, bulk))
            when(it == 0, second_half)

        loop(0, 2, phase)

    when(root, root_main)
    when(neither(root), arrive)

    def top_sends():
        when(aide, lambda: lead_copy(0).start())
        when(helper, lambda: lead_copy(1).start())
        panel_top(start)
        when(aide, lambda: lead_scatter(0, start))
        when(helper, lambda: lead_scatter(1, start))

    when(both(top, neither(root)), top_sends)
    when(both(both(mate, r < 2), neither(root)), lambda: feeds(start))

    def top_spread(which):
        down(which, start)
        across(which, start)

    def head_inverses(p):
        when(takes_part(2, r), lambda: next_piece(p).wait_recv())
        top_spread(2)
        for n in range(2):
            inverse_first(n, p).wait_recv()
            inverse_down(n, start)

    def aide_main():
        loop(0, 8, mirror_step)
        lead_from(1, 0).wait_recv()
        top_spread(0)
        inverse_piece(0).wait_recv()
        top_spread(1)
        loop(8, 16, mirror_step)
        head_inverses(0)

    when(aide, aide_main)
    when(both(hub, neither(aide)), lambda: loop(0, 16, mirror_step))

    def head_main():
        lead_from(0, 1).wait_recv()
        when(neither(helper), lambda: lead_from(1, 2).wait_recv())
        top_spread(0)
        inverse_piece(1).wait_recv()
        top_spread(1)
        head_inverses(2)

    when(head, head_main)

    def line_spread():
        for which in range(3):
            piece_taken(which)
            relay_piece(which, start)
            across(which, start)

    when(both(k == 1, inner), line_spread)
    when(runner, lambda: loop(0, 32, panel_line))

    def put(block, lo, hi, values):
        high = values.astype(jnp.bfloat16)
        parts[block, 0, lo:hi] = high
        parts[block, 1, lo:hi] = (values - high.astype(jnp.float32)).astype(jnp.bfloat16)

    def assemble():
        def block(n):
            return jnp.concatenate([lead[p, n] for p in range(16)], axis=0).astype(jnp.float32)

        collect(0)
        collect(1)
        first_inverse = jnp.concatenate([inv0[p] for p in range(16)], axis=0)
        put(0, 0, 256, first_inverse)
        parts_pair(0).start()
        side = dot32(first_inverse, block(0), ((1,), (0,)))
        work[:, 0:256] = block(1) - dot32(side, side, ((0,), (0,)))
        work[:, 256:512] = -dot32(side, first_inverse, ((0,), (0,)))
        rows = lax.broadcasted_iota(jnp.int32, (256, 256), 0)
        cols = lax.broadcasted_iota(jnp.int32, (256, 256), 1)
        work[:, 512:768] = jnp.where(rows == cols, 1.0, 0.0)
        collect(2)
        for n in range(4):
            if n < 2:
                packed = jnp.concatenate([inv1[4 * n + p] for p in range(4)], axis=0)
            else:

                def arrived(n=n - 2):
                    inverse_taken(n)
                    inverse_relay(n, start)

                when(inner, arrived)
                packed = xs[n - 2]
            inverse = jnp.concatenate([packed[:, 64:128], packed[:, 0:64]], axis=0)
            lo, hi = 64 * n, 64 * n + 64
            lines = dot32(inverse, work[lo:hi, :], ((1,), (0,)))
            put(1, lo, hi, lines[:, 256:512])
            put(2, lo, hi, lines[:, 512:768])
            if n < 3:
                work[hi:256, :] = work[hi:256, :] - dot32(lines[:, hi:256], lines, ((0,), (0,)))
        parts_pair(1).start()

    when(k == 1, assemble)

    def parts_take():
        parts_pair(0).wait_recv()
        parts_pair(1).wait_recv()

    when(k == 0, parts_take)
    when(mate, mirror_take)
    when(both(k == 1, inner), lambda: loop(0, 32, lambda n: panel_pair(n).wait_recv()))
    when(top, lambda: loop(0, 16, lambda m: panel_pair(16 * (1 - k) + m).wait_recv()))

    when(runner, lambda: loop(0, 32, panel_line_sent))
    when(top, lambda: panel_top(sent))
    when(both(mate, r < 2), lambda: feeds(sent))

    when(hub, lambda: loop(0, 16, mirror_sent))

    def core1_drain():
        for which in range(3):
            across(which, sent)
        for n in range(2):
            parts_pair(n).wait_send()

    when(k == 1, core1_drain)

    def line_drain():
        for which in range(3):
            down(which, sent)
        for n in range(2):
            inverse_down(n, sent)

    when(c == 1, line_drain)

    def relay_drain():
        for which in range(3):
            relay_piece(which, sent)
        inverse_relay(0, sent)

    when(both(k == 1, inner), relay_drain)

    def aide_drain():
        lead_copy(0).wait_send()
        lead_scatter(0, sent)

    when(aide, aide_drain)

    def helper_drain():
        lead_copy(1).wait_send()
        lead_scatter(1, sent)

    when(helper, helper_drain)

    def root_drain():
        from_root(sent, inverse_piece)
        from_root(sent, next_piece, 2)
        for n in range(2):
            from_root(sent, lambda p, n=n: inverse_first(n, p))

    when(root, root_drain)


def gather(kernel):
    bf16, f32 = jnp.bfloat16, jnp.float32
    dma = pltpu.SemaphoreType.DMA
    return pl.pallas_call(
        gather_kernel,
        out_shape=(
            jax.ShapeDtypeStruct((4, 2, 256, 256), bf16),
            jax.ShapeDtypeStruct((2, 2, 2, 256, 256), bf16),
            jax.ShapeDtypeStruct((3, 2, 256, 256), bf16),
        ),
        in_specs=[pl.BlockSpec(memory_space=pltpu.HBM)],
        out_specs=(
            pl.BlockSpec(memory_space=pl.ANY),
            pl.BlockSpec(memory_space=pl.ANY),
            pl.BlockSpec(memory_space=pltpu.VMEM),
        ),
        scratch_shapes=[
            pltpu.VMEM((16, 2, 16, 256), bf16),
            pltpu.VMEM((16, 16, 256), f32),
            pltpu.VMEM((8, 8, 128), f32),
            pltpu.VMEM((2, 32, 128), f32),
            pltpu.VMEM((3, 256, 256), bf16),
            pltpu.VMEM((384, 512), f32),
            pltpu.VMEM((2, 32, 128), f32),
            pltpu.VMEM((16, 16, 256), f32),
            pltpu.VMEM((8, 8, 128), f32),
            pltpu.VMEM((256, 768), f32),
            dma((32, 2)), dma((32,)), dma((32,)), dma((32,)),
            dma((16, 4)), dma((16,)), dma((16,)), dma((16,)),
            dma((2,)), dma((2,)),
            dma((16,)), dma((2,)), dma((3, 16)), dma((3,)), dma((3, 16)), dma((3, 16)), dma((2,)), dma((2,)),
            dma((4, 16)), dma((4,)), dma((2, 16)), dma((2,)), dma((3,)),
        ],
        compiler_params=pltpu.CompilerParams(
            collective_id=0, has_side_effects=True, vmem_limit_bytes=24 * 1024 * 1024
        ),
        name="gather_and_factor",
    )(kernel)


def update_kernel(kern, acol, brow, parts, panels, schur, old, pan, new, sems):
    r = lax.axis_index("row")
    c = lax.axis_index("col")
    k = lax.rem(c, 2)
    load = pltpu.make_async_copy(kern.at[0, :, 0], old, sems.at[0])
    load.start()
    f32 = jnp.float32
    tri = lax.broadcasted_iota(jnp.int32, (256, 256), 0) >= lax.broadcasted_iota(jnp.int32, (256, 256), 1)
    stores = []

    def store(src, dst):
        stores.append(pltpu.make_async_copy(src, dst, sems.at[1 + len(stores)]))
        stores[-1].start()

    def rows(a, b):
        return lax.dot_general(a, b, (((1,), (1,)), ((), ())), preferred_element_type=f32)

    lefts = []
    for h in range(2):
        a, b = (jnp.concatenate([acol[2 * h, s], acol[2 * h + 1, s]], axis=0) for s in range(2))
        first = rows(a, parts[0, 0]) + rows(a, parts[0, 1])
        second = rows(a, parts[1, 0]) + rows(a, parts[1, 1]) + rows(b, parts[2, 0]) + rows(b, parts[2, 1])
        lefts.append(jnp.concatenate([first.astype(jnp.bfloat16), second.astype(jnp.bfloat16)], axis=1))
        for e in range(2):
            i = 2 * h + e
            for n, solved in enumerate((first, second)):
                part = solved[256 * e : 256 * e + 256]
                if i == 0:
                    whole = jnp.logical_or(r > n, jnp.logical_and(r == n, tri))
                    part = jnp.where(whole, part, 0.0)
                pan[i, n] = part
            store(pan.at[i], panels.at[0, i])
    columns = []
    for j in range(2):
        a, b = brow[0, j, k], brow[1, j, k]
        upper = jnp.dot(parts[0, 0], a, preferred_element_type=f32) + jnp.dot(
            parts[0, 1], a, preferred_element_type=f32
        )
        lower = jnp.dot(parts[1, 0], a, preferred_element_type=f32) + jnp.dot(
            parts[1, 1], a, preferred_element_type=f32
        )
        lower = lower + jnp.dot(parts[2, 0], b, preferred_element_type=f32)
        lower = lower + jnp.dot(parts[2, 1], b, preferred_element_type=f32)
        columns.append(jnp.concatenate([upper, lower], axis=0).astype(jnp.bfloat16))
    mirror = jnp.concatenate(columns, axis=1)
    load.wait()
    for h in range(2):
        change = jnp.dot(lefts[h], mirror, preferred_element_type=f32)
        for e in range(2):
            i = 2 * h + e
            for j in range(2):
                out = old[i, j].astype(f32) - change[256 * e : 256 * e + 256, 256 * j : 256 * j + 256]
                if i == 0:
                    out = jnp.where(r >= 2, out, 0.0)
                if j == 0:
                    out = jnp.where(c >= 2, out, 0.0)
                new[i, j] = out.astype(jnp.bfloat16)
            store(new.at[i], schur.at[0, i, 0])
    for copy in stores:
        copy.wait()


def update(kernel, *gathered):
    hbm = pl.BlockSpec(memory_space=pltpu.HBM)
    return pl.pallas_call(
        update_kernel,
        out_shape=(
            jax.ShapeDtypeStruct((1, 4, 2, 256, 256), jnp.float32),
            jax.ShapeDtypeStruct((1, 4, 1, 2, 256, 256), jnp.bfloat16),
        ),
        in_specs=[hbm] + [pl.BlockSpec(memory_space=pltpu.VMEM)] * 3,
        out_specs=(hbm, hbm),
        scratch_shapes=[
            pltpu.VMEM((4, 2, 256, 256), jnp.bfloat16),
            pltpu.VMEM((4, 2, 256, 256), jnp.float32),
            pltpu.VMEM((4, 2, 256, 256), jnp.bfloat16),
            pltpu.SemaphoreType.DMA((9,)),
        ],
        compiler_params=pltpu.CompilerParams(vmem_limit_bytes=32 * 1024 * 1024),
        name="solve_and_update",
    )(kernel, *gathered)


def per_device(kernel):
    kernel = pltpu.with_memory_space_constraint(kernel, pltpu.HBM)
    return update(kernel, *gather(kernel))


def solution(mesh):
    in_specs = (P("row", None, "col", None, None, None),)
    out_specs = (P("row", None, None, None, None), P("row", None, "col", None, None, None))
    return jax.shard_map(per_device, mesh=mesh, in_specs=in_specs, out_specs=out_specs, check_vma=False)
```

```python
import functools

import jax
import jax.numpy as jnp
from jax import lax
from jax.experimental import pallas as pl
from jax.experimental.pallas import tpu as pltpu
from jax.sharding import PartitionSpec as P

MESH = pl.DeviceIdType.MESH
HI = lax.Precision.HIGHEST
PLANE = sorted(((a, b) for a in range(4) for b in range(4) if a or b), key=lambda d: -min(d[0], 4 - d[0]) - min(d[1], 4 - d[1]))
NEAR = ((0, 1), (0, 3), (1, 0), (3, 0))
LINE = sorted(range(1, 16), key=lambda d: -min(d, 16 - d))
FIRST = (8, 4, 12, 1, 15)
RELAY = {4: (2, 6, 3, 5), 8: (7, 9), 12: (10, 14, 11, 13)}
SKIP = {0: 3, 3: 6, 6: 8, 13: 10, 10: 9}
BACK = {0: 13, 3: 2, 2: 1, 6: 5, 5: 4, 8: 7, 13: 14, 14: 15, 10: 11, 11: 12}


def lookup(key, pairs):
    value = jnp.int32(0)
    for k, v in pairs.items():
        value = jnp.where(key == k, jnp.int32(v), value)
    return value


def member(key, keys):
    hit = key == keys[0]
    for k in keys[1:]:
        hit = jnp.logical_or(hit, key == k)
    return hit


def dot32(a, b, dims):
    return lax.dot_general(a, b, (dims, ((), ())), precision=HI, preferred_element_type=jnp.float32)


def row(v, i):
    return jnp.broadcast_to(v[i : i + 1, :], (8, 128))

def lane(v, i):
    return jnp.broadcast_to(v[:, i : i + 1], (8, 128))


def eliminate(strips, off):
    row_iota = lax.broadcasted_iota(jnp.int32, (8, 128), 0)
    strips = list(strips)
    diag = [lane(strips[0], off + i) for i in range(8)]
    pivots = []
    for s in range(8):
        later = range(s + 1, 8)
        cols = {t: [lane(strips[t], off + 8 * s + i) for i in range(8)] for t in later}
        if s < 7:
            raw = [lane(strips[s + 1], off + 8 * (s + 1) + i) for i in range(8)]
        head = strips[s]
        pivot = jnp.zeros((8, 128), jnp.float32)
        recips = []
        for i in range(8):
            own = diag[i]
            recip = 1.0 / row(own, i)
            recips.append(recip)
            pivot = jnp.where(row_iota == i, own, pivot)
            for j in range(i + 1, 8):
                line = row(own, j)
                diag[j] = diag[j] - (own * line) * recip
                factor = line * recip
                for t in later:
                    cols[t][j] = cols[t][j] - cols[t][i] * factor
            head = head - jnp.where(row_iota > i, own * recip, 0.0) * row(head, i)
        strips[s] = head
        pivots.append(pivot)
        if s < 7:
            near = cols[s + 1]
            scaled = [near[i] * recips[i] for i in range(8)]
            diag = []
            for j in range(8):
                terms = [scaled[i] * row(near[i], j) for i in range(8)]
                while len(terms) > 1:
                    terms = [terms[a] + terms[a + 1] for a in range(0, len(terms), 2)]
                diag.append(raw[j] - terms[0])
        heads = [row(head, i) * recips[i] for i in range(8)]
        for t in later:
            terms = [cols[t][i] * heads[i] for i in range(8)]
            while len(terms) > 1:
                terms = [terms[a] + terms[a + 1] for a in range(0, len(terms), 2)]
            strips[t] = strips[t] - terms[0]
    return strips, pivots


def factor_phase(g, store, middle):
    col_iota = lax.broadcasted_iota(jnp.int32, (8, 128), 1)
    row_iota = lax.broadcasted_iota(jnp.int32, (8, 128), 0)
    for b in range(4):
        odd = b % 2
        lo = 64 + 64 * b
        win = 128 * (b // 2)
        off = 64 * odd
        strips = []
        tile = g[lo:lo+64, win:win+128]
        for s in range(8):
            if odd:
                unit = jnp.where(col_iota == row_iota + 8 * s, 1.0, 0.0)
                strips.append(jnp.where(col_iota >= 64, tile[8*s:8*s+8], unit))
            else:
                unit = jnp.where(col_iota == row_iota + 8 * s + 64, 1.0, 0.0)
                strips.append(jnp.where(col_iota < 64, tile[8*s:8*s+8], unit))
        strips, pivots = eliminate(strips, off)
        keep = (col_iota < 64) if odd else (col_iota >= 64)
        wide = jnp.concatenate([jnp.where(keep, a * lax.rsqrt(p), 0.0) for a, p in zip(strips, pivots)], axis=0)
        turned = pltpu.roll(wide, 64, 1)
        low = wide if odd else turned
        high = turned if odd else wide
        if b == 1:
            middle()
        store(b, jnp.where(lax.broadcasted_iota(jnp.int32,(32,128),1) < 64, low[32:], high[:32]))
        base = lo if odd else lo - 64
        if b < 3:
            nwin = 128 * ((b + 1) // 2)
            u = dot32(wide, g[base:base+128, nwin:nwin+128], ((1,), (0,)))
            nxt = lo + 64
            noff = 64 * (1 - odd)
            if odd:
                g[nxt:nxt+64, nwin:nwin+128] = g[nxt:nxt+64, nwin:nwin+128] - dot32(u[:, 0:64], u, ((0,), (0,)))
            else:
                g[nxt:nxt+64, nwin:nwin+128] = g[nxt:nxt+64, nwin:nwin+128] - dot32(u, u, ((0,), (0,)))[64:128]
        lines = dot32(wide, g[base : base + 128, :], ((1,), (0,)))
        g[lo:lo+64, :] = lines
        if b < 3:
            first = 64 * (b + 1)
            change = dot32(lines[:, 0:256], lines, ((0,), (0,)))
            nxt = lo + 64
            nwin = 128 * ((b + 1) // 2)
            for lo_c, hi_c in ((0, nwin), (nwin + 128, 512)):
                if hi_c > lo_c:
                    g[nxt:nxt+64, lo_c:hi_c] = g[nxt:nxt+64, lo_c:hi_c] - change[first:first+64, lo_c:hi_c]
            if b < 2:
                g[nxt+64:320, :] = g[nxt+64:320, :] - change[first+64:256, :]


def set_identity(g):
    rows = lax.broadcasted_iota(jnp.int32, (256, 256), 0)
    cols = lax.broadcasted_iota(jnp.int32, (256, 256), 1)
    g[64:320, 256:512] = jnp.where(rows == cols, 1.0, 0.0)


def gather_kernel(
    kern, acol, brow, parts,
    lead, inv0, inv1, xs, gbuf, g, x_src, inv_src, inv1_src, work,
    p_send, p_recv, p_sib_send, p_sib_recv, m_send, m_recv, m_sib_send, m_sib_recv,
    lead_send, lead_recv, gs_send, gh_recv, gd_send, gd_recv, ga_send, ga_recv, parts_send, parts_recv,
    xr_send, xh_recv, xd_send, xd_recv, loc,
):
    r = lax.axis_index("row")
    c = lax.axis_index("col")
    x, y = lax.div(r, 4), lax.rem(r, 4)
    z, k = lax.div(c, 2), lax.rem(c, 2)
    zero, one = jnp.int32(0), jnp.int32(1)
    sibling = c + 1 - 2 * k
    both, neither = jnp.logical_and, jnp.logical_not
    top = z == 0
    inner = neither(top)

    def hub_core(row):
        return jnp.where(both(top, row != 0), 0, 1)

    hub = k == hub_core(r)
    mate = neither(hub)
    root = both(r == 0, c == 0)
    aide = both(r == 0, c == 1)
    helper = both(r == 1, c == 1)
    head = both(c == 1, r != 0)
    runner = both(k == 0, inner)
    skip_to = lookup(z, SKIP)
    back_to = lookup(z, BACK)
    has_skip = member(z, list(SKIP))
    has_back = member(z, list(BACK))
    parent = lookup(z, {v: q for q, v in list(SKIP.items()) + list(BACK.items())})
    children = has_skip.astype(jnp.int32) + has_back.astype(jnp.int32)
    relay_of = lookup(z, {v: q for q, vs in RELAY.items() for v in vs})
    barrier = pltpu.get_barrier_semaphore()

    def remote(src, dst, send, recv, row, col):
        return pltpu.make_async_remote_copy(
            src_ref=src, dst_ref=dst, send_sem=send, recv_sem=recv, device_id=(row, col), device_id_type=MESH
        )

    def signal(row, col):
        pl.semaphore_signal(barrier, inc=1, device_id=(row, col), device_id_type=MESH)

    def loop(lo, hi, body):
        def step(d, carry):
            body(d)
            return carry

        lax.fori_loop(lo, hi, step, 0)

    def when(cond, body):
        @pl.when(cond)
        def _():
            body()

    def start(copy):
        copy.start()

    def sent(copy):
        copy.wait_send()

    def peer(d):
        return lax.rem(x + d[0], 4) * 4 + lax.rem(y + d[1], 4)

    own_block = kern.at[0, 0, 0, 0]
    own_panel = pltpu.make_async_copy(kern.at[0, :, 0, 0], acol.at[:, k], loc.at[0])
    own_rows = pltpu.make_async_copy(kern.at[0, 0, 0], brow.at[lax.rem(r, 2), :, k], loc.at[1])
    own_lead = pltpu.make_async_copy(own_block, gbuf.at[0], loc.at[2])
    aide_piece = pltpu.make_async_copy(own_block.at[pl.ds(0, 16)], lead.at[0, 0], loc.at[2])
    helper_piece = pltpu.make_async_copy(own_block.at[pl.ds(16, 16)], lead.at[1, 1], loc.at[2])
    when(root, lambda: own_lead.start())
    when(aide, lambda: aide_piece.start())
    when(helper, lambda: helper_piece.start())
    when(top, lambda: own_panel.start())
    when(r < 2, lambda: own_rows.start())

    signal(r, sibling)

    def greet_panel():
        when(jnp.logical_or(parent != 0, r != 0), lambda: signal(r, 2 * parent))
        when(parent == 0, lambda: signal(r, one))

    when(runner, greet_panel)

    def greet_plane():
        for d in PLANE:
            signal(peer(d), c)
        when(inner, lambda: signal(r, one))
        when(relay_of != 0, lambda: signal(r, 2 * relay_of + 1))

    when(k == 1, greet_plane)

    def greet_mirror():
        for d in NEAR:
            signal(peer(d), hub_core(peer(d)))

    when(both(hub, top), greet_mirror)

    def greet_sources():
        signal(zero, zero)
        signal(zero, one)
        when(r != 1, lambda: signal(one, one))

    when(head, greet_sources)
    when(jnp.logical_or(root, aide), lambda: signal(one, one))

    def arrive():
        plane = jnp.where(k == 1, 15, 0) + jnp.where(both(hub, top), 4, 0)
        line = jnp.where(root, 0, jnp.where(top, 2, jnp.where(k == 0, children, 0)))
        down = jnp.where(c == 1, 15, 0)
        relays = jnp.where(jnp.logical_or(z == 4, z == 12), 4, jnp.where(z == 8, 2, 0))
        down = down + jnp.where(k == 1, relays, 0)
        more = jnp.where(root, 15, 0) + jnp.where(aide, 15, 0) + jnp.where(helper, 16, 0)
        pl.semaphore_wait(barrier, 1 + plane + line + down + more)
        when(top, lambda: own_panel.wait())
        when(r < 2, lambda: own_rows.wait())
        when(aide, lambda: aide_piece.wait())
        when(helper, lambda: helper_piece.wait())

    CHUNKS = tuple((i, quarter) for i in range(4) for quarter in range(4))

    def panel_copy(col, m, way):
        i, quarter = CHUNKS[m]
        chunk = acol.at[i, col, pl.ds(64 * quarter, 64)]
        n = 16 * col + m
        to = (r, 2 * skip_to) if way == 0 else (r, 2 * back_to) if way == 1 else (r, sibling)
        send = p_sib_send.at[n] if way == 2 else p_send.at[n, way]
        recv = p_sib_recv.at[n] if way == 2 else p_recv.at[n]
        return remote(chunk, chunk, send, recv, *to)

    def column_pair(col):
        return remote(acol.at[:, col], acol.at[:, col], p_sib_send.at[32], p_sib_recv.at[32], r, sibling)

    def panel_top(col, act):
        for m in range(16):
            act(panel_copy(col, m, 0))
            act(panel_copy(col, m, 1))

    def panel_line(t, act, arrive_first):
        col = jnp.where(r == 0, 1 - t, t)
        for m in range(16):
            if arrive_first:
                panel_copy(col, m, 0).wait_recv()
            when(has_skip, lambda m=m: act(panel_copy(col, m, 0)))
            when(has_back, lambda m=m: act(panel_copy(col, m, 1)))
            act(panel_copy(col, m, 2))

    def mirror_chunk(s, m):
        j, half = m // 4, m % 2
        return brow.at[s, j, (m // 2) % 2, pl.ds(128 * half, 128)]

    def mirror_copy(s, m, way, row):
        chunk = mirror_chunk(s, m)
        return remote(chunk, chunk, m_send.at[8 * s + m, way], m_recv.at[8 * s + m], row, 2 * z + hub_core(row))

    def mirror_pair(s, m):
        n = 8 * s + m
        return remote(mirror_chunk(s, m), mirror_chunk(s, m), m_sib_send.at[n], m_sib_recv.at[n], r, sibling)

    def mirror_feed(j, half):
        n = 8 * r + 4 * j + 2 * k + half
        chunk = brow.at[r, j, k, pl.ds(128 * half, 128)]
        return remote(chunk, chunk, m_sib_send.at[n], m_recv.at[n], r, sibling)

    def mirror_each(s, m, act):
        j, kc = m // 4, (m // 2) % 2
        rel = lax.rem(y + 4 - s, 4)
        ring_up = jnp.logical_or(rel == 0, both(s == 1, rel == 1))
        ring_down = jnp.logical_or(rel == 0, both(s == 0, rel == 3))
        line_up = jnp.logical_or(x == 0, both(s == 0, x == 1))
        line_down = jnp.logical_or(x == 0, both(s == 1, x == 3))
        if j == 0:
            ring_up, ring_down = both(ring_up, x == 0), both(ring_down, x == 0)
        else:
            line_up, line_down = both(line_up, rel == 0), both(line_down, rel == 0)
        when(ring_up, lambda: act(mirror_copy(s, m, 0, peer((0, 1)))))
        when(ring_down, lambda: act(mirror_copy(s, m, 1, peer((0, 3)))))
        when(line_up, lambda: act(mirror_copy(s, m, 2, peer((1, 0)))))
        when(line_down, lambda: act(mirror_copy(s, m, 3, peer((3, 0)))))
        when(both(kc != k, r != s), lambda: act(mirror_pair(s, m)))

    def mirror_half(t):
        nearer = jnp.where(jnp.logical_or(y == 0, y == 3), 0, 1)
        s = jnp.where(nearer == t, 0, 1)
        for m in range(8):
            when(jnp.logical_or(r != s, k != (m // 2) % 2), lambda m=m: mirror_copy(s, m, 0, r).wait_recv())
            mirror_each(s, m, start)

    def mirror_sent(s):
        for m in range(8):
            mirror_each(s, m, sent)

    def feeds(act):
        for j in range(2):
            for half in range(2):
                act(mirror_feed(j, half))

    def mirror_take():
        for s in range(2):

            def take(s=s):
                for kc in range(2):

                    def mine(kc=kc):
                        for j in range(2):
                            for half in range(2):
                                mirror_pair(s, 4 * j + 2 * kc + half).wait_recv()

                    when(k == kc, mine)

            when(r != s, take)

    def lead_from(n, p):
        rows = own_block.at[pl.ds(16 * p, 16)]
        return remote(rows, lead.at[p, n], gs_send.at[p], gh_recv.at[n], jnp.int32(p), one)

    def lead_scatter(n, act):
        for p in range(16):
            if p != n:
                act(lead_from(n, p))

    def view(which, p):
        if which < 2:
            return (lead, inv0)[which].at[p]
        return inv1.at[lax.div(p, 2)]

    def takes_part(which, row):
        return row >= 0 if which < 2 else lax.rem(row, 2) == 0

    def line_copy(which, d):
        piece = view(which, r)
        return remote(piece, piece, gd_send.at[which, d], gd_recv.at[which], r, jnp.int32(2 * d + 1))

    def down(which, act):
        def go():
            for d in FIRST:
                act(line_copy(which, d))

        when(takes_part(which, r), go)

    def relay(act, copy):
        for q, targets in RELAY.items():

            def go(targets=targets):
                for d in targets:
                    act(copy(d))

            when(z == q, go)

    def relay_piece(which, act):
        when(takes_part(which, r), lambda: relay(act, lambda d: line_copy(which, d)))

    def across(which, act):
        def go():
            for n, d in enumerate(PLANE):
                act(remote(view(which, r), view(which, r), ga_send.at[which, n], ga_recv.at[which, r], peer(d), c))

        when(takes_part(which, r), go)

    def piece_taken(which):
        copy = remote(view(which, r), view(which, r), gd_send.at[which, 0], gd_recv.at[which], r, sibling)
        when(takes_part(which, r), lambda: copy.wait_recv())

    def collect(which):
        def take(d):
            p = lax.rem(r + d, 16)
            copy = remote(view(which, p), view(which, p), ga_send.at[which, 0], ga_recv.at[which, p], r, sibling)
            when(takes_part(which, p), lambda: copy.wait_recv())

        loop(1, 16, take)

    def inverse_piece(p):
        return remote(inv_src.at[p], inv0.at[p], xr_send.at[0, p], xh_recv.at[0], jnp.int32(p), one)

    def next_piece(p):
        return remote(inv1_src.at[p // 2], inv1.at[p // 2], xr_send.at[1, p], xh_recv.at[1], jnp.int32(p), one)

    def inverse_first(n, p):
        return remote(x_src.at[n], xs.at[n], xr_send.at[2 + n, p], xh_recv.at[2 + n], jnp.int32(p), one)

    def from_root(act, copy, step=1):
        for d in PLANE:
            p = 4 * d[0] + d[1]
            if p % step == 0:
                act(copy(p))
        act(copy(0))

    def inverse_copy(n, d):
        return remote(xs.at[n], xs.at[n], xd_send.at[n, d], xd_recv.at[n], r, jnp.int32(2 * d + 1))

    def inverse_down(n, act):
        for d in FIRST if n == 0 else LINE:
            act(inverse_copy(n, d))

    def inverse_relay(n, act):
        if n == 0:
            relay(act, lambda d: inverse_copy(n, d))

    def inverse_taken(n):
        remote(xs.at[n], xs.at[n], xd_send.at[n, 0], xd_recv.at[n], r, sibling).wait_recv()

    def parts_pair(n):
        block = parts.at[0] if n == 0 else parts.at[pl.ds(1, 2)]
        return remote(block, block, parts_send.at[n], parts_recv.at[n], r, sibling)

    def lead_copy(n):
        return remote(own_block, gbuf.at[n + 1], lead_send.at[n], lead_recv.at[n], zero, zero)

    def root_main():
        own_lead.wait()
        g[0:64, :] = jnp.zeros((64, 512), jnp.float32)
        g[320:384, :] = jnp.zeros((64, 512), jnp.float32)
        g[64:320, 0:256] = gbuf[0].astype(jnp.float32)
        set_identity(g)

        def bulk():
            arrive()
            column_pair(0).start()
            feeds(start)

        def second_half():
            for p in range(16):
                inv_src[p] = g[64 + 16 * p : 80 + 16 * p, 256:512]
            from_root(start, inverse_piece)
            lead_copy(0).wait_recv()
            lead_copy(1).wait_recv()
            side = dot32(g[64:320, 256:512], gbuf[1].astype(jnp.float32), ((1,), (0,)))
            g[64:320, 0:256] = gbuf[2].astype(jnp.float32) - dot32(side, side, ((0,), (0,)))
            set_identity(g)

        def phase(it):
            def store(n, packed):
                if n < 2:
                    for part in range(4):
                        inv1_src[4 * n + part] = packed[8 * part : 8 * part + 8]
                    if n == 1:
                        when(it == 1, lambda: from_root(start, next_piece, 2))
                else:
                    x_src[n - 2] = packed
                    when(it == 1, lambda: from_root(start, lambda p: inverse_first(n - 2, p)))

            factor_phase(g, store, lambda: when(it == 0, bulk))
            when(it == 0, second_half)

        loop(0, 2, phase)

    when(root, root_main)
    when(neither(root), arrive)

    def top_sends():
        when(aide, lambda: lead_copy(0).start())
        when(helper, lambda: lead_copy(1).start())
        panel_top(k, start)
        column_pair(k).start()
        when(aide, lambda: lead_scatter(0, start))
        when(helper, lambda: lead_scatter(1, start))

    when(both(top, neither(root)), top_sends)
    when(both(both(mate, r < 2), neither(root)), lambda: feeds(start))

    def top_spread(which):
        down(which, start)
        across(which, start)

    def head_inverses(p):
        when(takes_part(2, r), lambda: next_piece(p).wait_recv())
        top_spread(2)
        for n in range(2):
            inverse_first(n, p).wait_recv()
            inverse_down(n, start)

    def aide_main():
        column_pair(0).wait_recv()
        panel_top(0, start)
        loop(0, 1, mirror_half)
        lead_from(1, 0).wait_recv()
        top_spread(0)
        inverse_piece(0).wait_recv()
        top_spread(1)
        loop(1, 2, mirror_half)
        head_inverses(0)

    when(aide, aide_main)
    when(both(hub, neither(aide)), lambda: loop(0, 2, mirror_half))

    def head_main():
        lead_from(0, 1).wait_recv()
        when(neither(helper), lambda: lead_from(1, 2).wait_recv())
        top_spread(0)
        inverse_piece(1).wait_recv()
        top_spread(1)
        head_inverses(2)

    when(head, head_main)

    def line_spread():
        for which in range(3):
            piece_taken(which)
            relay_piece(which, start)
            across(which, start)

    when(both(k == 1, inner), line_spread)
    when(runner, lambda: loop(0, 2, lambda t: panel_line(t, start, True)))

    def put(block, lo, hi, values):
        high = values.astype(jnp.bfloat16)
        parts[block, 0, lo:hi] = high
        parts[block, 1, lo:hi] = (values - high.astype(jnp.float32)).astype(jnp.bfloat16)

    def assemble():
        def block(n):
            return jnp.concatenate([lead[p, n] for p in range(16)], axis=0).astype(jnp.float32)

        collect(0)
        collect(1)
        first_inverse = jnp.concatenate([inv0[p] for p in range(16)], axis=0)
        put(0, 0, 256, first_inverse)
        parts_pair(0).start()
        side = dot32(first_inverse, block(0), ((1,), (0,)))
        work[:, 0:256] = block(1) - dot32(side, side, ((0,), (0,)))
        work[:, 256:512] = -dot32(side, first_inverse, ((0,), (0,)))
        rows = lax.broadcasted_iota(jnp.int32, (256, 256), 0)
        cols = lax.broadcasted_iota(jnp.int32, (256, 256), 1)
        work[:, 512:768] = jnp.where(rows == cols, 1.0, 0.0)
        collect(2)
        for n in range(4):
            if n < 2:
                packed = jnp.concatenate([inv1[4 * n + p] for p in range(4)], axis=0)
            else:

                def arrived(n=n - 2):
                    inverse_taken(n)
                    inverse_relay(n, start)

                when(inner, arrived)
                packed = xs[n - 2]
            inverse = jnp.concatenate([packed[:, 64:128], packed[:, 0:64]], axis=0)
            lo, hi = 64 * n, 64 * n + 64
            lines = dot32(inverse, work[lo:hi, :], ((1,), (0,)))
            put(1, lo, hi, lines[:, 256:512])
            put(2, lo, hi, lines[:, 512:768])
            if n < 3:
                work[hi:256, :] = work[hi:256, :] - dot32(lines[:, hi:256], lines, ((0,), (0,)))
        parts_pair(1).start()

    when(k == 1, assemble)

    def parts_take():
        parts_pair(0).wait_recv()
        parts_pair(1).wait_recv()

    when(k == 0, parts_take)
    when(mate, mirror_take)

    def column_taken(col):
        for m in range(16):
            panel_copy(col, m, 2).wait_recv()

    when(both(k == 1, inner), lambda: loop(0, 2, column_taken))
    when(both(top, neither(aide)), lambda: column_pair(1 - k).wait_recv())

    when(runner, lambda: loop(0, 2, lambda t: panel_line(t, sent, False)))

    def top_drain():
        column_pair(k).wait_send()
        when(neither(root), lambda: panel_top(k, sent))
        when(aide, lambda: panel_top(0, sent))

    when(top, top_drain)
    when(both(mate, r < 2), lambda: feeds(sent))

    when(hub, lambda: loop(0, 2, mirror_sent))

    def core1_drain():
        for which in range(3):
            across(which, sent)
        for n in range(2):
            parts_pair(n).wait_send()

    when(k == 1, core1_drain)

    def line_drain():
        for which in range(3):
            down(which, sent)
        for n in range(2):
            inverse_down(n, sent)

    when(c == 1, line_drain)

    def relay_drain():
        for which in range(3):
            relay_piece(which, sent)
        inverse_relay(0, sent)

    when(both(k == 1, inner), relay_drain)

    def aide_drain():
        lead_copy(0).wait_send()
        lead_scatter(0, sent)

    when(aide, aide_drain)

    def helper_drain():
        lead_copy(1).wait_send()
        lead_scatter(1, sent)

    when(helper, helper_drain)

    def root_drain():
        from_root(sent, inverse_piece)
        from_root(sent, next_piece, 2)
        for n in range(2):
            from_root(sent, lambda p, n=n: inverse_first(n, p))

    when(root, root_drain)


def gather(kernel):
    bf16, f32 = jnp.bfloat16, jnp.float32
    dma = pltpu.SemaphoreType.DMA
    return pl.pallas_call(
        gather_kernel,
        out_shape=(
            jax.ShapeDtypeStruct((4, 2, 256, 256), bf16),
            jax.ShapeDtypeStruct((2, 2, 2, 256, 256), bf16),
            jax.ShapeDtypeStruct((3, 2, 256, 256), bf16),
        ),
        in_specs=[pl.BlockSpec(memory_space=pltpu.HBM)],
        out_specs=(
            pl.BlockSpec(memory_space=pl.ANY),
            pl.BlockSpec(memory_space=pl.ANY),
            pl.BlockSpec(memory_space=pltpu.VMEM),
        ),
        scratch_shapes=[
            pltpu.VMEM((16, 2, 16, 256), bf16),
            pltpu.VMEM((16, 16, 256), f32),
            pltpu.VMEM((8, 8, 128), f32),
            pltpu.VMEM((2, 32, 128), f32),
            pltpu.VMEM((3, 256, 256), bf16),
            pltpu.VMEM((384, 512), f32),
            pltpu.VMEM((2, 32, 128), f32),
            pltpu.VMEM((16, 16, 256), f32),
            pltpu.VMEM((8, 8, 128), f32),
            pltpu.VMEM((256, 768), f32),
            dma((32, 2)), dma((32,)), dma((33,)), dma((33,)),
            dma((16, 4)), dma((16,)), dma((16,)), dma((16,)),
            dma((2,)), dma((2,)),
            dma((16,)), dma((2,)), dma((3, 16)), dma((3,)), dma((3, 16)), dma((3, 16)), dma((2,)), dma((2,)),
            dma((4, 16)), dma((4,)), dma((2, 16)), dma((2,)), dma((3,)),
        ],
        compiler_params=pltpu.CompilerParams(
            collective_id=0, has_side_effects=True, vmem_limit_bytes=24 * 1024 * 1024
        ),
        name="gather_and_factor",
    )(kernel)


def update_kernel(kern, acol, brow, parts, panels, schur, old, pan, new, sems):
    r = lax.axis_index("row")
    c = lax.axis_index("col")
    k = lax.rem(c, 2)
    load = pltpu.make_async_copy(kern.at[0, :, 0], old, sems.at[0])
    load.start()
    f32 = jnp.float32
    tri = lax.broadcasted_iota(jnp.int32, (256, 256), 0) >= lax.broadcasted_iota(jnp.int32, (256, 256), 1)
    stores = []

    def store(src, dst):
        stores.append(pltpu.make_async_copy(src, dst, sems.at[1 + len(stores)]))
        stores[-1].start()

    def rows(a, b):
        return lax.dot_general(a, b, (((1,), (1,)), ((), ())), preferred_element_type=f32)

    lefts = []
    for h in range(2):
        a, b = (jnp.concatenate([acol[2 * h, s], acol[2 * h + 1, s]], axis=0) for s in range(2))
        first = rows(a, parts[0, 0]) + rows(a, parts[0, 1])
        second = rows(a, parts[1, 0]) + rows(a, parts[1, 1]) + rows(b, parts[2, 0]) + rows(b, parts[2, 1])
        lefts.append(jnp.concatenate([first.astype(jnp.bfloat16), second.astype(jnp.bfloat16)], axis=1))
        for e in range(2):
            i = 2 * h + e
            for n, solved in enumerate((first, second)):
                part = solved[256 * e : 256 * e + 256]
                if i == 0:
                    whole = jnp.logical_or(r > n, jnp.logical_and(r == n, tri))
                    part = jnp.where(whole, part, 0.0)
                pan[i, n] = part
            store(pan.at[i], panels.at[0, i])
    columns = []
    for j in range(2):
        a, b = brow[0, j, k], brow[1, j, k]
        upper = jnp.dot(parts[0, 0], a, preferred_element_type=f32) + jnp.dot(
            parts[0, 1], a, preferred_element_type=f32
        )
        lower = jnp.dot(parts[1, 0], a, preferred_element_type=f32) + jnp.dot(
            parts[1, 1], a, preferred_element_type=f32
        )
        lower = lower + jnp.dot(parts[2, 0], b, preferred_element_type=f32)
        lower = lower + jnp.dot(parts[2, 1], b, preferred_element_type=f32)
        columns.append(jnp.concatenate([upper, lower], axis=0).astype(jnp.bfloat16))
    mirror = jnp.concatenate(columns, axis=1)
    load.wait()
    for h in range(2):
        change = jnp.dot(lefts[h], mirror, preferred_element_type=f32)
        for e in range(2):
            i = 2 * h + e
            for j in range(2):
                out = old[i, j].astype(f32) - change[256 * e : 256 * e + 256, 256 * j : 256 * j + 256]
                if i == 0:
                    out = jnp.where(r >= 2, out, 0.0)
                if j == 0:
                    out = jnp.where(c >= 2, out, 0.0)
                new[i, j] = out.astype(jnp.bfloat16)
            store(new.at[i], schur.at[0, i, 0])
    for copy in stores:
        copy.wait()


def update(kernel, *gathered):
    hbm = pl.BlockSpec(memory_space=pltpu.HBM)
    return pl.pallas_call(
        update_kernel,
        out_shape=(
            jax.ShapeDtypeStruct((1, 4, 2, 256, 256), jnp.float32),
            jax.ShapeDtypeStruct((1, 4, 1, 2, 256, 256), jnp.bfloat16),
        ),
        in_specs=[hbm] + [pl.BlockSpec(memory_space=pltpu.VMEM)] * 3,
        out_specs=(hbm, hbm),
        scratch_shapes=[
            pltpu.VMEM((4, 2, 256, 256), jnp.bfloat16),
            pltpu.VMEM((4, 2, 256, 256), jnp.float32),
            pltpu.VMEM((4, 2, 256, 256), jnp.bfloat16),
            pltpu.SemaphoreType.DMA((9,)),
        ],
        compiler_params=pltpu.CompilerParams(vmem_limit_bytes=32 * 1024 * 1024),
        name="solve_and_update",
    )(kernel, *gathered)


def per_device(kernel):
    kernel = pltpu.with_memory_space_constraint(kernel, pltpu.HBM)
    return update(kernel, *gather(kernel))


def solution(mesh):
    in_specs = (P("row", None, "col", None, None, None),)
    out_specs = (P("row", None, None, None, None), P("row", None, "col", None, None, None))
    return jax.shard_map(per_device, mesh=mesh, in_specs=in_specs, out_specs=out_specs, check_vma=False)
```

```python
import functools

import jax
import jax.numpy as jnp
from jax import lax
from jax.experimental import pallas as pl
from jax.experimental.pallas import tpu as pltpu
from jax.sharding import PartitionSpec as P

MESH = pl.DeviceIdType.MESH
HI = lax.Precision.HIGHEST
PLANE = sorted(((a, b) for a in range(4) for b in range(4) if a or b), key=lambda d: -min(d[0], 4 - d[0]) - min(d[1], 4 - d[1]))
NEAR = ((0, 1), (0, 3), (1, 0), (3, 0))
LINE = sorted(range(1, 16), key=lambda d: -min(d, 16 - d))
GROUPS = ((0, 2), (2, 3), (3, 4))
SKIP = {0: 3, 3: 6, 6: 8, 13: 10, 10: 9}
BACK = {0: 13, 3: 2, 2: 1, 6: 5, 5: 4, 8: 7, 13: 14, 14: 15, 10: 11, 11: 12}


def lookup(key, pairs):
    value = jnp.int32(0)
    for k, v in pairs.items():
        value = jnp.where(key == k, jnp.int32(v), value)
    return value


def member(key, keys):
    hit = key == keys[0]
    for k in keys[1:]:
        hit = jnp.logical_or(hit, key == k)
    return hit


def dot32(a, b, dims):
    return lax.dot_general(a, b, (dims, ((), ())), precision=HI, preferred_element_type=jnp.float32)


def row(v, i):
    return jnp.broadcast_to(v[i : i + 1, :], (8, 128))

def lane(v, i):
    return jnp.broadcast_to(v[:, i : i + 1], (8, 128))


def eliminate(strips, off):
    row_iota = lax.broadcasted_iota(jnp.int32, (8, 128), 0)
    strips = list(strips)
    diag = [lane(strips[0], off + i) for i in range(8)]
    pivots = []
    for s in range(8):
        later = range(s + 1, 8)
        cols = {t: [lane(strips[t], off + 8 * s + i) for i in range(8)] for t in later}
        if s < 7:
            raw = [lane(strips[s + 1], off + 8 * (s + 1) + i) for i in range(8)]
        head = strips[s]
        pivot = jnp.zeros((8, 128), jnp.float32)
        recips = []
        for i in range(8):
            own = diag[i]
            recip = 1.0 / row(own, i)
            recips.append(recip)
            pivot = jnp.where(row_iota == i, own, pivot)
            for j in range(i + 1, 8):
                line = row(own, j)
                diag[j] = diag[j] - (own * line) * recip
                factor = line * recip
                for t in later:
                    cols[t][j] = cols[t][j] - cols[t][i] * factor
            head = head - jnp.where(row_iota > i, own * recip, 0.0) * row(head, i)
        strips[s] = head
        pivots.append(pivot)
        if s < 7:
            near = cols[s + 1]
            scaled = [near[i] * recips[i] for i in range(8)]
            diag = []
            for j in range(8):
                terms = [scaled[i] * row(near[i], j) for i in range(8)]
                while len(terms) > 1:
                    terms = [terms[a] + terms[a + 1] for a in range(0, len(terms), 2)]
                diag.append(raw[j] - terms[0])
        heads = [row(head, i) * recips[i] for i in range(8)]
        for t in later:
            terms = [cols[t][i] * heads[i] for i in range(8)]
            while len(terms) > 1:
                terms = [terms[a] + terms[a + 1] for a in range(0, len(terms), 2)]
            strips[t] = strips[t] - terms[0]
    return strips, pivots


def factor_phase(g, store, middle):
    col_iota = lax.broadcasted_iota(jnp.int32, (8, 128), 1)
    row_iota = lax.broadcasted_iota(jnp.int32, (8, 128), 0)
    for b in range(4):
        odd = b % 2
        lo = 64 + 64 * b
        win = 128 * (b // 2)
        off = 64 * odd
        strips = []
        tile = g[lo:lo+64, win:win+128]
        for s in range(8):
            if odd:
                unit = jnp.where(col_iota == row_iota + 8 * s, 1.0, 0.0)
                strips.append(jnp.where(col_iota >= 64, tile[8*s:8*s+8], unit))
            else:
                unit = jnp.where(col_iota == row_iota + 8 * s + 64, 1.0, 0.0)
                strips.append(jnp.where(col_iota < 64, tile[8*s:8*s+8], unit))
        strips, pivots = eliminate(strips, off)
        keep = (col_iota < 64) if odd else (col_iota >= 64)
        wide = jnp.concatenate([jnp.where(keep, a * lax.rsqrt(p), 0.0) for a, p in zip(strips, pivots)], axis=0)
        turned = pltpu.roll(wide, 64, 1)
        low = wide if odd else turned
        high = turned if odd else wide
        if b == 1:
            middle()
        store(b, jnp.where(lax.broadcasted_iota(jnp.int32,(32,128),1) < 64, low[32:], high[:32]))
        base = lo if odd else lo - 64
        if b < 3:
            nwin = 128 * ((b + 1) // 2)
            u = dot32(wide, g[base:base+128, nwin:nwin+128], ((1,), (0,)))
            nxt = lo + 64
            noff = 64 * (1 - odd)
            if odd:
                g[nxt:nxt+64, nwin:nwin+128] = g[nxt:nxt+64, nwin:nwin+128] - dot32(u[:, 0:64], u, ((0,), (0,)))
            else:
                g[nxt:nxt+64, nwin:nwin+128] = g[nxt:nxt+64, nwin:nwin+128] - dot32(u, u, ((0,), (0,)))[64:128]
        lines = dot32(wide, g[base : base + 128, :], ((1,), (0,)))
        g[lo:lo+64, :] = lines
        if b < 3:
            first = 64 * (b + 1)
            change = dot32(lines[:, 0:256], lines, ((0,), (0,)))
            nxt = lo + 64
            nwin = 128 * ((b + 1) // 2)
            for lo_c, hi_c in ((0, nwin), (nwin + 128, 512)):
                if hi_c > lo_c:
                    g[nxt:nxt+64, lo_c:hi_c] = g[nxt:nxt+64, lo_c:hi_c] - change[first:first+64, lo_c:hi_c]
            if b < 2:
                g[nxt+64:320, :] = g[nxt+64:320, :] - change[first+64:256, :]


def set_identity(g):
    rows = lax.broadcasted_iota(jnp.int32, (256, 256), 0)
    cols = lax.broadcasted_iota(jnp.int32, (256, 256), 1)
    g[64:320, 256:512] = jnp.where(rows == cols, 1.0, 0.0)


def gather_kernel(
    kern, acol, brow, parts,
    lead, inv0, xs, gbuf, g, x_src, inv_src, work,
    p_send, p_recv, p_sib_send, p_sib_recv, m_send, m_recv, m_sib_send, m_sib_recv,
    lead_send, lead_recv, gs_send, gh_recv, gd_send, gd_recv, ga_send, ga_recv, parts_send, parts_recv,
    xr_send, xh_recv, xd_send, xd_recv, loc,
):
    r = lax.axis_index("row")
    c = lax.axis_index("col")
    x, y = lax.div(r, 4), lax.rem(r, 4)
    z, k = lax.div(c, 2), lax.rem(c, 2)
    zero, one = jnp.int32(0), jnp.int32(1)
    sibling = c + 1 - 2 * k
    both, neither = jnp.logical_and, jnp.logical_not
    top = z == 0
    inner = neither(top)

    def hub_core(row):
        return jnp.where(both(top, row != 0), 0, 1)

    hub = k == hub_core(r)
    mate = neither(hub)
    root = both(r == 0, c == 0)
    aide = both(r == 0, c == 1)
    helper = both(r == 1, c == 1)
    head = both(c == 1, r != 0)
    runner = both(k == 0, inner)
    skip_to = lookup(z, SKIP)
    back_to = lookup(z, BACK)
    has_skip = member(z, list(SKIP))
    has_back = member(z, list(BACK))
    parent = lookup(z, {v: q for q, v in list(SKIP.items()) + list(BACK.items())})
    children = has_skip.astype(jnp.int32) + has_back.astype(jnp.int32)
    barrier = pltpu.get_barrier_semaphore()

    def remote(src, dst, send, recv, row, col):
        return pltpu.make_async_remote_copy(
            src_ref=src, dst_ref=dst, send_sem=send, recv_sem=recv, device_id=(row, col), device_id_type=MESH
        )

    def signal(row, col):
        pl.semaphore_signal(barrier, inc=1, device_id=(row, col), device_id_type=MESH)

    def loop(lo, hi, body):
        def step(d, carry):
            body(d)
            return carry

        lax.fori_loop(lo, hi, step, 0)

    def when(cond, body):
        @pl.when(cond)
        def _():
            body()

    def start(copy):
        copy.start()

    def sent(copy):
        copy.wait_send()

    def peer(d):
        return lax.rem(x + d[0], 4) * 4 + lax.rem(y + d[1], 4)

    own_block = kern.at[0, 0, 0, 0]
    own_panel = pltpu.make_async_copy(kern.at[0, :, 0, 0], acol.at[:, k], loc.at[0])
    own_rows = pltpu.make_async_copy(kern.at[0, 0, 0], brow.at[lax.rem(r, 2), :, k], loc.at[1])
    own_lead = pltpu.make_async_copy(own_block, gbuf.at[0], loc.at[2])
    aide_piece = pltpu.make_async_copy(own_block.at[pl.ds(0, 16)], lead.at[0, 0], loc.at[2])
    helper_piece = pltpu.make_async_copy(own_block.at[pl.ds(16, 16)], lead.at[1, 1], loc.at[2])
    when(root, lambda: own_lead.start())
    when(aide, lambda: aide_piece.start())
    when(helper, lambda: helper_piece.start())
    when(top, lambda: own_panel.start())
    when(r < 2, lambda: own_rows.start())

    signal(r, sibling)

    def greet_panel():
        when(jnp.logical_or(parent != 0, r != 0), lambda: signal(r, 2 * parent))
        when(parent == 0, lambda: signal(r, one))

    when(runner, greet_panel)

    def greet_plane():
        for d in PLANE:
            signal(peer(d), c)
        when(inner, lambda: signal(r, one))

    when(k == 1, greet_plane)

    def greet_mirror():
        for d in NEAR:
            signal(peer(d), hub_core(peer(d)))

    when(both(hub, top), greet_mirror)

    def greet_sources():
        signal(zero, zero)
        signal(zero, one)
        when(r != 1, lambda: signal(one, one))

    when(head, greet_sources)
    when(jnp.logical_or(root, aide), lambda: signal(one, one))

    def arrive():
        plane = jnp.where(k == 1, 15, 0) + jnp.where(both(hub, top), 4, 0)
        line = jnp.where(root, 0, jnp.where(top, 2, jnp.where(k == 0, children, 0)))
        down = jnp.where(c == 1, 15, 0)
        more = jnp.where(root, 15, 0) + jnp.where(aide, 15, 0) + jnp.where(helper, 16, 0)
        pl.semaphore_wait(barrier, 1 + plane + line + down + more)
        when(top, lambda: own_panel.wait())
        when(r < 2, lambda: own_rows.wait())
        when(aide, lambda: aide_piece.wait())
        when(helper, lambda: helper_piece.wait())

    CHUNKS = tuple((i, quarter) for i in range(4) for quarter in range(4))

    def panel_copy(col, m, way):
        i, quarter = CHUNKS[m]
        chunk = acol.at[i, col, pl.ds(64 * quarter, 64)]
        n = 16 * col + m
        to = (r, 2 * skip_to) if way == 0 else (r, 2 * back_to) if way == 1 else (r, sibling)
        send = p_sib_send.at[n] if way == 2 else p_send.at[n, way]
        recv = p_sib_recv.at[n] if way == 2 else p_recv.at[n]
        return remote(chunk, chunk, send, recv, *to)

    def column_pair(col):
        return remote(acol.at[:, col], acol.at[:, col], p_sib_send.at[32], p_sib_recv.at[32], r, sibling)

    def panel_top(col, act):
        for m in range(16):
            act(panel_copy(col, m, 0))
            act(panel_copy(col, m, 1))

    def panel_line(t, act, arrive_first):
        col = jnp.where(r == 0, 1 - t, t)
        for m in range(16):
            if arrive_first:
                panel_copy(col, m, 0).wait_recv()
            when(has_skip, lambda m=m: act(panel_copy(col, m, 0)))
            when(has_back, lambda m=m: act(panel_copy(col, m, 1)))
            act(panel_copy(col, m, 2))

    def mirror_chunk(s, m):
        j, half = m // 4, m % 2
        return brow.at[s, j, (m // 2) % 2, pl.ds(128 * half, 128)]

    def mirror_copy(s, m, way, row):
        chunk = mirror_chunk(s, m)
        return remote(chunk, chunk, m_send.at[8 * s + m, way], m_recv.at[8 * s + m], row, 2 * z + hub_core(row))

    def mirror_pair(s, m):
        n = 8 * s + m
        return remote(mirror_chunk(s, m), mirror_chunk(s, m), m_sib_send.at[n], m_sib_recv.at[n], r, sibling)

    def mirror_feed(j, half):
        n = 8 * r + 4 * j + 2 * k + half
        chunk = brow.at[r, j, k, pl.ds(128 * half, 128)]
        return remote(chunk, chunk, m_sib_send.at[n], m_recv.at[n], r, sibling)

    def mirror_each(s, m, act):
        j, kc = m // 4, (m // 2) % 2
        rel = lax.rem(y + 4 - s, 4)
        ring_up = jnp.logical_or(rel == 0, both(s == 1, rel == 1))
        ring_down = jnp.logical_or(rel == 0, both(s == 0, rel == 3))
        line_up = jnp.logical_or(x == 0, both(s == 0, x == 1))
        line_down = jnp.logical_or(x == 0, both(s == 1, x == 3))
        if j == 0:
            ring_up, ring_down = both(ring_up, x == 0), both(ring_down, x == 0)
        else:
            line_up, line_down = both(line_up, rel == 0), both(line_down, rel == 0)
        when(ring_up, lambda: act(mirror_copy(s, m, 0, peer((0, 1)))))
        when(ring_down, lambda: act(mirror_copy(s, m, 1, peer((0, 3)))))
        when(line_up, lambda: act(mirror_copy(s, m, 2, peer((1, 0)))))
        when(line_down, lambda: act(mirror_copy(s, m, 3, peer((3, 0)))))
        when(both(kc != k, r != s), lambda: act(mirror_pair(s, m)))

    def mirror_half(t):
        nearer = jnp.where(jnp.logical_or(y == 0, y == 3), 0, 1)
        s = jnp.where(nearer == t, 0, 1)
        for m in range(8):
            when(jnp.logical_or(r != s, k != (m // 2) % 2), lambda m=m: mirror_copy(s, m, 0, r).wait_recv())
            mirror_each(s, m, start)

    def mirror_sent(s):
        for m in range(8):
            mirror_each(s, m, sent)

    def feeds(act):
        for j in range(2):
            for half in range(2):
                act(mirror_feed(j, half))

    def mirror_take():
        for s in range(2):

            def take(s=s):
                for kc in range(2):

                    def mine(kc=kc):
                        for j in range(2):
                            for half in range(2):
                                mirror_pair(s, 4 * j + 2 * kc + half).wait_recv()

                    when(k == kc, mine)

            when(r != s, take)

    def lead_from(n, p):
        rows = own_block.at[pl.ds(16 * p, 16)]
        return remote(rows, lead.at[p, n], gs_send.at[p], gh_recv.at[n], jnp.int32(p), one)

    def lead_scatter(n, act):
        for p in range(16):
            if p != n:
                act(lead_from(n, p))

    def view(which, p):
        return (lead, inv0)[which].at[p]

    def down(which, act):
        piece = view(which, r)
        for d in LINE:
            act(remote(piece, piece, gd_send.at[which, d], gd_recv.at[which], r, jnp.int32(2 * d + 1)))

    def across(which, act):
        piece = view(which, r)
        for n, d in enumerate(PLANE):
            act(remote(piece, piece, ga_send.at[which, n], ga_recv.at[which, r], peer(d), c))

    def piece_taken(which):
        piece = view(which, r)
        remote(piece, piece, gd_send.at[which, 0], gd_recv.at[which], r, sibling).wait_recv()

    def collect(which):
        def take(d):
            p = lax.rem(r + d, 16)
            piece = view(which, p)
            remote(piece, piece, ga_send.at[which, 0], ga_recv.at[which, p], r, sibling).wait_recv()

        loop(1, 16, take)

    def inverse_piece(p):
        return remote(inv_src.at[p], inv0.at[p], xr_send.at[0, p], xh_recv.at[0], jnp.int32(p), one)

    def group(buf, n):
        lo, hi = GROUPS[n]
        return buf.at[pl.ds(lo, hi - lo)]

    def inverse_first(n, p):
        return remote(group(x_src, n), group(xs, n), xr_send.at[1 + n, p], xh_recv.at[1 + n], jnp.int32(p), one)

    def from_root(act, copy):
        for d in PLANE:
            act(copy(4 * d[0] + d[1]))
        act(copy(0))

    def inverse_down(n, act):
        for d in LINE:
            act(remote(group(xs, n), group(xs, n), xd_send.at[n, d], xd_recv.at[n], r, jnp.int32(2 * d + 1)))

    def inverse_taken(n):
        remote(group(xs, n), group(xs, n), xd_send.at[n, 0], xd_recv.at[n], r, sibling).wait_recv()

    def parts_pair(n):
        block = parts.at[0] if n == 0 else parts.at[pl.ds(1, 2), :, pl.ds(64 * (n - 1), 64)]
        return remote(block, block, parts_send.at[n], parts_recv.at[n], r, sibling)

    def lead_copy(n):
        return remote(own_block, gbuf.at[n + 1], lead_send.at[n], lead_recv.at[n], zero, zero)

    def root_main():
        own_lead.wait()
        g[0:64, :] = jnp.zeros((64, 512), jnp.float32)
        g[320:384, :] = jnp.zeros((64, 512), jnp.float32)
        g[64:320, 0:256] = gbuf[0].astype(jnp.float32)
        set_identity(g)

        def bulk():
            arrive()
            column_pair(0).start()
            feeds(start)

        def second_half():
            for p in range(16):
                inv_src[p] = g[64 + 16 * p : 80 + 16 * p, 256:512]
            from_root(start, inverse_piece)
            lead_copy(0).wait_recv()
            lead_copy(1).wait_recv()
            side = dot32(g[64:320, 256:512], gbuf[1].astype(jnp.float32), ((1,), (0,)))
            g[64:320, 0:256] = gbuf[2].astype(jnp.float32) - dot32(side, side, ((0,), (0,)))
            set_identity(g)

        def phase(it):
            def store(n, packed):
                x_src[n] = packed
                for which, (lo, hi) in enumerate(GROUPS):
                    if hi == n + 1:
                        when(it == 1, lambda which=which: from_root(start, lambda p: inverse_first(which, p)))

            factor_phase(g, store, lambda: when(it == 0, bulk))
            when(it == 0, second_half)

        loop(0, 2, phase)

    when(root, root_main)
    when(neither(root), arrive)

    def top_sends():
        when(aide, lambda: lead_copy(0).start())
        when(helper, lambda: lead_copy(1).start())
        panel_top(k, start)
        column_pair(k).start()
        when(aide, lambda: lead_scatter(0, start))
        when(helper, lambda: lead_scatter(1, start))

    when(both(top, neither(root)), top_sends)
    when(both(both(mate, r < 2), neither(root)), lambda: feeds(start))

    def top_spread(which):
        down(which, start)
        across(which, start)

    def head_inverses(p):
        for n in range(3):
            inverse_first(n, p).wait_recv()
            inverse_down(n, start)

    def aide_main():
        column_pair(0).wait_recv()
        panel_top(0, start)
        loop(0, 1, mirror_half)
        lead_from(1, 0).wait_recv()
        top_spread(0)
        inverse_piece(0).wait_recv()
        top_spread(1)
        head_inverses(0)
        loop(1, 2, mirror_half)

    when(aide, aide_main)
    when(both(hub, neither(aide)), lambda: loop(0, 2, mirror_half))

    def head_main():
        lead_from(0, 1).wait_recv()
        when(neither(helper), lambda: lead_from(1, 2).wait_recv())
        top_spread(0)
        inverse_piece(1).wait_recv()
        top_spread(1)
        head_inverses(2)

    when(head, head_main)

    def line_spread():
        for which in range(2):
            piece_taken(which)
            across(which, start)

    when(both(k == 1, inner), line_spread)
    when(runner, lambda: loop(0, 2, lambda t: panel_line(t, start, True)))

    def put(block, lo, hi, values):
        high = values.astype(jnp.bfloat16)
        parts[block, 0, lo:hi] = high
        parts[block, 1, lo:hi] = (values - high.astype(jnp.float32)).astype(jnp.bfloat16)

    def assemble():
        def block(n):
            return jnp.concatenate([lead[p, n] for p in range(16)], axis=0).astype(jnp.float32)

        collect(0)
        collect(1)
        first_inverse = jnp.concatenate([inv0[p] for p in range(16)], axis=0)
        put(0, 0, 256, first_inverse)
        parts_pair(0).start()
        side = dot32(first_inverse, block(0), ((1,), (0,)))
        work[:, 0:256] = block(1) - dot32(side, side, ((0,), (0,)))
        work[:, 256:512] = -dot32(side, first_inverse, ((0,), (0,)))
        rows = lax.broadcasted_iota(jnp.int32, (256, 256), 0)
        cols = lax.broadcasted_iota(jnp.int32, (256, 256), 1)
        work[:, 512:768] = jnp.where(rows == cols, 1.0, 0.0)
        take = {lo: n for n, (lo, hi) in enumerate(GROUPS)}
        for n in range(4):
            if n in take:
                when(inner, lambda n=n: inverse_taken(take[n]))
            packed = xs[n]
            inverse = jnp.concatenate([packed[:, 64:128], packed[:, 0:64]], axis=0)
            lo, hi = 64 * n, 64 * n + 64
            lines = dot32(inverse, work[lo:hi, :], ((1,), (0,)))
            put(1, lo, hi, lines[:, 256:512])
            put(2, lo, hi, lines[:, 512:768])
            parts_pair(1 + n).start()
            if n < 3:
                work[hi:256, :] = work[hi:256, :] - dot32(lines[:, hi:256], lines, ((0,), (0,)))

    when(k == 1, assemble)

    def parts_take():
        for n in range(5):
            parts_pair(n).wait_recv()

    when(k == 0, parts_take)
    when(mate, mirror_take)

    def column_taken(col):
        for m in range(16):
            panel_copy(col, m, 2).wait_recv()

    when(both(k == 1, inner), lambda: loop(0, 2, column_taken))
    when(both(top, neither(aide)), lambda: column_pair(1 - k).wait_recv())

    when(runner, lambda: loop(0, 2, lambda t: panel_line(t, sent, False)))

    def top_drain():
        column_pair(k).wait_send()
        when(neither(root), lambda: panel_top(k, sent))
        when(aide, lambda: panel_top(0, sent))

    when(top, top_drain)
    when(both(mate, r < 2), lambda: feeds(sent))

    when(hub, lambda: loop(0, 2, mirror_sent))

    def core1_drain():
        for which in range(2):
            across(which, sent)
        for n in range(5):
            parts_pair(n).wait_send()

    when(k == 1, core1_drain)

    def line_drain():
        for which in range(2):
            down(which, sent)
        for n in range(3):
            inverse_down(n, sent)

    when(c == 1, line_drain)

    def aide_drain():
        lead_copy(0).wait_send()
        lead_scatter(0, sent)

    when(aide, aide_drain)

    def helper_drain():
        lead_copy(1).wait_send()
        lead_scatter(1, sent)

    when(helper, helper_drain)

    def root_drain():
        from_root(sent, inverse_piece)
        for n in range(3):
            from_root(sent, lambda p, n=n: inverse_first(n, p))

    when(root, root_drain)


def gather(kernel):
    bf16, f32 = jnp.bfloat16, jnp.float32
    dma = pltpu.SemaphoreType.DMA
    return pl.pallas_call(
        gather_kernel,
        out_shape=(
            jax.ShapeDtypeStruct((4, 2, 256, 256), bf16),
            jax.ShapeDtypeStruct((2, 2, 2, 256, 256), bf16),
            jax.ShapeDtypeStruct((3, 2, 256, 256), bf16),
        ),
        in_specs=[pl.BlockSpec(memory_space=pltpu.HBM)],
        out_specs=(
            pl.BlockSpec(memory_space=pl.ANY),
            pl.BlockSpec(memory_space=pl.ANY),
            pl.BlockSpec(memory_space=pltpu.VMEM),
        ),
        scratch_shapes=[
            pltpu.VMEM((16, 2, 16, 256), bf16),
            pltpu.VMEM((16, 16, 256), f32),
            pltpu.VMEM((4, 32, 128), f32),
            pltpu.VMEM((3, 256, 256), bf16),
            pltpu.VMEM((384, 512), f32),
            pltpu.VMEM((4, 32, 128), f32),
            pltpu.VMEM((16, 16, 256), f32),
            pltpu.VMEM((256, 768), f32),
            dma((32, 2)), dma((32,)), dma((33,)), dma((33,)),
            dma((16, 4)), dma((16,)), dma((16,)), dma((16,)),
            dma((2,)), dma((2,)),
            dma((16,)), dma((2,)), dma((2, 16)), dma((2,)), dma((2, 16)), dma((2, 16)), dma((5,)), dma((5,)),
            dma((4, 16)), dma((4,)), dma((3, 16)), dma((3,)), dma((3,)),
        ],
        compiler_params=pltpu.CompilerParams(
            collective_id=0, has_side_effects=True, vmem_limit_bytes=24 * 1024 * 1024
        ),
        name="gather_and_factor",
    )(kernel)


def update_kernel(kern, acol, brow, parts, panels, schur, old, pan, new, sems):
    r = lax.axis_index("row")
    c = lax.axis_index("col")
    k = lax.rem(c, 2)
    load = pltpu.make_async_copy(kern.at[0, :, 0], old, sems.at[0])
    load.start()
    f32 = jnp.float32
    tri = lax.broadcasted_iota(jnp.int32, (256, 256), 0) >= lax.broadcasted_iota(jnp.int32, (256, 256), 1)
    stores = []

    def store(src, dst):
        stores.append(pltpu.make_async_copy(src, dst, sems.at[1 + len(stores)]))
        stores[-1].start()

    def rows(a, b):
        return lax.dot_general(a, b, (((1,), (1,)), ((), ())), preferred_element_type=f32)

    lefts = []
    for h in range(2):
        a, b = (jnp.concatenate([acol[2 * h, s], acol[2 * h + 1, s]], axis=0) for s in range(2))
        first = rows(a, parts[0, 0]) + rows(a, parts[0, 1])
        second = rows(a, parts[1, 0]) + rows(a, parts[1, 1]) + rows(b, parts[2, 0]) + rows(b, parts[2, 1])
        lefts.append(jnp.concatenate([first.astype(jnp.bfloat16), second.astype(jnp.bfloat16)], axis=1))
        for e in range(2):
            i = 2 * h + e
            for n, solved in enumerate((first, second)):
                part = solved[256 * e : 256 * e + 256]
                if i == 0:
                    whole = jnp.logical_or(r > n, jnp.logical_and(r == n, tri))
                    part = jnp.where(whole, part, 0.0)
                pan[i, n] = part
            store(pan.at[i], panels.at[0, i])
    columns = []
    for j in range(2):
        a, b = brow[0, j, k], brow[1, j, k]
        upper = jnp.dot(parts[0, 0], a, preferred_element_type=f32) + jnp.dot(
            parts[0, 1], a, preferred_element_type=f32
        )
        lower = jnp.dot(parts[1, 0], a, preferred_element_type=f32) + jnp.dot(
            parts[1, 1], a, preferred_element_type=f32
        )
        lower = lower + jnp.dot(parts[2, 0], b, preferred_element_type=f32)
        lower = lower + jnp.dot(parts[2, 1], b, preferred_element_type=f32)
        columns.append(jnp.concatenate([upper, lower], axis=0).astype(jnp.bfloat16))
    mirror = jnp.concatenate(columns, axis=1)
    load.wait()
    for h in range(2):
        change = jnp.dot(lefts[h], mirror, preferred_element_type=f32)
        for e in range(2):
            i = 2 * h + e
            for j in range(2):
                out = old[i, j].astype(f32) - change[256 * e : 256 * e + 256, 256 * j : 256 * j + 256]
                if i == 0:
                    out = jnp.where(r >= 2, out, 0.0)
                if j == 0:
                    out = jnp.where(c >= 2, out, 0.0)
                new[i, j] = out.astype(jnp.bfloat16)
            store(new.at[i], schur.at[0, i, 0])
    for copy in stores:
        copy.wait()


def update(kernel, *gathered):
    hbm = pl.BlockSpec(memory_space=pltpu.HBM)
    return pl.pallas_call(
        update_kernel,
        out_shape=(
            jax.ShapeDtypeStruct((1, 4, 2, 256, 256), jnp.float32),
            jax.ShapeDtypeStruct((1, 4, 1, 2, 256, 256), jnp.bfloat16),
        ),
        in_specs=[hbm] + [pl.BlockSpec(memory_space=pltpu.VMEM)] * 3,
        out_specs=(hbm, hbm),
        scratch_shapes=[
            pltpu.VMEM((4, 2, 256, 256), jnp.bfloat16),
            pltpu.VMEM((4, 2, 256, 256), jnp.float32),
            pltpu.VMEM((4, 2, 256, 256), jnp.bfloat16),
            pltpu.SemaphoreType.DMA((9,)),
        ],
        compiler_params=pltpu.CompilerParams(vmem_limit_bytes=32 * 1024 * 1024),
        name="solve_and_update",
    )(kernel, *gathered)


def per_device(kernel):
    kernel = pltpu.with_memory_space_constraint(kernel, pltpu.HBM)
    return update(kernel, *gather(kernel))


def solution(mesh):
    in_specs = (P("row", None, "col", None, None, None),)
    out_specs = (P("row", None, None, None, None), P("row", None, "col", None, None, None))
    return jax.shard_map(per_device, mesh=mesh, in_specs=in_specs, out_specs=out_specs, check_vma=False)
```

```python
import functools

import jax
import jax.numpy as jnp
from jax import lax
from jax.experimental import pallas as pl
from jax.experimental.pallas import tpu as pltpu
from jax.sharding import PartitionSpec as P

MESH = pl.DeviceIdType.MESH
HI = lax.Precision.HIGHEST
PLANE = sorted(((a, b) for a in range(4) for b in range(4) if a or b), key=lambda d: -min(d[0], 4 - d[0]) - min(d[1], 4 - d[1]))
NEAR = ((0, 1), (0, 3), (1, 0), (3, 0))
LINE = sorted(range(1, 16), key=lambda d: -min(d, 16 - d))
SKIP = {0: 3, 3: 6, 6: 7, 7: 8, 13: 10, 10: 9}
BACK = {0: 13, 3: 2, 2: 1, 6: 5, 5: 4, 13: 14, 14: 15, 10: 11, 11: 12}


def lookup(key, pairs):
    value = jnp.int32(0)
    for k, v in pairs.items():
        value = jnp.where(key == k, jnp.int32(v), value)
    return value


def member(key, keys):
    hit = key == keys[0]
    for k in keys[1:]:
        hit = jnp.logical_or(hit, key == k)
    return hit


def dot32(a, b, dims):
    return lax.dot_general(a, b, (dims, ((), ())), precision=HI, preferred_element_type=jnp.float32)


def row(v, i):
    return jnp.broadcast_to(v[i : i + 1, :], (8, 128))

def lane(v, i):
    return jnp.broadcast_to(v[:, i : i + 1], (8, 128))


def eliminate(strips, off):
    row_iota = lax.broadcasted_iota(jnp.int32, (8, 128), 0)
    strips = list(strips)
    diag = [lane(strips[0], off + i) for i in range(8)]
    pivots = []
    for s in range(8):
        later = range(s + 1, 8)
        cols = {t: [lane(strips[t], off + 8 * s + i) for i in range(8)] for t in later}
        if s < 7:
            raw = [lane(strips[s + 1], off + 8 * (s + 1) + i) for i in range(8)]
        head = strips[s]
        pivot = jnp.zeros((8, 128), jnp.float32)
        recips = []
        for i in range(8):
            own = diag[i]
            recip = 1.0 / row(own, i)
            recips.append(recip)
            pivot = jnp.where(row_iota == i, own, pivot)
            for j in range(i + 1, 8):
                line = row(own, j)
                diag[j] = diag[j] - (own * line) * recip
                factor = line * recip
                for t in later:
                    cols[t][j] = cols[t][j] - cols[t][i] * factor
            head = head - jnp.where(row_iota > i, own * recip, 0.0) * row(head, i)
        strips[s] = head
        pivots.append(pivot)
        if s < 7:
            near = cols[s + 1]
            scaled = [near[i] * recips[i] for i in range(8)]
            diag = []
            for j in range(8):
                terms = [scaled[i] * row(near[i], j) for i in range(8)]
                while len(terms) > 1:
                    terms = [terms[a] + terms[a + 1] for a in range(0, len(terms), 2)]
                diag.append(raw[j] - terms[0])
        heads = [row(head, i) * recips[i] for i in range(8)]
        for t in later:
            terms = [cols[t][i] * heads[i] for i in range(8)]
            while len(terms) > 1:
                terms = [terms[a] + terms[a + 1] for a in range(0, len(terms), 2)]
            strips[t] = strips[t] - terms[0]
    return strips, pivots


def factor_phase(g, store, middle):
    col_iota = lax.broadcasted_iota(jnp.int32, (8, 128), 1)
    row_iota = lax.broadcasted_iota(jnp.int32, (8, 128), 0)
    for b in range(4):
        odd = b % 2
        lo = 64 + 64 * b
        win = 128 * (b // 2)
        off = 64 * odd
        strips = []
        tile = g[lo:lo+64, win:win+128]
        for s in range(8):
            if odd:
                unit = jnp.where(col_iota == row_iota + 8 * s, 1.0, 0.0)
                strips.append(jnp.where(col_iota >= 64, tile[8*s:8*s+8], unit))
            else:
                unit = jnp.where(col_iota == row_iota + 8 * s + 64, 1.0, 0.0)
                strips.append(jnp.where(col_iota < 64, tile[8*s:8*s+8], unit))
        strips, pivots = eliminate(strips, off)
        keep = (col_iota < 64) if odd else (col_iota >= 64)
        wide = jnp.concatenate([jnp.where(keep, a * lax.rsqrt(p), 0.0) for a, p in zip(strips, pivots)], axis=0)
        turned = pltpu.roll(wide, 64, 1)
        low = wide if odd else turned
        high = turned if odd else wide
        if b == 1:
            middle()
        store(b, jnp.where(lax.broadcasted_iota(jnp.int32,(32,128),1) < 64, low[32:], high[:32]))
        base = lo if odd else lo - 64
        if b < 3:
            nwin = 128 * ((b + 1) // 2)
            u = dot32(wide, g[base:base+128, nwin:nwin+128], ((1,), (0,)))
            nxt = lo + 64
            noff = 64 * (1 - odd)
            if odd:
                g[nxt:nxt+64, nwin:nwin+128] = g[nxt:nxt+64, nwin:nwin+128] - dot32(u[:, 0:64], u, ((0,), (0,)))
            else:
                g[nxt:nxt+64, nwin:nwin+128] = g[nxt:nxt+64, nwin:nwin+128] - dot32(u, u, ((0,), (0,)))[64:128]
        lines = dot32(wide, g[base : base + 128, :], ((1,), (0,)))
        g[lo:lo+64, :] = lines
        if b < 3:
            first = 64 * (b + 1)
            change = dot32(lines[:, 0:256], lines, ((0,), (0,)))
            nxt = lo + 64
            nwin = 128 * ((b + 1) // 2)
            for lo_c, hi_c in ((0, nwin), (nwin + 128, 512)):
                if hi_c > lo_c:
                    g[nxt:nxt+64, lo_c:hi_c] = g[nxt:nxt+64, lo_c:hi_c] - change[first:first+64, lo_c:hi_c]
            if b < 2:
                g[nxt+64:320, :] = g[nxt+64:320, :] - change[first+64:256, :]


def set_identity(g):
    rows = lax.broadcasted_iota(jnp.int32, (256, 256), 0)
    cols = lax.broadcasted_iota(jnp.int32, (256, 256), 1)
    g[64:320, 256:512] = jnp.where(rows == cols, 1.0, 0.0)


def gather_kernel(
    kern, acol, brow, parts,
    lead, inv0, inv1, xs, gbuf, g, x_src, inv_src, inv1_src, work,
    p_send, p_recv, p_sib_send, p_sib_recv, m_send, m_recv, m_sib_send, m_sib_recv,
    lead_send, lead_recv, gs_send, gh_recv, gd_send, gd_recv, ga_send, ga_recv, parts_send, parts_recv,
    xr_send, xh_recv, xd_send, xd_recv, loc,
):
    r = lax.axis_index("row")
    c = lax.axis_index("col")
    x, y = lax.div(r, 4), lax.rem(r, 4)
    z, k = lax.div(c, 2), lax.rem(c, 2)
    zero, one = jnp.int32(0), jnp.int32(1)
    sibling = c + 1 - 2 * k
    both, neither = jnp.logical_and, jnp.logical_not
    top = z == 0
    inner = neither(top)

    def hub_core(row):
        return jnp.where(both(top, row != 0), 0, 1)

    hub = k == hub_core(r)
    mate = neither(hub)
    root = both(r == 0, c == 0)
    aide = both(r == 0, c == 1)
    helper = both(r == 1, c == 1)
    head = both(c == 1, r != 0)
    runner = both(k == 0, inner)
    skip_to = lookup(z, SKIP)
    back_to = lookup(z, BACK)
    has_skip = member(z, list(SKIP))
    has_back = member(z, list(BACK))
    parent = lookup(z, {v: q for q, v in list(SKIP.items()) + list(BACK.items())})
    children = has_skip.astype(jnp.int32) + has_back.astype(jnp.int32)
    barrier = pltpu.get_barrier_semaphore()

    def remote(src, dst, send, recv, row, col):
        return pltpu.make_async_remote_copy(
            src_ref=src, dst_ref=dst, send_sem=send, recv_sem=recv, device_id=(row, col), device_id_type=MESH
        )

    def signal(row, col):
        pl.semaphore_signal(barrier, inc=1, device_id=(row, col), device_id_type=MESH)

    def loop(lo, hi, body):
        def step(d, carry):
            body(d)
            return carry

        lax.fori_loop(lo, hi, step, 0)

    def when(cond, body):
        @pl.when(cond)
        def _():
            body()

    def start(copy):
        copy.start()

    def sent(copy):
        copy.wait_send()

    def peer(d):
        return lax.rem(x + d[0], 4) * 4 + lax.rem(y + d[1], 4)

    own_block = kern.at[0, 0, 0, 0]
    own_panel = pltpu.make_async_copy(kern.at[0, :, 0, 0], acol.at[:, k], loc.at[0])
    own_rows = pltpu.make_async_copy(kern.at[0, 0, 0], brow.at[lax.rem(r, 2), :, k], loc.at[1])
    own_lead = pltpu.make_async_copy(own_block, gbuf.at[0], loc.at[2])
    aide_piece = pltpu.make_async_copy(own_block.at[pl.ds(0, 16)], lead.at[0, 0], loc.at[2])
    helper_piece = pltpu.make_async_copy(own_block.at[pl.ds(16, 16)], lead.at[1, 1], loc.at[2])
    when(root, lambda: own_lead.start())
    when(aide, lambda: aide_piece.start())
    when(helper, lambda: helper_piece.start())
    when(top, lambda: own_panel.start())
    when(r < 2, lambda: own_rows.start())

    signal(r, sibling)

    def greet_panel():
        when(jnp.logical_or(parent != 0, r != 0), lambda: signal(r, 2 * parent))
        when(parent == 0, lambda: signal(r, one))

    when(runner, greet_panel)

    def greet_plane():
        for d in PLANE:
            signal(peer(d), c)
        when(inner, lambda: signal(r, one))

    when(k == 1, greet_plane)

    def greet_mirror():
        for d in NEAR:
            signal(peer(d), hub_core(peer(d)))

    when(both(hub, top), greet_mirror)

    def greet_sources():
        signal(zero, zero)
        signal(zero, one)
        when(r != 1, lambda: signal(one, one))

    when(head, greet_sources)
    when(jnp.logical_or(root, aide), lambda: signal(one, one))

    def arrive():
        plane = jnp.where(k == 1, 15, 0) + jnp.where(both(hub, top), 4, 0)
        line = jnp.where(root, 0, jnp.where(top, 2, jnp.where(k == 0, children, 0)))
        down = jnp.where(c == 1, 15, 0)
        more = jnp.where(root, 15, 0) + jnp.where(aide, 15, 0) + jnp.where(helper, 16, 0)
        pl.semaphore_wait(barrier, 1 + plane + line + down + more)
        when(top, lambda: own_panel.wait())
        when(r < 2, lambda: own_rows.wait())
        when(aide, lambda: aide_piece.wait())
        when(helper, lambda: helper_piece.wait())

    CHUNKS = tuple((i, quarter) for i in range(4) for quarter in range(4))

    def panel_copy(col, m, way):
        i, quarter = CHUNKS[m]
        chunk = acol.at[i, col, pl.ds(64 * quarter, 64)]
        n = 16 * col + m
        to = (r, 2 * skip_to) if way == 0 else (r, 2 * back_to) if way == 1 else (r, sibling)
        send = p_sib_send.at[n] if way == 2 else p_send.at[n, way]
        recv = p_sib_recv.at[n] if way == 2 else p_recv.at[n]
        return remote(chunk, chunk, send, recv, *to)

    def column_pair(col):
        return remote(acol.at[:, col], acol.at[:, col], p_sib_send.at[32], p_sib_recv.at[32], r, sibling)

    def panel_top(col, act):
        for m in range(16):
            act(panel_copy(col, m, 0))
            act(panel_copy(col, m, 1))

    def panel_line(t, act, arrive_first):
        col = jnp.where(r == 0, 1 - t, t)
        for m in range(16):
            if arrive_first:
                panel_copy(col, m, 0).wait_recv()
            when(has_skip, lambda m=m: act(panel_copy(col, m, 0)))
            when(has_back, lambda m=m: act(panel_copy(col, m, 1)))
            act(panel_copy(col, m, 2))

    def mirror_chunk(s, m):
        j, half = m // 4, m % 2
        return brow.at[s, j, (m // 2) % 2, pl.ds(128 * half, 128)]

    def mirror_copy(s, m, way, row):
        chunk = mirror_chunk(s, m)
        return remote(chunk, chunk, m_send.at[8 * s + m, way], m_recv.at[8 * s + m], row, 2 * z + hub_core(row))

    def mirror_pair(s, m):
        n = 8 * s + m
        return remote(mirror_chunk(s, m), mirror_chunk(s, m), m_sib_send.at[n], m_sib_recv.at[n], r, sibling)

    def mirror_feed(j, half):
        n = 8 * r + 4 * j + 2 * k + half
        chunk = brow.at[r, j, k, pl.ds(128 * half, 128)]
        return remote(chunk, chunk, m_sib_send.at[n], m_recv.at[n], r, sibling)

    def mirror_each(s, m, act):
        j, kc = m // 4, (m // 2) % 2
        rel = lax.rem(y + 4 - s, 4)
        ring_up = jnp.logical_or(rel == 0, both(s == 1, rel == 1))
        ring_down = jnp.logical_or(rel == 0, both(s == 0, rel == 3))
        line_up = jnp.logical_or(x == 0, both(s == 0, x == 1))
        line_down = jnp.logical_or(x == 0, both(s == 1, x == 3))
        if j == 0:
            ring_up, ring_down = both(ring_up, x == 0), both(ring_down, x == 0)
        else:
            line_up, line_down = both(line_up, rel == 0), both(line_down, rel == 0)
        when(ring_up, lambda: act(mirror_copy(s, m, 0, peer((0, 1)))))
        when(ring_down, lambda: act(mirror_copy(s, m, 1, peer((0, 3)))))
        when(line_up, lambda: act(mirror_copy(s, m, 2, peer((1, 0)))))
        when(line_down, lambda: act(mirror_copy(s, m, 3, peer((3, 0)))))
        when(both(kc != k, r != s), lambda: act(mirror_pair(s, m)))

    def mirror_half(t):
        nearer = jnp.where(jnp.logical_or(y == 0, y == 3), 0, 1)
        s = jnp.where(nearer == t, 0, 1)
        for m in range(8):
            when(jnp.logical_or(r != s, k != (m // 2) % 2), lambda m=m: mirror_copy(s, m, 0, r).wait_recv())
            mirror_each(s, m, start)

    def mirror_sent(s):
        for m in range(8):
            mirror_each(s, m, sent)

    def feeds(act):
        for j in range(2):
            for half in range(2):
                act(mirror_feed(j, half))

    def mirror_take():
        for s in range(2):

            def take(s=s):
                for kc in range(2):

                    def mine(kc=kc):
                        for j in range(2):
                            for half in range(2):
                                mirror_pair(s, 4 * j + 2 * kc + half).wait_recv()

                    when(k == kc, mine)

            when(r != s, take)

    def lead_from(n, p):
        rows = own_block.at[pl.ds(16 * p, 16)]
        return remote(rows, lead.at[p, n], gs_send.at[p], gh_recv.at[n], jnp.int32(p), one)

    def lead_scatter(n, act):
        for p in range(16):
            if p != n:
                act(lead_from(n, p))

    def view(which, p):
        if which < 2:
            return (lead, inv0)[which].at[p]
        return inv1.at[lax.div(p, 2)]

    def takes_part(which, row):
        return row >= 0 if which < 2 else lax.rem(row, 2) == 0

    def down(which, act):
        piece = view(which, r)

        def go():
            for d in LINE:
                act(remote(piece, piece, gd_send.at[which, d], gd_recv.at[which], r, jnp.int32(2 * d + 1)))

        when(takes_part(which, r), go)

    def across(which, act):
        piece = view(which, r)

        def go():
            for n, d in enumerate(PLANE):
                act(remote(piece, piece, ga_send.at[which, n], ga_recv.at[which, r], peer(d), c))

        when(takes_part(which, r), go)

    def piece_taken(which):
        piece = view(which, r)
        copy = remote(piece, piece, gd_send.at[which, 0], gd_recv.at[which], r, sibling)
        when(takes_part(which, r), lambda: copy.wait_recv())

    def collect(which):
        def take(d):
            p = lax.rem(r + d, 16)
            piece = view(which, p)
            copy = remote(piece, piece, ga_send.at[which, 0], ga_recv.at[which, p], r, sibling)
            when(takes_part(which, p), lambda: copy.wait_recv())

        loop(1, 16, take)

    def inverse_piece(p):
        return remote(inv_src.at[p], inv0.at[p], xr_send.at[0, p], xh_recv.at[0], jnp.int32(p), one)

    def next_piece(p):
        return remote(inv1_src.at[p // 2], inv1.at[p // 2], xr_send.at[1, p], xh_recv.at[1], jnp.int32(p), one)

    def inverse_first(n, p):
        return remote(x_src.at[n], xs.at[n], xr_send.at[2 + n, p], xh_recv.at[2 + n], jnp.int32(p), one)

    def from_root(act, copy, step=1):
        for d in PLANE:
            p = 4 * d[0] + d[1]
            if p % step == 0:
                act(copy(p))
        act(copy(0))

    def inverse_down(n, act):
        for d in LINE:
            act(remote(xs.at[n], xs.at[n], xd_send.at[n, d], xd_recv.at[n], r, jnp.int32(2 * d + 1)))

    def inverse_taken(n):
        remote(xs.at[n], xs.at[n], xd_send.at[n, 0], xd_recv.at[n], r, sibling).wait_recv()

    def parts_pair(n):
        block = parts.at[0] if n == 0 else parts.at[pl.ds(1, 2), :, pl.ds(64 * (n - 1), 64)]
        return remote(block, block, parts_send.at[n], parts_recv.at[n], r, sibling)

    def lead_copy(n):
        return remote(own_block, gbuf.at[n + 1], lead_send.at[n], lead_recv.at[n], zero, zero)

    def root_main():
        own_lead.wait()
        g[0:64, :] = jnp.zeros((64, 512), jnp.float32)
        g[320:384, :] = jnp.zeros((64, 512), jnp.float32)
        g[64:320, 0:256] = gbuf[0].astype(jnp.float32)
        set_identity(g)

        def bulk():
            arrive()
            column_pair(0).start()
            feeds(start)

        def second_half():
            for p in range(16):
                inv_src[p] = g[64 + 16 * p : 80 + 16 * p, 256:512]
            from_root(start, inverse_piece)
            lead_copy(0).wait_recv()
            lead_copy(1).wait_recv()
            side = dot32(g[64:320, 256:512], gbuf[1].astype(jnp.float32), ((1,), (0,)))
            g[64:320, 0:256] = gbuf[2].astype(jnp.float32) - dot32(side, side, ((0,), (0,)))
            set_identity(g)

        def phase(it):
            def store(n, packed):
                if n < 2:
                    for part in range(4):
                        inv1_src[4 * n + part] = packed[8 * part : 8 * part + 8]
                    if n == 1:
                        when(it == 1, lambda: from_root(start, next_piece, 2))
                else:
                    x_src[n - 2] = packed
                    when(it == 1, lambda: from_root(start, lambda p: inverse_first(n - 2, p)))

            factor_phase(g, store, lambda: when(it == 0, bulk))
            when(it == 0, second_half)

        loop(0, 2, phase)

    when(root, root_main)
    when(neither(root), arrive)

    def top_sends():
        when(aide, lambda: lead_copy(0).start())
        when(helper, lambda: lead_copy(1).start())
        panel_top(k, start)
        column_pair(k).start()
        when(aide, lambda: lead_scatter(0, start))
        when(helper, lambda: lead_scatter(1, start))

    when(both(top, neither(root)), top_sends)
    when(both(both(mate, r < 2), neither(root)), lambda: feeds(start))

    def top_spread(which):
        down(which, start)
        across(which, start)

    def head_inverses(p):
        when(takes_part(2, r), lambda: next_piece(p).wait_recv())
        top_spread(2)
        for n in range(2):
            inverse_first(n, p).wait_recv()
            inverse_down(n, start)

    def aide_main():
        column_pair(0).wait_recv()
        panel_top(0, start)
        loop(0, 1, mirror_half)
        lead_from(1, 0).wait_recv()
        top_spread(0)
        inverse_piece(0).wait_recv()
        top_spread(1)
        head_inverses(0)
        loop(1, 2, mirror_half)

    when(aide, aide_main)
    when(both(hub, neither(aide)), lambda: loop(0, 2, mirror_half))

    def head_main():
        lead_from(0, 1).wait_recv()
        when(neither(helper), lambda: lead_from(1, 2).wait_recv())
        top_spread(0)
        inverse_piece(1).wait_recv()
        top_spread(1)
        head_inverses(2)

    when(head, head_main)

    def line_spread():
        for which in range(3):
            piece_taken(which)
            across(which, start)

    when(both(k == 1, inner), line_spread)
    when(runner, lambda: loop(0, 2, lambda t: panel_line(t, start, True)))

    def put(block, lo, hi, values):
        high = values.astype(jnp.bfloat16)
        parts[block, 0, lo:hi] = high
        parts[block, 1, lo:hi] = (values - high.astype(jnp.float32)).astype(jnp.bfloat16)

    def assemble():
        def block(n):
            return jnp.concatenate([lead[p, n] for p in range(16)], axis=0).astype(jnp.float32)

        collect(0)
        collect(1)
        first_inverse = jnp.concatenate([inv0[p] for p in range(16)], axis=0)
        put(0, 0, 256, first_inverse)
        parts_pair(0).start()
        side = dot32(first_inverse, block(0), ((1,), (0,)))
        work[:, 0:256] = block(1) - dot32(side, side, ((0,), (0,)))
        work[:, 256:512] = -dot32(side, first_inverse, ((0,), (0,)))
        rows = lax.broadcasted_iota(jnp.int32, (256, 256), 0)
        cols = lax.broadcasted_iota(jnp.int32, (256, 256), 1)
        work[:, 512:768] = jnp.where(rows == cols, 1.0, 0.0)
        collect(2)
        for n in range(4):
            if n < 2:
                packed = jnp.concatenate([inv1[4 * n + p] for p in range(4)], axis=0)
            else:
                when(inner, lambda n=n: inverse_taken(n - 2))
                packed = xs[n - 2]
            inverse = jnp.concatenate([packed[:, 64:128], packed[:, 0:64]], axis=0)
            lo, hi = 64 * n, 64 * n + 64
            lines = dot32(inverse, work[lo:hi, :], ((1,), (0,)))
            put(1, lo, hi, lines[:, 256:512])
            put(2, lo, hi, lines[:, 512:768])
            parts_pair(1 + n).start()
            if n < 3:
                work[hi:256, :] = work[hi:256, :] - dot32(lines[:, hi:256], lines, ((0,), (0,)))

    when(k == 1, assemble)

    def parts_take():
        for n in range(5):
            parts_pair(n).wait_recv()

    when(k == 0, parts_take)
    when(mate, mirror_take)

    def column_taken(col):
        for m in range(16):
            panel_copy(col, m, 2).wait_recv()

    when(both(k == 1, inner), lambda: loop(0, 2, column_taken))
    when(both(top, neither(aide)), lambda: column_pair(1 - k).wait_recv())

    when(runner, lambda: loop(0, 2, lambda t: panel_line(t, sent, False)))

    def top_drain():
        column_pair(k).wait_send()
        when(neither(root), lambda: panel_top(k, sent))
        when(aide, lambda: panel_top(0, sent))

    when(top, top_drain)
    when(both(mate, r < 2), lambda: feeds(sent))

    when(hub, lambda: loop(0, 2, mirror_sent))

    def core1_drain():
        for which in range(3):
            across(which, sent)
        for n in range(5):
            parts_pair(n).wait_send()

    when(k == 1, core1_drain)

    def line_drain():
        for which in range(3):
            down(which, sent)
        for n in range(2):
            inverse_down(n, sent)

    when(c == 1, line_drain)

    def aide_drain():
        lead_copy(0).wait_send()
        lead_scatter(0, sent)

    when(aide, aide_drain)

    def helper_drain():
        lead_copy(1).wait_send()
        lead_scatter(1, sent)

    when(helper, helper_drain)

    def root_drain():
        from_root(sent, inverse_piece)
        from_root(sent, next_piece, 2)
        for n in range(2):
            from_root(sent, lambda p, n=n: inverse_first(n, p))

    when(root, root_drain)


def gather(kernel):
    bf16, f32 = jnp.bfloat16, jnp.float32
    dma = pltpu.SemaphoreType.DMA
    return pl.pallas_call(
        gather_kernel,
        out_shape=(
            jax.ShapeDtypeStruct((4, 2, 256, 256), bf16),
            jax.ShapeDtypeStruct((2, 2, 2, 256, 256), bf16),
            jax.ShapeDtypeStruct((3, 2, 256, 256), bf16),
        ),
        in_specs=[pl.BlockSpec(memory_space=pltpu.HBM)],
        out_specs=(
            pl.BlockSpec(memory_space=pl.ANY),
            pl.BlockSpec(memory_space=pl.ANY),
            pl.BlockSpec(memory_space=pltpu.VMEM),
        ),
        scratch_shapes=[
            pltpu.VMEM((16, 2, 16, 256), bf16),
            pltpu.VMEM((16, 16, 256), f32),
            pltpu.VMEM((8, 8, 128), f32),
            pltpu.VMEM((2, 32, 128), f32),
            pltpu.VMEM((3, 256, 256), bf16),
            pltpu.VMEM((384, 512), f32),
            pltpu.VMEM((2, 32, 128), f32),
            pltpu.VMEM((16, 16, 256), f32),
            pltpu.VMEM((8, 8, 128), f32),
            pltpu.VMEM((256, 768), f32),
            dma((32, 2)), dma((32,)), dma((33,)), dma((33,)),
            dma((16, 4)), dma((16,)), dma((16,)), dma((16,)),
            dma((2,)), dma((2,)),
            dma((16,)), dma((2,)), dma((3, 16)), dma((3,)), dma((3, 16)), dma((3, 16)), dma((5,)), dma((5,)),
            dma((4, 16)), dma((4,)), dma((2, 16)), dma((2,)), dma((3,)),
        ],
        compiler_params=pltpu.CompilerParams(
            collective_id=0, has_side_effects=True, vmem_limit_bytes=24 * 1024 * 1024
        ),
        name="gather_and_factor",
    )(kernel)


def update_kernel(kern, acol, brow, parts, panels, schur, old, pan, new, sems):
    r = lax.axis_index("row")
    c = lax.axis_index("col")
    k = lax.rem(c, 2)
    load = pltpu.make_async_copy(kern.at[0, :, 0], old, sems.at[0])
    load.start()
    f32 = jnp.float32
    tri = lax.broadcasted_iota(jnp.int32, (256, 256), 0) >= lax.broadcasted_iota(jnp.int32, (256, 256), 1)
    stores = []

    def store(src, dst):
        stores.append(pltpu.make_async_copy(src, dst, sems.at[1 + len(stores)]))
        stores[-1].start()

    def rows(a, b):
        return lax.dot_general(a, b, (((1,), (1,)), ((), ())), preferred_element_type=f32)

    lefts = []
    for h in range(2):
        a, b = (jnp.concatenate([acol[2 * h, s], acol[2 * h + 1, s]], axis=0) for s in range(2))
        first = rows(a, parts[0, 0]) + rows(a, parts[0, 1])
        second = rows(a, parts[1, 0]) + rows(a, parts[1, 1]) + rows(b, parts[2, 0]) + rows(b, parts[2, 1])
        lefts.append(jnp.concatenate([first.astype(jnp.bfloat16), second.astype(jnp.bfloat16)], axis=1))
        for e in range(2):
            i = 2 * h + e
            for n, solved in enumerate((first, second)):
                part = solved[256 * e : 256 * e + 256]
                if i == 0:
                    whole = jnp.logical_or(r > n, jnp.logical_and(r == n, tri))
                    part = jnp.where(whole, part, 0.0)
                pan[i, n] = part
            store(pan.at[i], panels.at[0, i])
    columns = []
    for j in range(2):
        a, b = brow[0, j, k], brow[1, j, k]
        upper = jnp.dot(parts[0, 0], a, preferred_element_type=f32) + jnp.dot(
            parts[0, 1], a, preferred_element_type=f32
        )
        lower = jnp.dot(parts[1, 0], a, preferred_element_type=f32) + jnp.dot(
            parts[1, 1], a, preferred_element_type=f32
        )
        lower = lower + jnp.dot(parts[2, 0], b, preferred_element_type=f32)
        lower = lower + jnp.dot(parts[2, 1], b, preferred_element_type=f32)
        columns.append(jnp.concatenate([upper, lower], axis=0).astype(jnp.bfloat16))
    mirror = jnp.concatenate(columns, axis=1)
    load.wait()
    for h in range(2):
        change = jnp.dot(lefts[h], mirror, preferred_element_type=f32)
        for e in range(2):
            i = 2 * h + e
            for j in range(2):
                out = old[i, j].astype(f32) - change[256 * e : 256 * e + 256, 256 * j : 256 * j + 256]
                if i == 0:
                    out = jnp.where(r >= 2, out, 0.0)
                if j == 0:
                    out = jnp.where(c >= 2, out, 0.0)
                new[i, j] = out.astype(jnp.bfloat16)
            store(new.at[i], schur.at[0, i, 0])
    for copy in stores:
        copy.wait()


def update(kernel, *gathered):
    hbm = pl.BlockSpec(memory_space=pltpu.HBM)
    return pl.pallas_call(
        update_kernel,
        out_shape=(
            jax.ShapeDtypeStruct((1, 4, 2, 256, 256), jnp.float32),
            jax.ShapeDtypeStruct((1, 4, 1, 2, 256, 256), jnp.bfloat16),
        ),
        in_specs=[hbm] + [pl.BlockSpec(memory_space=pltpu.VMEM)] * 3,
        out_specs=(hbm, hbm),
        scratch_shapes=[
            pltpu.VMEM((4, 2, 256, 256), jnp.bfloat16),
            pltpu.VMEM((4, 2, 256, 256), jnp.float32),
            pltpu.VMEM((4, 2, 256, 256), jnp.bfloat16),
            pltpu.SemaphoreType.DMA((9,)),
        ],
        compiler_params=pltpu.CompilerParams(vmem_limit_bytes=32 * 1024 * 1024),
        name="solve_and_update",
    )(kernel, *gathered)


def per_device(kernel):
    kernel = pltpu.with_memory_space_constraint(kernel, pltpu.HBM)
    return update(kernel, *gather(kernel))


def solution(mesh):
    in_specs = (P("row", None, "col", None, None, None),)
    out_specs = (P("row", None, None, None, None), P("row", None, "col", None, None, None))
    return jax.shard_map(per_device, mesh=mesh, in_specs=in_specs, out_specs=out_specs, check_vma=False)
```

```python
import functools

import jax
import jax.numpy as jnp
from jax import lax
from jax.experimental import pallas as pl
from jax.experimental.pallas import tpu as pltpu
from jax.sharding import PartitionSpec as P

MESH = pl.DeviceIdType.MESH
HI = lax.Precision.HIGHEST
PLANE = sorted(((a, b) for a in range(4) for b in range(4) if a or b), key=lambda d: -min(d[0], 4 - d[0]) - min(d[1], 4 - d[1]))
NEAR = ((0, 1), (0, 3), (1, 0), (3, 0))
LINE = sorted(range(1, 16), key=lambda d: -min(d, 16 - d))
GATE = 13
SKIP = {0: 3, 3: 6, 6: 7, 7: 8, 13: 10, 10: 9}
BACK = {0: 13, 3: 2, 2: 1, 6: 5, 5: 4, 13: 14, 14: 15, 10: 11, 11: 12}


def lookup(key, pairs):
    value = jnp.int32(0)
    for k, v in pairs.items():
        value = jnp.where(key == k, jnp.int32(v), value)
    return value


def member(key, keys):
    hit = key == keys[0]
    for k in keys[1:]:
        hit = jnp.logical_or(hit, key == k)
    return hit


def dot32(a, b, dims):
    return lax.dot_general(a, b, (dims, ((), ())), precision=HI, preferred_element_type=jnp.float32)


def row(v, i):
    return jnp.broadcast_to(v[i : i + 1, :], (8, 128))

def lane(v, i):
    return jnp.broadcast_to(v[:, i : i + 1], (8, 128))


def eliminate(strips, off):
    row_iota = lax.broadcasted_iota(jnp.int32, (8, 128), 0)
    strips = list(strips)
    diag = [lane(strips[0], off + i) for i in range(8)]
    pivots = []
    for s in range(8):
        later = range(s + 1, 8)
        cols = {t: [lane(strips[t], off + 8 * s + i) for i in range(8)] for t in later}
        if s < 7:
            raw = [lane(strips[s + 1], off + 8 * (s + 1) + i) for i in range(8)]
        head = strips[s]
        pivot = jnp.zeros((8, 128), jnp.float32)
        recips = []
        for i in range(8):
            own = diag[i]
            recip = 1.0 / row(own, i)
            recips.append(recip)
            pivot = jnp.where(row_iota == i, own, pivot)
            for j in range(i + 1, 8):
                line = row(own, j)
                diag[j] = diag[j] - (own * line) * recip
                factor = line * recip
                for t in later:
                    cols[t][j] = cols[t][j] - cols[t][i] * factor
            head = head - jnp.where(row_iota > i, own * recip, 0.0) * row(head, i)
        strips[s] = head
        pivots.append(pivot)
        if s < 7:
            near = cols[s + 1]
            scaled = [near[i] * recips[i] for i in range(8)]
            diag = []
            for j in range(8):
                terms = [scaled[i] * row(near[i], j) for i in range(8)]
                while len(terms) > 1:
                    terms = [terms[a] + terms[a + 1] for a in range(0, len(terms), 2)]
                diag.append(raw[j] - terms[0])
        heads = [row(head, i) * recips[i] for i in range(8)]
        for t in later:
            terms = [cols[t][i] * heads[i] for i in range(8)]
            while len(terms) > 1:
                terms = [terms[a] + terms[a + 1] for a in range(0, len(terms), 2)]
            strips[t] = strips[t] - terms[0]
    return strips, pivots


def factor_phase(g, store, middle):
    col_iota = lax.broadcasted_iota(jnp.int32, (8, 128), 1)
    row_iota = lax.broadcasted_iota(jnp.int32, (8, 128), 0)
    for b in range(4):
        odd = b % 2
        lo = 64 + 64 * b
        win = 128 * (b // 2)
        off = 64 * odd
        strips = []
        tile = g[lo:lo+64, win:win+128]
        for s in range(8):
            if odd:
                unit = jnp.where(col_iota == row_iota + 8 * s, 1.0, 0.0)
                strips.append(jnp.where(col_iota >= 64, tile[8*s:8*s+8], unit))
            else:
                unit = jnp.where(col_iota == row_iota + 8 * s + 64, 1.0, 0.0)
                strips.append(jnp.where(col_iota < 64, tile[8*s:8*s+8], unit))
        strips, pivots = eliminate(strips, off)
        keep = (col_iota < 64) if odd else (col_iota >= 64)
        wide = jnp.concatenate([jnp.where(keep, a * lax.rsqrt(p), 0.0) for a, p in zip(strips, pivots)], axis=0)
        turned = pltpu.roll(wide, 64, 1)
        low = wide if odd else turned
        high = turned if odd else wide
        if b == 1:
            middle()
        store(b, jnp.where(lax.broadcasted_iota(jnp.int32,(32,128),1) < 64, low[32:], high[:32]))
        base = lo if odd else lo - 64
        if b < 3:
            nwin = 128 * ((b + 1) // 2)
            u = dot32(wide, g[base:base+128, nwin:nwin+128], ((1,), (0,)))
            nxt = lo + 64
            noff = 64 * (1 - odd)
            if odd:
                g[nxt:nxt+64, nwin:nwin+128] = g[nxt:nxt+64, nwin:nwin+128] - dot32(u[:, 0:64], u, ((0,), (0,)))
            else:
                g[nxt:nxt+64, nwin:nwin+128] = g[nxt:nxt+64, nwin:nwin+128] - dot32(u, u, ((0,), (0,)))[64:128]
        lines = dot32(wide, g[base : base + 128, :], ((1,), (0,)))
        g[lo:lo+64, :] = lines
        if b < 3:
            first = 64 * (b + 1)
            change = dot32(lines[:, 0:256], lines, ((0,), (0,)))
            nxt = lo + 64
            nwin = 128 * ((b + 1) // 2)
            for lo_c, hi_c in ((0, nwin), (nwin + 128, 512)):
                if hi_c > lo_c:
                    g[nxt:nxt+64, lo_c:hi_c] = g[nxt:nxt+64, lo_c:hi_c] - change[first:first+64, lo_c:hi_c]
            if b < 2:
                g[nxt+64:320, :] = g[nxt+64:320, :] - change[first+64:256, :]


def set_identity(g):
    rows = lax.broadcasted_iota(jnp.int32, (256, 256), 0)
    cols = lax.broadcasted_iota(jnp.int32, (256, 256), 1)
    g[64:320, 256:512] = jnp.where(rows == cols, 1.0, 0.0)


def gather_kernel(
    kern, acol, brow, parts,
    lead, inv0, inv1, xs, gbuf, g, x_src, inv_src, inv1_src, work,
    p_send, p_recv, p_sib_send, p_sib_recv, m_send, m_recv, m_sib_send, m_sib_recv,
    lead_send, lead_recv, gs_send, gh_recv, gd_send, gd_recv, ga_send, ga_recv, parts_send, parts_recv,
    xr_send, xh_recv, xd_send, xd_recv, loc,
):
    r = lax.axis_index("row")
    c = lax.axis_index("col")
    x, y = lax.div(r, 4), lax.rem(r, 4)
    z, k = lax.div(c, 2), lax.rem(c, 2)
    zero, one = jnp.int32(0), jnp.int32(1)
    sibling = c + 1 - 2 * k
    both, neither = jnp.logical_and, jnp.logical_not
    top = z == 0
    inner = neither(top)

    def hub_core(row):
        return jnp.where(both(top, row != 0), 0, 1)

    hub = k == hub_core(r)
    mate = neither(hub)
    root = both(r == 0, c == 0)
    aide = both(r == 0, c == 1)
    helper = both(r == 1, c == 1)
    head = both(c == 1, r != 0)
    runner = both(k == 0, inner)
    skip_to = lookup(z, SKIP)
    back_to = lookup(z, BACK)
    has_skip = member(z, list(SKIP))
    has_back = member(z, list(BACK))
    parent = lookup(z, {v: q for q, v in list(SKIP.items()) + list(BACK.items())})
    children = has_skip.astype(jnp.int32) + has_back.astype(jnp.int32)
    barrier = pltpu.get_barrier_semaphore()

    def remote(src, dst, send, recv, row, col):
        return pltpu.make_async_remote_copy(
            src_ref=src, dst_ref=dst, send_sem=send, recv_sem=recv, device_id=(row, col), device_id_type=MESH
        )

    def signal(row, col):
        pl.semaphore_signal(barrier, inc=1, device_id=(row, col), device_id_type=MESH)

    def loop(lo, hi, body):
        def step(d, carry):
            body(d)
            return carry

        lax.fori_loop(lo, hi, step, 0)

    def when(cond, body):
        @pl.when(cond)
        def _():
            body()

    def start(copy):
        copy.start()

    def sent(copy):
        copy.wait_send()

    def peer(d):
        return lax.rem(x + d[0], 4) * 4 + lax.rem(y + d[1], 4)

    own_block = kern.at[0, 0, 0, 0]
    own_panel = pltpu.make_async_copy(kern.at[0, :, 0, 0], acol.at[:, k], loc.at[0])
    own_rows = pltpu.make_async_copy(kern.at[0, 0, 0], brow.at[lax.rem(r, 2), :, k], loc.at[1])
    own_lead = pltpu.make_async_copy(own_block, gbuf.at[0], loc.at[2])
    aide_piece = pltpu.make_async_copy(own_block.at[pl.ds(0, 16)], lead.at[0, 0], loc.at[2])
    helper_piece = pltpu.make_async_copy(own_block.at[pl.ds(16, 16)], lead.at[1, 1], loc.at[2])
    when(root, lambda: own_lead.start())
    when(aide, lambda: aide_piece.start())
    when(helper, lambda: helper_piece.start())
    when(top, lambda: own_panel.start())
    when(r < 2, lambda: own_rows.start())

    signal(r, sibling)

    def greet_panel():
        when(jnp.logical_or(parent != 0, r != 0), lambda: signal(r, 2 * parent))
        when(parent == 0, lambda: signal(r, one))

    when(runner, greet_panel)

    def greet_plane():
        for d in PLANE:
            signal(peer(d), c)
        when(inner, lambda: signal(r, one))

    when(k == 1, greet_plane)

    def greet_mirror():
        for d in NEAR:
            signal(peer(d), hub_core(peer(d)))

    when(both(hub, top), greet_mirror)

    def greet_sources():
        signal(zero, zero)
        signal(zero, one)
        when(r != 1, lambda: signal(one, one))

    when(head, greet_sources)
    when(jnp.logical_or(root, aide), lambda: signal(one, one))

    def arrive():
        plane = jnp.where(k == 1, 15, 0) + jnp.where(both(hub, top), 4, 0)
        line = jnp.where(root, 0, jnp.where(top, 2, jnp.where(k == 0, children, 0)))
        down = jnp.where(c == 1, 15, 0)
        more = jnp.where(root, 15, 0) + jnp.where(aide, 15, 0) + jnp.where(helper, 16, 0)
        pl.semaphore_wait(barrier, 1 + plane + line + down + more)
        when(top, lambda: own_panel.wait())
        when(r < 2, lambda: own_rows.wait())
        when(aide, lambda: aide_piece.wait())
        when(helper, lambda: helper_piece.wait())

    CHUNKS = tuple((i, quarter) for i in range(4) for quarter in range(4))

    def panel_copy(col, m, way):
        i, quarter = CHUNKS[m]
        chunk = acol.at[i, col, pl.ds(64 * quarter, 64)]
        n = 16 * col + m
        to = (r, 2 * skip_to) if way == 0 else (r, 2 * back_to) if way == 1 else (r, sibling)
        send = p_sib_send.at[n] if way == 2 else p_send.at[n, way]
        recv = p_sib_recv.at[n] if way == 2 else p_recv.at[n]
        return remote(chunk, chunk, send, recv, *to)

    def column_pair(col):
        return remote(acol.at[:, col], acol.at[:, col], p_sib_send.at[32], p_sib_recv.at[32], r, sibling)

    def panel_top(col, act, lo=0, hi=16):
        for m in range(lo, hi):
            act(panel_copy(col, m, 0))
            act(panel_copy(col, m, 1))

    def panel_line(t, act, arrive_first):
        col = jnp.where(r == 0, 1 - t, t)
        for m in range(16):
            if arrive_first:
                panel_copy(col, m, 0).wait_recv()
            when(has_skip, lambda m=m: act(panel_copy(col, m, 0)))
            when(has_back, lambda m=m: act(panel_copy(col, m, 1)))
            act(panel_copy(col, m, 2))

    def mirror_chunk(s, m):
        j, half = m // 4, m % 2
        return brow.at[s, j, (m // 2) % 2, pl.ds(128 * half, 128)]

    def mirror_copy(s, m, way, row):
        chunk = mirror_chunk(s, m)
        return remote(chunk, chunk, m_send.at[8 * s + m, way], m_recv.at[8 * s + m], row, 2 * z + hub_core(row))

    def mirror_pair(s, m):
        n = 8 * s + m
        return remote(mirror_chunk(s, m), mirror_chunk(s, m), m_sib_send.at[n], m_sib_recv.at[n], r, sibling)

    def mirror_feed(j, half):
        n = 8 * r + 4 * j + 2 * k + half
        chunk = brow.at[r, j, k, pl.ds(128 * half, 128)]
        return remote(chunk, chunk, m_sib_send.at[n], m_recv.at[n], r, sibling)

    def mirror_each(s, m, act):
        j, kc = m // 4, (m // 2) % 2
        rel = lax.rem(y + 4 - s, 4)
        ring_up = jnp.logical_or(rel == 0, both(s == 1, rel == 1))
        ring_down = jnp.logical_or(rel == 0, both(s == 0, rel == 3))
        line_up = jnp.logical_or(x == 0, both(s == 0, x == 1))
        line_down = jnp.logical_or(x == 0, both(s == 1, x == 3))
        if j == 0:
            ring_up, ring_down = both(ring_up, x == 0), both(ring_down, x == 0)
        else:
            line_up, line_down = both(line_up, rel == 0), both(line_down, rel == 0)
        when(ring_up, lambda: act(mirror_copy(s, m, 0, peer((0, 1)))))
        when(ring_down, lambda: act(mirror_copy(s, m, 1, peer((0, 3)))))
        when(line_up, lambda: act(mirror_copy(s, m, 2, peer((1, 0)))))
        when(line_down, lambda: act(mirror_copy(s, m, 3, peer((3, 0)))))
        when(both(kc != k, r != s), lambda: act(mirror_pair(s, m)))

    def mirror_half(t):
        nearer = jnp.where(jnp.logical_or(y == 0, y == 3), 0, 1)
        s = jnp.where(nearer == t, 0, 1)
        for m in range(8):
            when(jnp.logical_or(r != s, k != (m // 2) % 2), lambda m=m: mirror_copy(s, m, 0, r).wait_recv())
            mirror_each(s, m, start)

    def mirror_sent(s):
        for m in range(8):
            mirror_each(s, m, sent)

    def feeds(act):
        for j in range(2):
            for half in range(2):
                act(mirror_feed(j, half))

    def mirror_take():
        for s in range(2):

            def take(s=s):
                for kc in range(2):

                    def mine(kc=kc):
                        for j in range(2):
                            for half in range(2):
                                mirror_pair(s, 4 * j + 2 * kc + half).wait_recv()

                    when(k == kc, mine)

            when(r != s, take)

    def lead_from(n, p):
        rows = own_block.at[pl.ds(16 * p, 16)]
        return remote(rows, lead.at[p, n], gs_send.at[p], gh_recv.at[n], jnp.int32(p), one)

    def lead_scatter(n, act):
        for p in range(16):
            if p != n:
                act(lead_from(n, p))

    def view(which, p):
        if which < 2:
            return (lead, inv0)[which].at[p]
        return inv1.at[lax.div(p, 2)]

    def takes_part(which, row):
        return row >= 0 if which < 2 else lax.rem(row, 2) == 0

    def down(which, act):
        piece = view(which, r)

        def go():
            for d in LINE:
                act(remote(piece, piece, gd_send.at[which, d], gd_recv.at[which], r, jnp.int32(2 * d + 1)))

        when(takes_part(which, r), go)

    def across(which, act):
        piece = view(which, r)

        def go():
            for n, d in enumerate(PLANE):
                act(remote(piece, piece, ga_send.at[which, n], ga_recv.at[which, r], peer(d), c))

        when(takes_part(which, r), go)

    def piece_taken(which):
        piece = view(which, r)
        copy = remote(piece, piece, gd_send.at[which, 0], gd_recv.at[which], r, sibling)
        when(takes_part(which, r), lambda: copy.wait_recv())

    def collect(which):
        def take(d):
            p = lax.rem(r + d, 16)
            piece = view(which, p)
            copy = remote(piece, piece, ga_send.at[which, 0], ga_recv.at[which, p], r, sibling)
            when(takes_part(which, p), lambda: copy.wait_recv())

        loop(1, 16, take)

    def inverse_piece(p):
        return remote(inv_src.at[p], inv0.at[p], xr_send.at[0, p], xh_recv.at[0], jnp.int32(p), one)

    def next_piece(p):
        return remote(inv1_src.at[p // 2], inv1.at[p // 2], xr_send.at[1, p], xh_recv.at[1], jnp.int32(p), one)

    def inverse_first(n, p):
        return remote(x_src.at[n], xs.at[n], xr_send.at[2 + n, p], xh_recv.at[2 + n], jnp.int32(p), one)

    def from_root(act, copy, step=1):
        for d in PLANE:
            p = 4 * d[0] + d[1]
            if p % step == 0:
                act(copy(p))
        act(copy(0))

    def inverse_down(n, act):
        for d in LINE:
            act(remote(xs.at[n], xs.at[n], xd_send.at[n, d], xd_recv.at[n], r, jnp.int32(2 * d + 1)))

    def inverse_taken(n):
        remote(xs.at[n], xs.at[n], xd_send.at[n, 0], xd_recv.at[n], r, sibling).wait_recv()

    def parts_pair(n):
        block = parts.at[0] if n == 0 else parts.at[pl.ds(1, 2), :, pl.ds(64 * (n - 1), 64)]
        return remote(block, block, parts_send.at[n], parts_recv.at[n], r, sibling)

    def lead_copy(n):
        return remote(own_block, gbuf.at[n + 1], lead_send.at[n], lead_recv.at[n], zero, zero)

    def root_main():
        own_lead.wait()
        g[0:64, :] = jnp.zeros((64, 512), jnp.float32)
        g[320:384, :] = jnp.zeros((64, 512), jnp.float32)
        g[64:320, 0:256] = gbuf[0].astype(jnp.float32)
        set_identity(g)

        def bulk():
            arrive()
            column_pair(0).start()
            feeds(start)

        def second_half():
            for p in range(16):
                inv_src[p] = g[64 + 16 * p : 80 + 16 * p, 256:512]
            from_root(start, inverse_piece)
            lead_copy(0).wait_recv()
            lead_copy(1).wait_recv()
            side = dot32(g[64:320, 256:512], gbuf[1].astype(jnp.float32), ((1,), (0,)))
            g[64:320, 0:256] = gbuf[2].astype(jnp.float32) - dot32(side, side, ((0,), (0,)))
            set_identity(g)

        def phase(it):
            def store(n, packed):
                if n < 2:
                    for part in range(4):
                        inv1_src[4 * n + part] = packed[8 * part : 8 * part + 8]
                    if n == 1:
                        when(it == 1, lambda: from_root(start, next_piece, 2))
                else:
                    x_src[n - 2] = packed
                    when(it == 1, lambda: from_root(start, lambda p: inverse_first(n - 2, p)))

            factor_phase(g, store, lambda: when(it == 0, bulk))
            when(it == 0, second_half)

        loop(0, 2, phase)

    when(root, root_main)
    when(neither(root), arrive)

    def top_sends():
        when(aide, lambda: lead_copy(0).start())
        when(helper, lambda: lead_copy(1).start())
        panel_top(k, start)
        column_pair(k).start()
        when(aide, lambda: lead_scatter(0, start))
        when(helper, lambda: lead_scatter(1, start))

    when(both(top, neither(root)), top_sends)
    when(both(both(mate, r < 2), neither(root)), lambda: feeds(start))

    def top_spread(which):
        down(which, start)
        across(which, start)

    def head_inverses(p):
        when(takes_part(2, r), lambda: next_piece(p).wait_recv())
        top_spread(2)
        for n in range(2):
            inverse_first(n, p).wait_recv()
            inverse_down(n, start)

    def aide_main():
        column_pair(0).wait_recv()
        panel_top(0, start)
        loop(0, 1, mirror_half)
        lead_from(1, 0).wait_recv()
        inverse_piece(0).wait_recv()
        panel_top(1, sent, 0, GATE)
        panel_top(0, sent, 0, GATE)
        top_spread(1)
        top_spread(0)
        head_inverses(0)
        loop(1, 2, mirror_half)

    when(aide, aide_main)
    when(both(hub, neither(aide)), lambda: loop(0, 2, mirror_half))

    def head_main():
        lead_from(0, 1).wait_recv()
        when(neither(helper), lambda: lead_from(1, 2).wait_recv())
        inverse_piece(1).wait_recv()
        panel_top(1, sent, 0, GATE)
        top_spread(1)
        top_spread(0)
        head_inverses(2)

    when(head, head_main)

    def line_spread():
        for which in (1, 0, 2):
            piece_taken(which)
            across(which, start)

    when(both(k == 1, inner), line_spread)
    when(runner, lambda: loop(0, 2, lambda t: panel_line(t, start, True)))

    def put(block, lo, hi, values):
        high = values.astype(jnp.bfloat16)
        parts[block, 0, lo:hi] = high
        parts[block, 1, lo:hi] = (values - high.astype(jnp.float32)).astype(jnp.bfloat16)

    def assemble():
        def block(n):
            return jnp.concatenate([lead[p, n] for p in range(16)], axis=0).astype(jnp.float32)

        collect(0)
        collect(1)
        first_inverse = jnp.concatenate([inv0[p] for p in range(16)], axis=0)
        put(0, 0, 256, first_inverse)
        parts_pair(0).start()
        side = dot32(first_inverse, block(0), ((1,), (0,)))
        work[:, 0:256] = block(1) - dot32(side, side, ((0,), (0,)))
        work[:, 256:512] = -dot32(side, first_inverse, ((0,), (0,)))
        rows = lax.broadcasted_iota(jnp.int32, (256, 256), 0)
        cols = lax.broadcasted_iota(jnp.int32, (256, 256), 1)
        work[:, 512:768] = jnp.where(rows == cols, 1.0, 0.0)
        collect(2)
        for n in range(4):
            if n < 2:
                packed = jnp.concatenate([inv1[4 * n + p] for p in range(4)], axis=0)
            else:
                when(inner, lambda n=n: inverse_taken(n - 2))
                packed = xs[n - 2]
            inverse = jnp.concatenate([packed[:, 64:128], packed[:, 0:64]], axis=0)
            lo, hi = 64 * n, 64 * n + 64
            lines = dot32(inverse, work[lo:hi, :], ((1,), (0,)))
            put(1, lo, hi, lines[:, 256:512])
            put(2, lo, hi, lines[:, 512:768])
            parts_pair(1 + n).start()
            if n < 3:
                work[hi:256, :] = work[hi:256, :] - dot32(lines[:, hi:256], lines, ((0,), (0,)))

    when(k == 1, assemble)

    def parts_take():
        for n in range(5):
            parts_pair(n).wait_recv()

    when(k == 0, parts_take)
    when(mate, mirror_take)

    def column_taken(col):
        for m in range(16):
            panel_copy(col, m, 2).wait_recv()

    when(both(k == 1, inner), lambda: loop(0, 2, column_taken))
    when(both(top, neither(aide)), lambda: column_pair(1 - k).wait_recv())

    when(runner, lambda: loop(0, 2, lambda t: panel_line(t, sent, False)))

    def top_drain():
        column_pair(k).wait_send()
        when(both(k == 0, neither(root)), lambda: panel_top(0, sent))
        when(k == 1, lambda: panel_top(1, sent, GATE))
        when(aide, lambda: panel_top(0, sent, GATE))

    when(top, top_drain)
    when(both(mate, r < 2), lambda: feeds(sent))

    when(hub, lambda: loop(0, 2, mirror_sent))

    def core1_drain():
        for which in range(3):
            across(which, sent)
        for n in range(5):
            parts_pair(n).wait_send()

    when(k == 1, core1_drain)

    def line_drain():
        for which in range(3):
            down(which, sent)
        for n in range(2):
            inverse_down(n, sent)

    when(c == 1, line_drain)

    def aide_drain():
        lead_copy(0).wait_send()
        lead_scatter(0, sent)

    when(aide, aide_drain)

    def helper_drain():
        lead_copy(1).wait_send()
        lead_scatter(1, sent)

    when(helper, helper_drain)

    def root_drain():
        from_root(sent, inverse_piece)
        from_root(sent, next_piece, 2)
        for n in range(2):
            from_root(sent, lambda p, n=n: inverse_first(n, p))

    when(root, root_drain)


def gather(kernel):
    bf16, f32 = jnp.bfloat16, jnp.float32
    dma = pltpu.SemaphoreType.DMA
    return pl.pallas_call(
        gather_kernel,
        out_shape=(
            jax.ShapeDtypeStruct((4, 2, 256, 256), bf16),
            jax.ShapeDtypeStruct((2, 2, 2, 256, 256), bf16),
            jax.ShapeDtypeStruct((3, 2, 256, 256), bf16),
        ),
        in_specs=[pl.BlockSpec(memory_space=pltpu.HBM)],
        out_specs=(
            pl.BlockSpec(memory_space=pl.ANY),
            pl.BlockSpec(memory_space=pl.ANY),
            pl.BlockSpec(memory_space=pltpu.VMEM),
        ),
        scratch_shapes=[
            pltpu.VMEM((16, 2, 16, 256), bf16),
            pltpu.VMEM((16, 16, 256), f32),
            pltpu.VMEM((8, 8, 128), f32),
            pltpu.VMEM((2, 32, 128), f32),
            pltpu.VMEM((3, 256, 256), bf16),
            pltpu.VMEM((384, 512), f32),
            pltpu.VMEM((2, 32, 128), f32),
            pltpu.VMEM((16, 16, 256), f32),
            pltpu.VMEM((8, 8, 128), f32),
            pltpu.VMEM((256, 768), f32),
            dma((32, 2)), dma((32,)), dma((33,)), dma((33,)),
            dma((16, 4)), dma((16,)), dma((16,)), dma((16,)),
            dma((2,)), dma((2,)),
            dma((16,)), dma((2,)), dma((3, 16)), dma((3,)), dma((3, 16)), dma((3, 16)), dma((5,)), dma((5,)),
            dma((4, 16)), dma((4,)), dma((2, 16)), dma((2,)), dma((3,)),
        ],
        compiler_params=pltpu.CompilerParams(
            collective_id=0, has_side_effects=True, vmem_limit_bytes=24 * 1024 * 1024
        ),
        name="gather_and_factor",
    )(kernel)


def update_kernel(kern, acol, brow, parts, panels, schur, old, pan, new, sems):
    r = lax.axis_index("row")
    c = lax.axis_index("col")
    k = lax.rem(c, 2)
    load = pltpu.make_async_copy(kern.at[0, :, 0], old, sems.at[0])
    load.start()
    f32 = jnp.float32
    tri = lax.broadcasted_iota(jnp.int32, (256, 256), 0) >= lax.broadcasted_iota(jnp.int32, (256, 256), 1)
    stores = []

    def store(src, dst):
        stores.append(pltpu.make_async_copy(src, dst, sems.at[1 + len(stores)]))
        stores[-1].start()

    def rows(a, b):
        return lax.dot_general(a, b, (((1,), (1,)), ((), ())), preferred_element_type=f32)

    lefts = []
    for h in range(2):
        a, b = (jnp.concatenate([acol[2 * h, s], acol[2 * h + 1, s]], axis=0) for s in range(2))
        first = rows(a, parts[0, 0]) + rows(a, parts[0, 1])
        second = rows(a, parts[1, 0]) + rows(a, parts[1, 1]) + rows(b, parts[2, 0]) + rows(b, parts[2, 1])
        lefts.append(jnp.concatenate([first.astype(jnp.bfloat16), second.astype(jnp.bfloat16)], axis=1))
        for e in range(2):
            i = 2 * h + e
            for n, solved in enumerate((first, second)):
                part = solved[256 * e : 256 * e + 256]
                if i == 0:
                    whole = jnp.logical_or(r > n, jnp.logical_and(r == n, tri))
                    part = jnp.where(whole, part, 0.0)
                pan[i, n] = part
            store(pan.at[i], panels.at[0, i])
    columns = []
    for j in range(2):
        a, b = brow[0, j, k], brow[1, j, k]
        upper = jnp.dot(parts[0, 0], a, preferred_element_type=f32) + jnp.dot(
            parts[0, 1], a, preferred_element_type=f32
        )
        lower = jnp.dot(parts[1, 0], a, preferred_element_type=f32) + jnp.dot(
            parts[1, 1], a, preferred_element_type=f32
        )
        lower = lower + jnp.dot(parts[2, 0], b, preferred_element_type=f32)
        lower = lower + jnp.dot(parts[2, 1], b, preferred_element_type=f32)
        columns.append(jnp.concatenate([upper, lower], axis=0).astype(jnp.bfloat16))
    mirror = jnp.concatenate(columns, axis=1)
    load.wait()
    for h in range(2):
        change = jnp.dot(lefts[h], mirror, preferred_element_type=f32)
        for e in range(2):
            i = 2 * h + e
            for j in range(2):
                out = old[i, j].astype(f32) - change[256 * e : 256 * e + 256, 256 * j : 256 * j + 256]
                if i == 0:
                    out = jnp.where(r >= 2, out, 0.0)
                if j == 0:
                    out = jnp.where(c >= 2, out, 0.0)
                new[i, j] = out.astype(jnp.bfloat16)
            store(new.at[i], schur.at[0, i, 0])
    for copy in stores:
        copy.wait()


def update(kernel, *gathered):
    hbm = pl.BlockSpec(memory_space=pltpu.HBM)
    return pl.pallas_call(
        update_kernel,
        out_shape=(
            jax.ShapeDtypeStruct((1, 4, 2, 256, 256), jnp.float32),
            jax.ShapeDtypeStruct((1, 4, 1, 2, 256, 256), jnp.bfloat16),
        ),
        in_specs=[hbm] + [pl.BlockSpec(memory_space=pltpu.VMEM)] * 3,
        out_specs=(hbm, hbm),
        scratch_shapes=[
            pltpu.VMEM((4, 2, 256, 256), jnp.bfloat16),
            pltpu.VMEM((4, 2, 256, 256), jnp.float32),
            pltpu.VMEM((4, 2, 256, 256), jnp.bfloat16),
            pltpu.SemaphoreType.DMA((9,)),
        ],
        compiler_params=pltpu.CompilerParams(vmem_limit_bytes=32 * 1024 * 1024),
        name="solve_and_update",
    )(kernel, *gathered)


def per_device(kernel):
    kernel = pltpu.with_memory_space_constraint(kernel, pltpu.HBM)
    return update(kernel, *gather(kernel))


def solution(mesh):
    in_specs = (P("row", None, "col", None, None, None),)
    out_specs = (P("row", None, None, None, None), P("row", None, "col", None, None, None))
    return jax.shard_map(per_device, mesh=mesh, in_specs=in_specs, out_specs=out_specs, check_vma=False)
```

```python
import functools

import jax
import jax.numpy as jnp
from jax import lax
from jax.experimental import pallas as pl
from jax.experimental.pallas import tpu as pltpu
from jax.sharding import PartitionSpec as P

MESH = pl.DeviceIdType.MESH
HI = lax.Precision.HIGHEST
PLANE = sorted(((a, b) for a in range(4) for b in range(4) if a or b), key=lambda d: -min(d[0], 4 - d[0]) - min(d[1], 4 - d[1]))
NEAR = ((0, 1), (0, 3), (1, 0), (3, 0))
LINE = sorted(range(1, 16), key=lambda d: -min(d, 16 - d))
SKIP = {0: 3, 3: 5, 5: 6, 6: 7, 13: 11, 11: 9, 9: 8}
BACK = {0: 13, 3: 2, 2: 1, 5: 4, 13: 14, 14: 15, 11: 12, 9: 10}


def lookup(key, pairs):
    value = jnp.int32(0)
    for k, v in pairs.items():
        value = jnp.where(key == k, jnp.int32(v), value)
    return value


def member(key, keys):
    hit = key == keys[0]
    for k in keys[1:]:
        hit = jnp.logical_or(hit, key == k)
    return hit


def dot32(a, b, dims):
    return lax.dot_general(a, b, (dims, ((), ())), precision=HI, preferred_element_type=jnp.float32)


def row(v, i):
    return jnp.broadcast_to(v[i : i + 1, :], (8, 128))

def lane(v, i):
    return jnp.broadcast_to(v[:, i : i + 1], (8, 128))


def eliminate(strips, off):
    row_iota = lax.broadcasted_iota(jnp.int32, (8, 128), 0)
    strips = list(strips)
    diag = [lane(strips[0], off + i) for i in range(8)]
    pivots = []
    for s in range(8):
        later = range(s + 1, 8)
        cols = {t: [lane(strips[t], off + 8 * s + i) for i in range(8)] for t in later}
        if s < 7:
            raw = [lane(strips[s + 1], off + 8 * (s + 1) + i) for i in range(8)]
        head = strips[s]
        pivot = jnp.zeros((8, 128), jnp.float32)
        recips = []
        for i in range(8):
            own = diag[i]
            recip = 1.0 / row(own, i)
            recips.append(recip)
            pivot = jnp.where(row_iota == i, own, pivot)
            for j in range(i + 1, 8):
                line = row(own, j)
                diag[j] = diag[j] - (own * line) * recip
                factor = line * recip
                for t in later:
                    cols[t][j] = cols[t][j] - cols[t][i] * factor
            head = head - jnp.where(row_iota > i, own * recip, 0.0) * row(head, i)
        strips[s] = head
        pivots.append(pivot)
        if s < 7:
            near = cols[s + 1]
            scaled = [near[i] * recips[i] for i in range(8)]
            diag = []
            for j in range(8):
                terms = [scaled[i] * row(near[i], j) for i in range(8)]
                while len(terms) > 1:
                    terms = [terms[a] + terms[a + 1] for a in range(0, len(terms), 2)]
                diag.append(raw[j] - terms[0])
        heads = [row(head, i) * recips[i] for i in range(8)]
        for t in later:
            terms = [cols[t][i] * heads[i] for i in range(8)]
            while len(terms) > 1:
                terms = [terms[a] + terms[a + 1] for a in range(0, len(terms), 2)]
            strips[t] = strips[t] - terms[0]
    return strips, pivots


def factor_phase(g, store, middle):
    col_iota = lax.broadcasted_iota(jnp.int32, (8, 128), 1)
    row_iota = lax.broadcasted_iota(jnp.int32, (8, 128), 0)
    for b in range(4):
        odd = b % 2
        lo = 64 + 64 * b
        win = 128 * (b // 2)
        off = 64 * odd
        strips = []
        tile = g[lo:lo+64, win:win+128]
        for s in range(8):
            if odd:
                unit = jnp.where(col_iota == row_iota + 8 * s, 1.0, 0.0)
                strips.append(jnp.where(col_iota >= 64, tile[8*s:8*s+8], unit))
            else:
                unit = jnp.where(col_iota == row_iota + 8 * s + 64, 1.0, 0.0)
                strips.append(jnp.where(col_iota < 64, tile[8*s:8*s+8], unit))
        strips, pivots = eliminate(strips, off)
        keep = (col_iota < 64) if odd else (col_iota >= 64)
        wide = jnp.concatenate([jnp.where(keep, a * lax.rsqrt(p), 0.0) for a, p in zip(strips, pivots)], axis=0)
        turned = pltpu.roll(wide, 64, 1)
        low = wide if odd else turned
        high = turned if odd else wide
        if b == 1:
            middle()
        store(b, jnp.where(lax.broadcasted_iota(jnp.int32,(32,128),1) < 64, low[32:], high[:32]))
        base = lo if odd else lo - 64
        if b < 3:
            nwin = 128 * ((b + 1) // 2)
            u = dot32(wide, g[base:base+128, nwin:nwin+128], ((1,), (0,)))
            nxt = lo + 64
            noff = 64 * (1 - odd)
            if odd:
                g[nxt:nxt+64, nwin:nwin+128] = g[nxt:nxt+64, nwin:nwin+128] - dot32(u[:, 0:64], u, ((0,), (0,)))
            else:
                g[nxt:nxt+64, nwin:nwin+128] = g[nxt:nxt+64, nwin:nwin+128] - dot32(u, u, ((0,), (0,)))[64:128]
        lines = dot32(wide, g[base : base + 128, :], ((1,), (0,)))
        g[lo:lo+64, :] = lines
        if b < 3:
            first = 64 * (b + 1)
            change = dot32(lines[:, 0:256], lines, ((0,), (0,)))
            nxt = lo + 64
            nwin = 128 * ((b + 1) // 2)
            for lo_c, hi_c in ((0, nwin), (nwin + 128, 512)):
                if hi_c > lo_c:
                    g[nxt:nxt+64, lo_c:hi_c] = g[nxt:nxt+64, lo_c:hi_c] - change[first:first+64, lo_c:hi_c]
            if b < 2:
                g[nxt+64:320, :] = g[nxt+64:320, :] - change[first+64:256, :]


def set_identity(g):
    rows = lax.broadcasted_iota(jnp.int32, (256, 256), 0)
    cols = lax.broadcasted_iota(jnp.int32, (256, 256), 1)
    g[64:320, 256:512] = jnp.where(rows == cols, 1.0, 0.0)


def gather_kernel(
    kern, acol, brow, parts,
    lead, inv0, inv1, xs, gbuf, g, x_src, inv_src, inv1_src, work,
    p_send, p_recv, p_sib_send, p_sib_recv, m_send, m_recv, m_sib_send, m_sib_recv,
    lead_send, lead_recv, gs_send, gh_recv, gd_send, gd_recv, ga_send, ga_recv, parts_send, parts_recv,
    xr_send, xh_recv, xd_send, xd_recv, loc,
):
    r = lax.axis_index("row")
    c = lax.axis_index("col")
    x, y = lax.div(r, 4), lax.rem(r, 4)
    z, k = lax.div(c, 2), lax.rem(c, 2)
    zero, one = jnp.int32(0), jnp.int32(1)
    sibling = c + 1 - 2 * k
    both, neither = jnp.logical_and, jnp.logical_not
    top = z == 0
    inner = neither(top)

    def hub_core(row):
        return jnp.where(both(top, row != 0), 0, 1)

    hub = k == hub_core(r)
    mate = neither(hub)
    root = both(r == 0, c == 0)
    aide = both(r == 0, c == 1)
    helper = both(r == 1, c == 1)
    head = both(c == 1, r != 0)
    runner = both(k == 0, inner)
    skip_to = lookup(z, SKIP)
    back_to = lookup(z, BACK)
    has_skip = member(z, list(SKIP))
    has_back = member(z, list(BACK))
    parent = lookup(z, {v: q for q, v in list(SKIP.items()) + list(BACK.items())})
    children = has_skip.astype(jnp.int32) + has_back.astype(jnp.int32)
    barrier = pltpu.get_barrier_semaphore()

    def remote(src, dst, send, recv, row, col):
        return pltpu.make_async_remote_copy(
            src_ref=src, dst_ref=dst, send_sem=send, recv_sem=recv, device_id=(row, col), device_id_type=MESH
        )

    def signal(row, col):
        pl.semaphore_signal(barrier, inc=1, device_id=(row, col), device_id_type=MESH)

    def loop(lo, hi, body):
        def step(d, carry):
            body(d)
            return carry

        lax.fori_loop(lo, hi, step, 0)

    def when(cond, body):
        @pl.when(cond)
        def _():
            body()

    def start(copy):
        copy.start()

    def sent(copy):
        copy.wait_send()

    def peer(d):
        return lax.rem(x + d[0], 4) * 4 + lax.rem(y + d[1], 4)

    own_block = kern.at[0, 0, 0, 0]
    own_panel = pltpu.make_async_copy(kern.at[0, :, 0, 0], acol.at[:, k], loc.at[0])
    own_rows = pltpu.make_async_copy(kern.at[0, 0, 0], brow.at[lax.rem(r, 2), :, k], loc.at[1])
    own_lead = pltpu.make_async_copy(own_block, gbuf.at[0], loc.at[2])
    aide_piece = pltpu.make_async_copy(own_block.at[pl.ds(0, 16)], lead.at[0, 0], loc.at[2])
    helper_piece = pltpu.make_async_copy(own_block.at[pl.ds(16, 16)], lead.at[1, 1], loc.at[2])
    when(root, lambda: own_lead.start())
    when(aide, lambda: aide_piece.start())
    when(helper, lambda: helper_piece.start())
    when(top, lambda: own_panel.start())
    when(r < 2, lambda: own_rows.start())

    signal(r, sibling)

    def greet_panel():
        when(jnp.logical_or(parent != 0, r != 0), lambda: signal(r, 2 * parent))
        when(parent == 0, lambda: signal(r, one))

    when(runner, greet_panel)

    def greet_plane():
        for d in PLANE:
            signal(peer(d), c)
        when(inner, lambda: signal(r, one))

    when(k == 1, greet_plane)

    def greet_mirror():
        for d in NEAR:
            signal(peer(d), hub_core(peer(d)))

    when(both(hub, top), greet_mirror)

    def greet_sources():
        signal(zero, zero)
        signal(zero, one)
        when(r != 1, lambda: signal(one, one))

    when(head, greet_sources)
    when(jnp.logical_or(root, aide), lambda: signal(one, one))

    def arrive():
        plane = jnp.where(k == 1, 15, 0) + jnp.where(both(hub, top), 4, 0)
        line = jnp.where(root, 0, jnp.where(top, 2, jnp.where(k == 0, children, 0)))
        down = jnp.where(c == 1, 15, 0)
        more = jnp.where(root, 15, 0) + jnp.where(aide, 15, 0) + jnp.where(helper, 16, 0)
        pl.semaphore_wait(barrier, 1 + plane + line + down + more)
        when(top, lambda: own_panel.wait())
        when(r < 2, lambda: own_rows.wait())
        when(aide, lambda: aide_piece.wait())
        when(helper, lambda: helper_piece.wait())

    CHUNKS = tuple((i, quarter) for i in range(4) for quarter in range(4))

    def panel_copy(col, m, way):
        i, quarter = CHUNKS[m]
        chunk = acol.at[i, col, pl.ds(64 * quarter, 64)]
        n = 16 * col + m
        to = (r, 2 * skip_to) if way == 0 else (r, 2 * back_to) if way == 1 else (r, sibling)
        send = p_sib_send.at[n] if way == 2 else p_send.at[n, way]
        recv = p_sib_recv.at[n] if way == 2 else p_recv.at[n]
        return remote(chunk, chunk, send, recv, *to)

    def column_pair(col):
        return remote(acol.at[:, col], acol.at[:, col], p_sib_send.at[32], p_sib_recv.at[32], r, sibling)

    def panel_top(col, act):
        for m in range(16):
            act(panel_copy(col, m, 0))
            act(panel_copy(col, m, 1))

    def panel_line(t, act, arrive_first):
        col = jnp.where(r == 0, 1 - t, t)
        for m in range(16):
            if arrive_first:
                panel_copy(col, m, 0).wait_recv()
            when(has_skip, lambda m=m: act(panel_copy(col, m, 0)))
            when(has_back, lambda m=m: act(panel_copy(col, m, 1)))
            act(panel_copy(col, m, 2))

    def mirror_chunk(s, m):
        j, half = m // 4, m % 2
        return brow.at[s, j, (m // 2) % 2, pl.ds(128 * half, 128)]

    def mirror_copy(s, m, way, row):
        chunk = mirror_chunk(s, m)
        return remote(chunk, chunk, m_send.at[8 * s + m, way], m_recv.at[8 * s + m], row, 2 * z + hub_core(row))

    def mirror_pair(s, m):
        n = 8 * s + m
        return remote(mirror_chunk(s, m), mirror_chunk(s, m), m_sib_send.at[n], m_sib_recv.at[n], r, sibling)

    def mirror_feed(j, half):
        n = 8 * r + 4 * j + 2 * k + half
        chunk = brow.at[r, j, k, pl.ds(128 * half, 128)]
        return remote(chunk, chunk, m_sib_send.at[n], m_recv.at[n], r, sibling)

    def mirror_each(s, m, act):
        j, kc = m // 4, (m // 2) % 2
        rel = lax.rem(y + 4 - s, 4)
        ring_up = jnp.logical_or(rel == 0, both(s == 1, rel == 1))
        ring_down = jnp.logical_or(rel == 0, both(s == 0, rel == 3))
        line_up = jnp.logical_or(x == 0, both(s == 0, x == 1))
        line_down = jnp.logical_or(x == 0, both(s == 1, x == 3))
        if j == 0:
            ring_up, ring_down = both(ring_up, x == 0), both(ring_down, x == 0)
        else:
            line_up, line_down = both(line_up, rel == 0), both(line_down, rel == 0)
        when(ring_up, lambda: act(mirror_copy(s, m, 0, peer((0, 1)))))
        when(ring_down, lambda: act(mirror_copy(s, m, 1, peer((0, 3)))))
        when(line_up, lambda: act(mirror_copy(s, m, 2, peer((1, 0)))))
        when(line_down, lambda: act(mirror_copy(s, m, 3, peer((3, 0)))))
        when(both(kc != k, r != s), lambda: act(mirror_pair(s, m)))

    def mirror_half(t):
        nearer = jnp.where(jnp.logical_or(y == 0, y == 3), 0, 1)
        s = jnp.where(nearer == t, 0, 1)
        for m in range(8):
            when(jnp.logical_or(r != s, k != (m // 2) % 2), lambda m=m: mirror_copy(s, m, 0, r).wait_recv())
            mirror_each(s, m, start)

    def mirror_sent(s):
        for m in range(8):
            mirror_each(s, m, sent)

    def feeds(act):
        for j in range(2):
            for half in range(2):
                act(mirror_feed(j, half))

    def mirror_take():
        for s in range(2):

            def take(s=s):
                for kc in range(2):

                    def mine(kc=kc):
                        for j in range(2):
                            for half in range(2):
                                mirror_pair(s, 4 * j + 2 * kc + half).wait_recv()

                    when(k == kc, mine)

            when(r != s, take)

    def lead_from(n, p):
        rows = own_block.at[pl.ds(16 * p, 16)]
        return remote(rows, lead.at[p, n], gs_send.at[p], gh_recv.at[n], jnp.int32(p), one)

    def lead_scatter(n, act):
        for p in range(16):
            if p != n:
                act(lead_from(n, p))

    def view(which, p):
        if which < 2:
            return (lead, inv0)[which].at[p]
        return inv1.at[lax.div(p, 2)]

    def takes_part(which, row):
        return row >= 0 if which < 2 else lax.rem(row, 2) == 0

    def down(which, act):
        piece = view(which, r)

        def go():
            for d in LINE:
                act(remote(piece, piece, gd_send.at[which, d], gd_recv.at[which], r, jnp.int32(2 * d + 1)))

        when(takes_part(which, r), go)

    def across(which, act):
        piece = view(which, r)

        def go():
            for n, d in enumerate(PLANE):
                act(remote(piece, piece, ga_send.at[which, n], ga_recv.at[which, r], peer(d), c))

        when(takes_part(which, r), go)

    def piece_taken(which):
        piece = view(which, r)
        copy = remote(piece, piece, gd_send.at[which, 0], gd_recv.at[which], r, sibling)
        when(takes_part(which, r), lambda: copy.wait_recv())

    def collect(which):
        def take(d):
            p = lax.rem(r + d, 16)
            piece = view(which, p)
            copy = remote(piece, piece, ga_send.at[which, 0], ga_recv.at[which, p], r, sibling)
            when(takes_part(which, p), lambda: copy.wait_recv())

        loop(1, 16, take)

    def inverse_piece(p):
        return remote(inv_src.at[p], inv0.at[p], xr_send.at[0, p], xh_recv.at[0], jnp.int32(p), one)

    def next_piece(p):
        return remote(inv1_src.at[p // 2], inv1.at[p // 2], xr_send.at[1, p], xh_recv.at[1], jnp.int32(p), one)

    def inverse_first(n, p):
        return remote(x_src.at[n], xs.at[n], xr_send.at[2 + n, p], xh_recv.at[2 + n], jnp.int32(p), one)

    def from_root(act, copy, step=1):
        for d in PLANE:
            p = 4 * d[0] + d[1]
            if p % step == 0:
                act(copy(p))
        act(copy(0))

    def inverse_down(n, act):
        for d in LINE:
            act(remote(xs.at[n], xs.at[n], xd_send.at[n, d], xd_recv.at[n], r, jnp.int32(2 * d + 1)))

    def inverse_taken(n):
        remote(xs.at[n], xs.at[n], xd_send.at[n, 0], xd_recv.at[n], r, sibling).wait_recv()

    def parts_pair(n):
        block = parts.at[0] if n == 0 else parts.at[pl.ds(1, 2), :, pl.ds(64 * (n - 1), 64)]
        return remote(block, block, parts_send.at[n], parts_recv.at[n], r, sibling)

    def lead_copy(n):
        return remote(own_block, gbuf.at[n + 1], lead_send.at[n], lead_recv.at[n], zero, zero)

    def root_main():
        own_lead.wait()
        g[0:64, :] = jnp.zeros((64, 512), jnp.float32)
        g[320:384, :] = jnp.zeros((64, 512), jnp.float32)
        g[64:320, 0:256] = gbuf[0].astype(jnp.float32)
        set_identity(g)

        def bulk():
            arrive()
            column_pair(0).start()
            feeds(start)

        def second_half():
            for p in range(16):
                inv_src[p] = g[64 + 16 * p : 80 + 16 * p, 256:512]
            from_root(start, inverse_piece)
            lead_copy(0).wait_recv()
            lead_copy(1).wait_recv()
            side = dot32(g[64:320, 256:512], gbuf[1].astype(jnp.float32), ((1,), (0,)))
            g[64:320, 0:256] = gbuf[2].astype(jnp.float32) - dot32(side, side, ((0,), (0,)))
            set_identity(g)

        def phase(it):
            def store(n, packed):
                if n < 2:
                    for part in range(4):
                        inv1_src[4 * n + part] = packed[8 * part : 8 * part + 8]
                    if n == 1:
                        when(it == 1, lambda: from_root(start, next_piece, 2))
                else:
                    x_src[n - 2] = packed
                    when(it == 1, lambda: from_root(start, lambda p: inverse_first(n - 2, p)))

            factor_phase(g, store, lambda: when(it == 0, bulk))
            when(it == 0, second_half)

        loop(0, 2, phase)

    when(root, root_main)
    when(neither(root), arrive)

    def top_sends():
        when(aide, lambda: lead_copy(0).start())
        when(helper, lambda: lead_copy(1).start())
        panel_top(k, start)
        column_pair(k).start()
        when(aide, lambda: lead_scatter(0, start))
        when(helper, lambda: lead_scatter(1, start))

    when(both(top, neither(root)), top_sends)
    when(both(both(mate, r < 2), neither(root)), lambda: feeds(start))

    def top_spread(which):
        down(which, start)
        across(which, start)

    def head_inverses(p):
        when(takes_part(2, r), lambda: next_piece(p).wait_recv())
        top_spread(2)
        for n in range(2):
            inverse_first(n, p).wait_recv()
            inverse_down(n, start)

    def aide_main():
        column_pair(0).wait_recv()
        panel_top(0, start)
        loop(0, 1, mirror_half)
        lead_from(1, 0).wait_recv()
        top_spread(0)
        inverse_piece(0).wait_recv()
        top_spread(1)
        head_inverses(0)
        loop(1, 2, mirror_half)

    when(aide, aide_main)
    when(both(hub, neither(aide)), lambda: loop(0, 2, mirror_half))

    def head_main():
        lead_from(0, 1).wait_recv()
        when(neither(helper), lambda: lead_from(1, 2).wait_recv())
        top_spread(0)
        inverse_piece(1).wait_recv()
        top_spread(1)
        head_inverses(2)

    when(head, head_main)

    def line_spread():
        for which in range(3):
            piece_taken(which)
            across(which, start)

    when(both(k == 1, inner), line_spread)
    when(runner, lambda: loop(0, 2, lambda t: panel_line(t, start, True)))

    def put(block, lo, hi, values):
        high = values.astype(jnp.bfloat16)
        parts[block, 0, lo:hi] = high
        parts[block, 1, lo:hi] = (values - high.astype(jnp.float32)).astype(jnp.bfloat16)

    def assemble():
        def block(n):
            return jnp.concatenate([lead[p, n] for p in range(16)], axis=0).astype(jnp.float32)

        collect(0)
        collect(1)
        first_inverse = jnp.concatenate([inv0[p] for p in range(16)], axis=0)
        put(0, 0, 256, first_inverse)
        parts_pair(0).start()
        side = dot32(first_inverse, block(0), ((1,), (0,)))
        work[:, 0:256] = block(1) - dot32(side, side, ((0,), (0,)))
        work[:, 256:512] = -dot32(side, first_inverse, ((0,), (0,)))
        rows = lax.broadcasted_iota(jnp.int32, (256, 256), 0)
        cols = lax.broadcasted_iota(jnp.int32, (256, 256), 1)
        work[:, 512:768] = jnp.where(rows == cols, 1.0, 0.0)
        collect(2)
        for n in range(4):
            if n < 2:
                packed = jnp.concatenate([inv1[4 * n + p] for p in range(4)], axis=0)
            else:
                when(inner, lambda n=n: inverse_taken(n - 2))
                packed = xs[n - 2]
            inverse = jnp.concatenate([packed[:, 64:128], packed[:, 0:64]], axis=0)
            lo, hi = 64 * n, 64 * n + 64
            lines = dot32(inverse, work[lo:hi, :], ((1,), (0,)))
            put(1, lo, hi, lines[:, 256:512])
            put(2, lo, hi, lines[:, 512:768])
            parts_pair(1 + n).start()
            if n < 3:
                work[hi:256, :] = work[hi:256, :] - dot32(lines[:, hi:256], lines, ((0,), (0,)))

    when(k == 1, assemble)

    def parts_take():
        for n in range(5):
            parts_pair(n).wait_recv()

    when(k == 0, parts_take)
    when(mate, mirror_take)

    def column_taken(col):
        for m in range(16):
            panel_copy(col, m, 2).wait_recv()

    when(both(k == 1, inner), lambda: loop(0, 2, column_taken))
    when(both(top, neither(aide)), lambda: column_pair(1 - k).wait_recv())

    when(runner, lambda: loop(0, 2, lambda t: panel_line(t, sent, False)))

    def top_drain():
        column_pair(k).wait_send()
        when(neither(root), lambda: panel_top(k, sent))
        when(aide, lambda: panel_top(0, sent))

    when(top, top_drain)
    when(both(mate, r < 2), lambda: feeds(sent))

    when(hub, lambda: loop(0, 2, mirror_sent))

    def core1_drain():
        for which in range(3):
            across(which, sent)
        for n in range(5):
            parts_pair(n).wait_send()

    when(k == 1, core1_drain)

    def line_drain():
        for which in range(3):
            down(which, sent)
        for n in range(2):
            inverse_down(n, sent)

    when(c == 1, line_drain)

    def aide_drain():
        lead_copy(0).wait_send()
        lead_scatter(0, sent)

    when(aide, aide_drain)

    def helper_drain():
        lead_copy(1).wait_send()
        lead_scatter(1, sent)

    when(helper, helper_drain)

    def root_drain():
        from_root(sent, inverse_piece)
        from_root(sent, next_piece, 2)
        for n in range(2):
            from_root(sent, lambda p, n=n: inverse_first(n, p))

    when(root, root_drain)


def gather(kernel):
    bf16, f32 = jnp.bfloat16, jnp.float32
    dma = pltpu.SemaphoreType.DMA
    return pl.pallas_call(
        gather_kernel,
        out_shape=(
            jax.ShapeDtypeStruct((4, 2, 256, 256), bf16),
            jax.ShapeDtypeStruct((2, 2, 2, 256, 256), bf16),
            jax.ShapeDtypeStruct((3, 2, 256, 256), bf16),
        ),
        in_specs=[pl.BlockSpec(memory_space=pltpu.HBM)],
        out_specs=(
            pl.BlockSpec(memory_space=pl.ANY),
            pl.BlockSpec(memory_space=pl.ANY),
            pl.BlockSpec(memory_space=pltpu.VMEM),
        ),
        scratch_shapes=[
            pltpu.VMEM((16, 2, 16, 256), bf16),
            pltpu.VMEM((16, 16, 256), f32),
            pltpu.VMEM((8, 8, 128), f32),
            pltpu.VMEM((2, 32, 128), f32),
            pltpu.VMEM((3, 256, 256), bf16),
            pltpu.VMEM((384, 512), f32),
            pltpu.VMEM((2, 32, 128), f32),
            pltpu.VMEM((16, 16, 256), f32),
            pltpu.VMEM((8, 8, 128), f32),
            pltpu.VMEM((256, 768), f32),
            dma((32, 2)), dma((32,)), dma((33,)), dma((33,)),
            dma((16, 4)), dma((16,)), dma((16,)), dma((16,)),
            dma((2,)), dma((2,)),
            dma((16,)), dma((2,)), dma((3, 16)), dma((3,)), dma((3, 16)), dma((3, 16)), dma((5,)), dma((5,)),
            dma((4, 16)), dma((4,)), dma((2, 16)), dma((2,)), dma((3,)),
        ],
        compiler_params=pltpu.CompilerParams(
            collective_id=0, has_side_effects=True, vmem_limit_bytes=24 * 1024 * 1024
        ),
        name="gather_and_factor",
    )(kernel)


def update_kernel(kern, acol, brow, parts, panels, schur, old, pan, new, sems):
    r = lax.axis_index("row")
    c = lax.axis_index("col")
    k = lax.rem(c, 2)
    load = pltpu.make_async_copy(kern.at[0, :, 0], old, sems.at[0])
    load.start()
    f32 = jnp.float32
    tri = lax.broadcasted_iota(jnp.int32, (256, 256), 0) >= lax.broadcasted_iota(jnp.int32, (256, 256), 1)
    stores = []

    def store(src, dst):
        stores.append(pltpu.make_async_copy(src, dst, sems.at[1 + len(stores)]))
        stores[-1].start()

    def rows(a, b):
        return lax.dot_general(a, b, (((1,), (1,)), ((), ())), preferred_element_type=f32)

    lefts = []
    for h in range(2):
        a, b = (jnp.concatenate([acol[2 * h, s], acol[2 * h + 1, s]], axis=0) for s in range(2))
        first = rows(a, parts[0, 0]) + rows(a, parts[0, 1])
        second = rows(a, parts[1, 0]) + rows(a, parts[1, 1]) + rows(b, parts[2, 0]) + rows(b, parts[2, 1])
        lefts.append(jnp.concatenate([first.astype(jnp.bfloat16), second.astype(jnp.bfloat16)], axis=1))
        for e in range(2):
            i = 2 * h + e
            for n, solved in enumerate((first, second)):
                part = solved[256 * e : 256 * e + 256]
                if i == 0:
                    whole = jnp.logical_or(r > n, jnp.logical_and(r == n, tri))
                    part = jnp.where(whole, part, 0.0)
                pan[i, n] = part
            store(pan.at[i], panels.at[0, i])
    columns = []
    for j in range(2):
        a, b = brow[0, j, k], brow[1, j, k]
        upper = jnp.dot(parts[0, 0], a, preferred_element_type=f32) + jnp.dot(
            parts[0, 1], a, preferred_element_type=f32
        )
        lower = jnp.dot(parts[1, 0], a, preferred_element_type=f32) + jnp.dot(
            parts[1, 1], a, preferred_element_type=f32
        )
        lower = lower + jnp.dot(parts[2, 0], b, preferred_element_type=f32)
        lower = lower + jnp.dot(parts[2, 1], b, preferred_element_type=f32)
        columns.append(jnp.concatenate([upper, lower], axis=0).astype(jnp.bfloat16))
    mirror = jnp.concatenate(columns, axis=1)
    load.wait()
    for h in range(2):
        change = jnp.dot(lefts[h], mirror, preferred_element_type=f32)
        for e in range(2):
            i = 2 * h + e
            for j in range(2):
                out = old[i, j].astype(f32) - change[256 * e : 256 * e + 256, 256 * j : 256 * j + 256]
                if i == 0:
                    out = jnp.where(r >= 2, out, 0.0)
                if j == 0:
                    out = jnp.where(c >= 2, out, 0.0)
                new[i, j] = out.astype(jnp.bfloat16)
            store(new.at[i], schur.at[0, i, 0])
    for copy in stores:
        copy.wait()


def update(kernel, *gathered):
    hbm = pl.BlockSpec(memory_space=pltpu.HBM)
    return pl.pallas_call(
        update_kernel,
        out_shape=(
            jax.ShapeDtypeStruct((1, 4, 2, 256, 256), jnp.float32),
            jax.ShapeDtypeStruct((1, 4, 1, 2, 256, 256), jnp.bfloat16),
        ),
        in_specs=[hbm] + [pl.BlockSpec(memory_space=pltpu.VMEM)] * 3,
        out_specs=(hbm, hbm),
        scratch_shapes=[
            pltpu.VMEM((4, 2, 256, 256), jnp.bfloat16),
            pltpu.VMEM((4, 2, 256, 256), jnp.float32),
            pltpu.VMEM((4, 2, 256, 256), jnp.bfloat16),
            pltpu.SemaphoreType.DMA((9,)),
        ],
        compiler_params=pltpu.CompilerParams(vmem_limit_bytes=32 * 1024 * 1024),
        name="solve_and_update",
    )(kernel, *gathered)


def per_device(kernel):
    kernel = pltpu.with_memory_space_constraint(kernel, pltpu.HBM)
    return update(kernel, *gather(kernel))


def solution(mesh):
    in_specs = (P("row", None, "col", None, None, None),)
    out_specs = (P("row", None, None, None, None), P("row", None, "col", None, None, None))
    return jax.shard_map(per_device, mesh=mesh, in_specs=in_specs, out_specs=out_specs, check_vma=False)
```

```python
import functools

import jax
import jax.numpy as jnp
from jax import lax
from jax.experimental import pallas as pl
from jax.experimental.pallas import tpu as pltpu
from jax.sharding import PartitionSpec as P

MESH = pl.DeviceIdType.MESH
HI = lax.Precision.HIGHEST
PLANE = sorted(((a, b) for a in range(4) for b in range(4) if a or b), key=lambda d: -min(d[0], 4 - d[0]) - min(d[1], 4 - d[1]))
NEAR = ((0, 1), (0, 3), (1, 0), (3, 0))
LINE = sorted(range(1, 16), key=lambda d: -min(d, 16 - d))
SKIP = {0: 2, 2: 4, 4: 6, 6: 7, 13: 11, 11: 9, 9: 8}
BACK = {0: 13, 2: 1, 4: 3, 6: 5, 13: 14, 14: 15, 11: 12, 9: 10}


def lookup(key, pairs):
    value = jnp.int32(0)
    for k, v in pairs.items():
        value = jnp.where(key == k, jnp.int32(v), value)
    return value


def member(key, keys):
    hit = key == keys[0]
    for k in keys[1:]:
        hit = jnp.logical_or(hit, key == k)
    return hit


def dot32(a, b, dims):
    return lax.dot_general(a, b, (dims, ((), ())), precision=HI, preferred_element_type=jnp.float32)


def row(v, i):
    return jnp.broadcast_to(v[i : i + 1, :], (8, 128))

def lane(v, i):
    return jnp.broadcast_to(v[:, i : i + 1], (8, 128))


def eliminate(strips, off):
    row_iota = lax.broadcasted_iota(jnp.int32, (8, 128), 0)
    strips = list(strips)
    diag = [lane(strips[0], off + i) for i in range(8)]
    pivots = []
    for s in range(8):
        later = range(s + 1, 8)
        cols = {t: [lane(strips[t], off + 8 * s + i) for i in range(8)] for t in later}
        if s < 7:
            raw = [lane(strips[s + 1], off + 8 * (s + 1) + i) for i in range(8)]
        head = strips[s]
        pivot = jnp.zeros((8, 128), jnp.float32)
        recips = []
        for i in range(8):
            own = diag[i]
            recip = 1.0 / row(own, i)
            recips.append(recip)
            pivot = jnp.where(row_iota == i, own, pivot)
            for j in range(i + 1, 8):
                line = row(own, j)
                diag[j] = diag[j] - (own * line) * recip
                factor = line * recip
                for t in later:
                    cols[t][j] = cols[t][j] - cols[t][i] * factor
            head = head - jnp.where(row_iota > i, own * recip, 0.0) * row(head, i)
        strips[s] = head
        pivots.append(pivot)
        if s < 7:
            near = cols[s + 1]
            scaled = [near[i] * recips[i] for i in range(8)]
            diag = []
            for j in range(8):
                terms = [scaled[i] * row(near[i], j) for i in range(8)]
                while len(terms) > 1:
                    terms = [terms[a] + terms[a + 1] for a in range(0, len(terms), 2)]
                diag.append(raw[j] - terms[0])
        heads = [row(head, i) * recips[i] for i in range(8)]
        for t in later:
            terms = [cols[t][i] * heads[i] for i in range(8)]
            while len(terms) > 1:
                terms = [terms[a] + terms[a + 1] for a in range(0, len(terms), 2)]
            strips[t] = strips[t] - terms[0]
    return strips, pivots


def factor_phase(g, store, middle):
    col_iota = lax.broadcasted_iota(jnp.int32, (8, 128), 1)
    row_iota = lax.broadcasted_iota(jnp.int32, (8, 128), 0)
    for b in range(4):
        odd = b % 2
        lo = 64 + 64 * b
        win = 128 * (b // 2)
        off = 64 * odd
        strips = []
        tile = g[lo:lo+64, win:win+128]
        for s in range(8):
            if odd:
                unit = jnp.where(col_iota == row_iota + 8 * s, 1.0, 0.0)
                strips.append(jnp.where(col_iota >= 64, tile[8*s:8*s+8], unit))
            else:
                unit = jnp.where(col_iota == row_iota + 8 * s + 64, 1.0, 0.0)
                strips.append(jnp.where(col_iota < 64, tile[8*s:8*s+8], unit))
        strips, pivots = eliminate(strips, off)
        keep = (col_iota < 64) if odd else (col_iota >= 64)
        wide = jnp.concatenate([jnp.where(keep, a * lax.rsqrt(p), 0.0) for a, p in zip(strips, pivots)], axis=0)
        turned = pltpu.roll(wide, 64, 1)
        low = wide if odd else turned
        high = turned if odd else wide
        if b == 1:
            middle()
        store(b, jnp.where(lax.broadcasted_iota(jnp.int32,(32,128),1) < 64, low[32:], high[:32]))
        base = lo if odd else lo - 64
        if b < 3:
            nwin = 128 * ((b + 1) // 2)
            u = dot32(wide, g[base:base+128, nwin:nwin+128], ((1,), (0,)))
            nxt = lo + 64
            noff = 64 * (1 - odd)
            if odd:
                g[nxt:nxt+64, nwin:nwin+128] = g[nxt:nxt+64, nwin:nwin+128] - dot32(u[:, 0:64], u, ((0,), (0,)))
            else:
                g[nxt:nxt+64, nwin:nwin+128] = g[nxt:nxt+64, nwin:nwin+128] - dot32(u, u, ((0,), (0,)))[64:128]
        lines = dot32(wide, g[base : base + 128, :], ((1,), (0,)))
        g[lo:lo+64, :] = lines
        if b < 3:
            first = 64 * (b + 1)
            change = dot32(lines[:, 0:256], lines, ((0,), (0,)))
            nxt = lo + 64
            nwin = 128 * ((b + 1) // 2)
            for lo_c, hi_c in ((0, nwin), (nwin + 128, 512)):
                if hi_c > lo_c:
                    g[nxt:nxt+64, lo_c:hi_c] = g[nxt:nxt+64, lo_c:hi_c] - change[first:first+64, lo_c:hi_c]
            if b < 2:
                g[nxt+64:320, :] = g[nxt+64:320, :] - change[first+64:256, :]


def set_identity(g):
    rows = lax.broadcasted_iota(jnp.int32, (256, 256), 0)
    cols = lax.broadcasted_iota(jnp.int32, (256, 256), 1)
    g[64:320, 256:512] = jnp.where(rows == cols, 1.0, 0.0)


def gather_kernel(
    kern, acol, brow, parts,
    lead, inv0, inv1, xs, gbuf, g, x_src, inv_src, inv1_src, work,
    p_send, p_recv, p_sib_send, p_sib_recv, m_send, m_recv, m_sib_send, m_sib_recv,
    lead_send, lead_recv, gs_send, gh_recv, gd_send, gd_recv, ga_send, ga_recv, parts_send, parts_recv,
    xr_send, xh_recv, xd_send, xd_recv, loc,
):
    r = lax.axis_index("row")
    c = lax.axis_index("col")
    x, y = lax.div(r, 4), lax.rem(r, 4)
    z, k = lax.div(c, 2), lax.rem(c, 2)
    zero, one = jnp.int32(0), jnp.int32(1)
    sibling = c + 1 - 2 * k
    both, neither = jnp.logical_and, jnp.logical_not
    top = z == 0
    inner = neither(top)

    def hub_core(row):
        return jnp.where(both(top, row != 0), 0, 1)

    hub = k == hub_core(r)
    mate = neither(hub)
    root = both(r == 0, c == 0)
    aide = both(r == 0, c == 1)
    helper = both(r == 1, c == 1)
    head = both(c == 1, r != 0)
    runner = both(k == 0, inner)
    skip_to = lookup(z, SKIP)
    back_to = lookup(z, BACK)
    has_skip = member(z, list(SKIP))
    has_back = member(z, list(BACK))
    parent = lookup(z, {v: q for q, v in list(SKIP.items()) + list(BACK.items())})
    children = has_skip.astype(jnp.int32) + has_back.astype(jnp.int32)
    barrier = pltpu.get_barrier_semaphore()

    def remote(src, dst, send, recv, row, col):
        return pltpu.make_async_remote_copy(
            src_ref=src, dst_ref=dst, send_sem=send, recv_sem=recv, device_id=(row, col), device_id_type=MESH
        )

    def signal(row, col):
        pl.semaphore_signal(barrier, inc=1, device_id=(row, col), device_id_type=MESH)

    def loop(lo, hi, body):
        def step(d, carry):
            body(d)
            return carry

        lax.fori_loop(lo, hi, step, 0)

    def when(cond, body):
        @pl.when(cond)
        def _():
            body()

    def start(copy):
        copy.start()

    def sent(copy):
        copy.wait_send()

    def peer(d):
        return lax.rem(x + d[0], 4) * 4 + lax.rem(y + d[1], 4)

    own_block = kern.at[0, 0, 0, 0]
    own_panel = pltpu.make_async_copy(kern.at[0, :, 0, 0], acol.at[:, k], loc.at[0])
    own_rows = pltpu.make_async_copy(kern.at[0, 0, 0], brow.at[lax.rem(r, 2), :, k], loc.at[1])
    own_lead = pltpu.make_async_copy(own_block, gbuf.at[0], loc.at[2])
    aide_piece = pltpu.make_async_copy(own_block.at[pl.ds(0, 16)], lead.at[0, 0], loc.at[2])
    helper_piece = pltpu.make_async_copy(own_block.at[pl.ds(16, 16)], lead.at[1, 1], loc.at[2])
    when(root, lambda: own_lead.start())
    when(aide, lambda: aide_piece.start())
    when(helper, lambda: helper_piece.start())
    when(top, lambda: own_panel.start())
    when(r < 2, lambda: own_rows.start())

    signal(r, sibling)

    def greet_panel():
        when(jnp.logical_or(parent != 0, r != 0), lambda: signal(r, 2 * parent))
        when(parent == 0, lambda: signal(r, one))

    when(runner, greet_panel)

    def greet_plane():
        for d in PLANE:
            signal(peer(d), c)
        when(inner, lambda: signal(r, one))

    when(k == 1, greet_plane)

    def greet_mirror():
        for d in NEAR:
            signal(peer(d), hub_core(peer(d)))

    when(both(hub, top), greet_mirror)

    def greet_sources():
        signal(zero, zero)
        signal(zero, one)
        when(r != 1, lambda: signal(one, one))

    when(head, greet_sources)
    when(jnp.logical_or(root, aide), lambda: signal(one, one))

    def arrive():
        plane = jnp.where(k == 1, 15, 0) + jnp.where(both(hub, top), 4, 0)
        line = jnp.where(root, 0, jnp.where(top, 2, jnp.where(k == 0, children, 0)))
        down = jnp.where(c == 1, 15, 0)
        more = jnp.where(root, 15, 0) + jnp.where(aide, 15, 0) + jnp.where(helper, 16, 0)
        pl.semaphore_wait(barrier, 1 + plane + line + down + more)
        when(top, lambda: own_panel.wait())
        when(r < 2, lambda: own_rows.wait())
        when(aide, lambda: aide_piece.wait())
        when(helper, lambda: helper_piece.wait())

    CHUNKS = tuple((i, quarter) for i in range(4) for quarter in range(4))

    def panel_copy(col, m, way):
        i, quarter = CHUNKS[m]
        chunk = acol.at[i, col, pl.ds(64 * quarter, 64)]
        n = 16 * col + m
        to = (r, 2 * skip_to) if way == 0 else (r, 2 * back_to) if way == 1 else (r, sibling)
        send = p_sib_send.at[n] if way == 2 else p_send.at[n, way]
        recv = p_sib_recv.at[n] if way == 2 else p_recv.at[n]
        return remote(chunk, chunk, send, recv, *to)

    def column_pair(col):
        return remote(acol.at[:, col], acol.at[:, col], p_sib_send.at[32], p_sib_recv.at[32], r, sibling)

    def panel_top(col, act):
        for m in range(16):
            act(panel_copy(col, m, 0))
            act(panel_copy(col, m, 1))

    def panel_line(t, act, arrive_first):
        col = jnp.where(r == 0, 1 - t, t)
        for m in range(16):
            if arrive_first:
                panel_copy(col, m, 0).wait_recv()
            when(has_skip, lambda m=m: act(panel_copy(col, m, 0)))
            when(has_back, lambda m=m: act(panel_copy(col, m, 1)))
            act(panel_copy(col, m, 2))

    def mirror_chunk(s, m):
        j, half = m // 4, m % 2
        return brow.at[s, j, (m // 2) % 2, pl.ds(128 * half, 128)]

    def mirror_copy(s, m, way, row):
        chunk = mirror_chunk(s, m)
        return remote(chunk, chunk, m_send.at[8 * s + m, way], m_recv.at[8 * s + m], row, 2 * z + hub_core(row))

    def mirror_pair(s, m):
        n = 8 * s + m
        return remote(mirror_chunk(s, m), mirror_chunk(s, m), m_sib_send.at[n], m_sib_recv.at[n], r, sibling)

    def mirror_feed(j, half):
        n = 8 * r + 4 * j + 2 * k + half
        chunk = brow.at[r, j, k, pl.ds(128 * half, 128)]
        return remote(chunk, chunk, m_sib_send.at[n], m_recv.at[n], r, sibling)

    def mirror_each(s, m, act):
        j, kc = m // 4, (m // 2) % 2
        rel = lax.rem(y + 4 - s, 4)
        ring_up = jnp.logical_or(rel == 0, both(s == 1, rel == 1))
        ring_down = jnp.logical_or(rel == 0, both(s == 0, rel == 3))
        line_up = jnp.logical_or(x == 0, both(s == 0, x == 1))
        line_down = jnp.logical_or(x == 0, both(s == 1, x == 3))
        if j == 0:
            ring_up, ring_down = both(ring_up, x == 0), both(ring_down, x == 0)
        else:
            line_up, line_down = both(line_up, rel == 0), both(line_down, rel == 0)
        when(ring_up, lambda: act(mirror_copy(s, m, 0, peer((0, 1)))))
        when(ring_down, lambda: act(mirror_copy(s, m, 1, peer((0, 3)))))
        when(line_up, lambda: act(mirror_copy(s, m, 2, peer((1, 0)))))
        when(line_down, lambda: act(mirror_copy(s, m, 3, peer((3, 0)))))
        when(both(kc != k, r != s), lambda: act(mirror_pair(s, m)))

    def mirror_half(t):
        nearer = jnp.where(jnp.logical_or(y == 0, y == 3), 0, 1)
        s = jnp.where(nearer == t, 0, 1)
        for m in range(8):
            when(jnp.logical_or(r != s, k != (m // 2) % 2), lambda m=m: mirror_copy(s, m, 0, r).wait_recv())
            mirror_each(s, m, start)

    def mirror_sent(s):
        for m in range(8):
            mirror_each(s, m, sent)

    def feeds(act):
        for j in range(2):
            for half in range(2):
                act(mirror_feed(j, half))

    def mirror_take():
        for s in range(2):

            def take(s=s):
                for kc in range(2):

                    def mine(kc=kc):
                        for j in range(2):
                            for half in range(2):
                                mirror_pair(s, 4 * j + 2 * kc + half).wait_recv()

                    when(k == kc, mine)

            when(r != s, take)

    def lead_from(n, p):
        rows = own_block.at[pl.ds(16 * p, 16)]
        return remote(rows, lead.at[p, n], gs_send.at[p], gh_recv.at[n], jnp.int32(p), one)

    def lead_scatter(n, act):
        for p in range(16):
            if p != n:
                act(lead_from(n, p))

    def view(which, p):
        if which < 2:
            return (lead, inv0)[which].at[p]
        return inv1.at[lax.div(p, 2)]

    def takes_part(which, row):
        return row >= 0 if which < 2 else lax.rem(row, 2) == 0

    def down(which, act):
        piece = view(which, r)

        def go():
            for d in LINE:
                act(remote(piece, piece, gd_send.at[which, d], gd_recv.at[which], r, jnp.int32(2 * d + 1)))

        when(takes_part(which, r), go)

    def across(which, act):
        piece = view(which, r)

        def go():
            for n, d in enumerate(PLANE):
                act(remote(piece, piece, ga_send.at[which, n], ga_recv.at[which, r], peer(d), c))

        when(takes_part(which, r), go)

    def piece_taken(which):
        piece = view(which, r)
        copy = remote(piece, piece, gd_send.at[which, 0], gd_recv.at[which], r, sibling)
        when(takes_part(which, r), lambda: copy.wait_recv())

    def collect(which):
        def take(d):
            p = lax.rem(r + d, 16)
            piece = view(which, p)
            copy = remote(piece, piece, ga_send.at[which, 0], ga_recv.at[which, p], r, sibling)
            when(takes_part(which, p), lambda: copy.wait_recv())

        loop(1, 16, take)

    def inverse_piece(p):
        return remote(inv_src.at[p], inv0.at[p], xr_send.at[0, p], xh_recv.at[0], jnp.int32(p), one)

    def next_piece(p):
        return remote(inv1_src.at[p // 2], inv1.at[p // 2], xr_send.at[1, p], xh_recv.at[1], jnp.int32(p), one)

    def inverse_first(n, p):
        return remote(x_src.at[n], xs.at[n], xr_send.at[2 + n, p], xh_recv.at[2 + n], jnp.int32(p), one)

    def from_root(act, copy, step=1):
        for d in PLANE:
            p = 4 * d[0] + d[1]
            if p % step == 0:
                act(copy(p))
        act(copy(0))

    def inverse_down(n, act):
        for d in LINE:
            act(remote(xs.at[n], xs.at[n], xd_send.at[n, d], xd_recv.at[n], r, jnp.int32(2 * d + 1)))

    def inverse_taken(n):
        remote(xs.at[n], xs.at[n], xd_send.at[n, 0], xd_recv.at[n], r, sibling).wait_recv()

    def parts_pair(n):
        block = parts.at[0] if n == 0 else parts.at[pl.ds(1, 2), :, pl.ds(64 * (n - 1), 64)]
        return remote(block, block, parts_send.at[n], parts_recv.at[n], r, sibling)

    def lead_copy(n):
        return remote(own_block, gbuf.at[n + 1], lead_send.at[n], lead_recv.at[n], zero, zero)

    def root_main():
        own_lead.wait()
        g[0:64, :] = jnp.zeros((64, 512), jnp.float32)
        g[320:384, :] = jnp.zeros((64, 512), jnp.float32)
        g[64:320, 0:256] = gbuf[0].astype(jnp.float32)
        set_identity(g)

        def bulk():
            arrive()
            column_pair(0).start()
            feeds(start)

        def second_half():
            for p in range(16):
                inv_src[p] = g[64 + 16 * p : 80 + 16 * p, 256:512]
            from_root(start, inverse_piece)
            lead_copy(0).wait_recv()
            lead_copy(1).wait_recv()
            side = dot32(g[64:320, 256:512], gbuf[1].astype(jnp.float32), ((1,), (0,)))
            g[64:320, 0:256] = gbuf[2].astype(jnp.float32) - dot32(side, side, ((0,), (0,)))
            set_identity(g)

        def phase(it):
            def store(n, packed):
                if n < 2:
                    for part in range(4):
                        inv1_src[4 * n + part] = packed[8 * part : 8 * part + 8]
                    if n == 1:
                        when(it == 1, lambda: from_root(start, next_piece, 2))
                else:
                    x_src[n - 2] = packed
                    when(it == 1, lambda: from_root(start, lambda p: inverse_first(n - 2, p)))

            factor_phase(g, store, lambda: when(it == 0, bulk))
            when(it == 0, second_half)

        loop(0, 2, phase)

    when(root, root_main)
    when(neither(root), arrive)

    def top_sends():
        when(aide, lambda: lead_copy(0).start())
        when(helper, lambda: lead_copy(1).start())
        panel_top(k, start)
        column_pair(k).start()
        when(aide, lambda: lead_scatter(0, start))
        when(helper, lambda: lead_scatter(1, start))

    when(both(top, neither(root)), top_sends)
    when(both(both(mate, r < 2), neither(root)), lambda: feeds(start))

    def top_spread(which):
        down(which, start)
        across(which, start)

    def head_inverses(p):
        when(takes_part(2, r), lambda: next_piece(p).wait_recv())
        top_spread(2)
        for n in range(2):
            inverse_first(n, p).wait_recv()
            inverse_down(n, start)

    def aide_main():
        column_pair(0).wait_recv()
        panel_top(0, start)
        loop(0, 1, mirror_half)
        lead_from(1, 0).wait_recv()
        top_spread(0)
        inverse_piece(0).wait_recv()
        top_spread(1)
        head_inverses(0)
        loop(1, 2, mirror_half)

    when(aide, aide_main)
    when(both(hub, neither(aide)), lambda: loop(0, 2, mirror_half))

    def head_main():
        lead_from(0, 1).wait_recv()
        when(neither(helper), lambda: lead_from(1, 2).wait_recv())
        top_spread(0)
        inverse_piece(1).wait_recv()
        top_spread(1)
        head_inverses(2)

    when(head, head_main)

    def line_spread():
        for which in range(3):
            piece_taken(which)
            across(which, start)

    when(both(k == 1, inner), line_spread)
    when(runner, lambda: loop(0, 2, lambda t: panel_line(t, start, True)))

    def put(block, lo, hi, values):
        high = values.astype(jnp.bfloat16)
        parts[block, 0, lo:hi] = high
        parts[block, 1, lo:hi] = (values - high.astype(jnp.float32)).astype(jnp.bfloat16)

    def assemble():
        def block(n):
            return jnp.concatenate([lead[p, n] for p in range(16)], axis=0).astype(jnp.float32)

        collect(0)
        collect(1)
        first_inverse = jnp.concatenate([inv0[p] for p in range(16)], axis=0)
        put(0, 0, 256, first_inverse)
        parts_pair(0).start()
        side = dot32(first_inverse, block(0), ((1,), (0,)))
        work[:, 0:256] = block(1) - dot32(side, side, ((0,), (0,)))
        work[:, 256:512] = -dot32(side, first_inverse, ((0,), (0,)))
        rows = lax.broadcasted_iota(jnp.int32, (256, 256), 0)
        cols = lax.broadcasted_iota(jnp.int32, (256, 256), 1)
        work[:, 512:768] = jnp.where(rows == cols, 1.0, 0.0)
        collect(2)
        for n in range(4):
            if n < 2:
                packed = jnp.concatenate([inv1[4 * n + p] for p in range(4)], axis=0)
            else:
                when(inner, lambda n=n: inverse_taken(n - 2))
                packed = xs[n - 2]
            inverse = jnp.concatenate([packed[:, 64:128], packed[:, 0:64]], axis=0)
            lo, hi = 64 * n, 64 * n + 64
            lines = dot32(inverse, work[lo:hi, :], ((1,), (0,)))
            put(1, lo, hi, lines[:, 256:512])
            put(2, lo, hi, lines[:, 512:768])
            parts_pair(1 + n).start()
            if n < 3:
                work[hi:256, :] = work[hi:256, :] - dot32(lines[:, hi:256], lines, ((0,), (0,)))

    when(k == 1, assemble)

    def parts_take():
        for n in range(5):
            parts_pair(n).wait_recv()

    when(k == 0, parts_take)
    when(mate, mirror_take)

    def column_taken(col):
        for m in range(16):
            panel_copy(col, m, 2).wait_recv()

    when(both(k == 1, inner), lambda: loop(0, 2, column_taken))
    when(both(top, neither(aide)), lambda: column_pair(1 - k).wait_recv())

    when(runner, lambda: loop(0, 2, lambda t: panel_line(t, sent, False)))

    def top_drain():
        column_pair(k).wait_send()
        when(neither(root), lambda: panel_top(k, sent))
        when(aide, lambda: panel_top(0, sent))

    when(top, top_drain)
    when(both(mate, r < 2), lambda: feeds(sent))

    when(hub, lambda: loop(0, 2, mirror_sent))

    def core1_drain():
        for which in range(3):
            across(which, sent)
        for n in range(5):
            parts_pair(n).wait_send()

    when(k == 1, core1_drain)

    def line_drain():
        for which in range(3):
            down(which, sent)
        for n in range(2):
            inverse_down(n, sent)

    when(c == 1, line_drain)

    def aide_drain():
        lead_copy(0).wait_send()
        lead_scatter(0, sent)

    when(aide, aide_drain)

    def helper_drain():
        lead_copy(1).wait_send()
        lead_scatter(1, sent)

    when(helper, helper_drain)

    def root_drain():
        from_root(sent, inverse_piece)
        from_root(sent, next_piece, 2)
        for n in range(2):
            from_root(sent, lambda p, n=n: inverse_first(n, p))

    when(root, root_drain)


def gather(kernel):
    bf16, f32 = jnp.bfloat16, jnp.float32
    dma = pltpu.SemaphoreType.DMA
    return pl.pallas_call(
        gather_kernel,
        out_shape=(
            jax.ShapeDtypeStruct((4, 2, 256, 256), bf16),
            jax.ShapeDtypeStruct((2, 2, 2, 256, 256), bf16),
            jax.ShapeDtypeStruct((3, 2, 256, 256), bf16),
        ),
        in_specs=[pl.BlockSpec(memory_space=pltpu.HBM)],
        out_specs=(
            pl.BlockSpec(memory_space=pl.ANY),
            pl.BlockSpec(memory_space=pl.ANY),
            pl.BlockSpec(memory_space=pltpu.VMEM),
        ),
        scratch_shapes=[
            pltpu.VMEM((16, 2, 16, 256), bf16),
            pltpu.VMEM((16, 16, 256), f32),
            pltpu.VMEM((8, 8, 128), f32),
            pltpu.VMEM((2, 32, 128), f32),
            pltpu.VMEM((3, 256, 256), bf16),
            pltpu.VMEM((384, 512), f32),
            pltpu.VMEM((2, 32, 128), f32),
            pltpu.VMEM((16, 16, 256), f32),
            pltpu.VMEM((8, 8, 128), f32),
            pltpu.VMEM((256, 768), f32),
            dma((32, 2)), dma((32,)), dma((33,)), dma((33,)),
            dma((16, 4)), dma((16,)), dma((16,)), dma((16,)),
            dma((2,)), dma((2,)),
            dma((16,)), dma((2,)), dma((3, 16)), dma((3,)), dma((3, 16)), dma((3, 16)), dma((5,)), dma((5,)),
            dma((4, 16)), dma((4,)), dma((2, 16)), dma((2,)), dma((3,)),
        ],
        compiler_params=pltpu.CompilerParams(
            collective_id=0, has_side_effects=True, vmem_limit_bytes=24 * 1024 * 1024
        ),
        name="gather_and_factor",
    )(kernel)


def update_kernel(kern, acol, brow, parts, panels, schur, old, pan, new, sems):
    r = lax.axis_index("row")
    c = lax.axis_index("col")
    k = lax.rem(c, 2)
    load = pltpu.make_async_copy(kern.at[0, :, 0], old, sems.at[0])
    load.start()
    f32 = jnp.float32
    tri = lax.broadcasted_iota(jnp.int32, (256, 256), 0) >= lax.broadcasted_iota(jnp.int32, (256, 256), 1)
    stores = []

    def store(src, dst):
        stores.append(pltpu.make_async_copy(src, dst, sems.at[1 + len(stores)]))
        stores[-1].start()

    def rows(a, b):
        return lax.dot_general(a, b, (((1,), (1,)), ((), ())), preferred_element_type=f32)

    lefts = []
    for h in range(2):
        a, b = (jnp.concatenate([acol[2 * h, s], acol[2 * h + 1, s]], axis=0) for s in range(2))
        first = rows(a, parts[0, 0]) + rows(a, parts[0, 1])
        second = rows(a, parts[1, 0]) + rows(a, parts[1, 1]) + rows(b, parts[2, 0]) + rows(b, parts[2, 1])
        lefts.append(jnp.concatenate([first.astype(jnp.bfloat16), second.astype(jnp.bfloat16)], axis=1))
        for e in range(2):
            i = 2 * h + e
            for n, solved in enumerate((first, second)):
                part = solved[256 * e : 256 * e + 256]
                if i == 0:
                    whole = jnp.logical_or(r > n, jnp.logical_and(r == n, tri))
                    part = jnp.where(whole, part, 0.0)
                pan[i, n] = part
            store(pan.at[i], panels.at[0, i])
    columns = []
    for j in range(2):
        a, b = brow[0, j, k], brow[1, j, k]
        upper = jnp.dot(parts[0, 0], a, preferred_element_type=f32) + jnp.dot(
            parts[0, 1], a, preferred_element_type=f32
        )
        lower = jnp.dot(parts[1, 0], a, preferred_element_type=f32) + jnp.dot(
            parts[1, 1], a, preferred_element_type=f32
        )
        lower = lower + jnp.dot(parts[2, 0], b, preferred_element_type=f32)
        lower = lower + jnp.dot(parts[2, 1], b, preferred_element_type=f32)
        columns.append(jnp.concatenate([upper, lower], axis=0).astype(jnp.bfloat16))
    mirror = jnp.concatenate(columns, axis=1)
    load.wait()
    for h in range(2):
        change = jnp.dot(lefts[h], mirror, preferred_element_type=f32)
        for e in range(2):
            i = 2 * h + e
            for j in range(2):
                out = old[i, j].astype(f32) - change[256 * e : 256 * e + 256, 256 * j : 256 * j + 256]
                if i == 0:
                    out = jnp.where(r >= 2, out, 0.0)
                if j == 0:
                    out = jnp.where(c >= 2, out, 0.0)
                new[i, j] = out.astype(jnp.bfloat16)
            store(new.at[i], schur.at[0, i, 0])
    for copy in stores:
        copy.wait()


def update(kernel, *gathered):
    hbm = pl.BlockSpec(memory_space=pltpu.HBM)
    return pl.pallas_call(
        update_kernel,
        out_shape=(
            jax.ShapeDtypeStruct((1, 4, 2, 256, 256), jnp.float32),
            jax.ShapeDtypeStruct((1, 4, 1, 2, 256, 256), jnp.bfloat16),
        ),
        in_specs=[hbm] + [pl.BlockSpec(memory_space=pltpu.VMEM)] * 3,
        out_specs=(hbm, hbm),
        scratch_shapes=[
            pltpu.VMEM((4, 2, 256, 256), jnp.bfloat16),
            pltpu.VMEM((4, 2, 256, 256), jnp.float32),
            pltpu.VMEM((4, 2, 256, 256), jnp.bfloat16),
            pltpu.SemaphoreType.DMA((9,)),
        ],
        compiler_params=pltpu.CompilerParams(vmem_limit_bytes=32 * 1024 * 1024),
        name="solve_and_update",
    )(kernel, *gathered)


def per_device(kernel):
    kernel = pltpu.with_memory_space_constraint(kernel, pltpu.HBM)
    return update(kernel, *gather(kernel))


def solution(mesh):
    in_specs = (P("row", None, "col", None, None, None),)
    out_specs = (P("row", None, None, None, None), P("row", None, "col", None, None, None))
    return jax.shard_map(per_device, mesh=mesh, in_specs=in_specs, out_specs=out_specs, check_vma=False)
```
